32 devices in a mesh: dp: 4 (over z), expert: 8 (over y, x, core).
Axes of the slice: x: 2, y: 2, z: 4, core: 2. Of those that a mesh axis runs over, the one named last changes fastest.
Arguments:
- tokens: bfloat16 [16384, 768], P(('dp', 'expert')), may hold values from -6 to 6
- segment_ids: int32 [32, 512], P(('dp', 'expert')), may hold values from 0 to 3, never falling along the last dimension, each value on 1 to 256 neighbouring positions
- token_expert: int32 [16384, 1], P(('dp', 'expert')), may hold values from 0 to 7; in each aligned block of 512 rows (0 to 511, 512 to 1023, ...) at most 128 rows name the same one
- gates: float32 [16384], P(('dp', 'expert')), may hold values from 0.3 to 1
- ln1_gain: float32 [768], replicated, may hold values from 0.1 to 1.9
- w_qkv: bfloat16 [768, 2304], replicated, may hold values from -0.21875 to 0.21875
- w_out: bfloat16 [768, 768], replicated, may hold values from -1.25 to 1.25
- ln2_gain: float32 [768], replicated, may hold values from 0.1 to 1.9
- expert_in: bfloat16 [8, 768, 3072], P('expert'), may hold values from -0.21875 to 0.21875
- expert_out: bfloat16 [8, 3072, 768], P('expert'), may hold values from -0.109375 to 0.109375
- cotangent: bfloat16 [16384, 768], P(('dp', 'expert')), may hold values from -6 to 6
Outputs:
- block_out: bfloat16 [16384, 768], P(('dp', 'expert'))
- grad_tokens: bfloat16 [16384, 768], P(('dp', 'expert'))
- grad_ln1: float32 [768], P('dp')
- grad_qkv: float32 [768, 2304], P(None, 'dp')
- grad_out: float32 [768, 768], P(None, 'dp')
- grad_ln2: float32 [768], P('dp')
- grad_expert_in: float32 [8, 768, 3072], P('expert', 'dp')
- grad_expert_out: float32 [8, 3072, 768], P('expert', 'dp')
The draws below stay inside these ranges and needn't reach their ends.
Inputs may be any that keep to these rules, and one draw needn't show every extreme that they name: `token_expert`: in the 512 rows of one device no expert is named by more than 128 tokens; in some device one expert is named exactly 128 times. `segment_ids`: within a row the numbers never fall; each document has 1 to 256 positions, one exactly that many.
All inputs are finite; a program needn't handle non-finite values.
Results may differ from the reference program's by a relative error of at most 0.012.
Values may be sent and summed in bfloat16 or wider, within the bound.
A program may use at most 192 MiB of HBM per device.

```python
import math
import jax
import jax.numpy as jnp
import numpy as np
from jax import lax

D = 768
HEAD_DIM = 64
FF = 3072
EXPERTS = 8
TOK_DEV = 512
SEGS = 4
SEQS = 32
TOKENS = 16384
CAP = 128
N_DP = 4
N_EXPERT = 8


def block_scale(own_key, extent, shards, low, largest):
    factor_of, own = 1.0, jax.random.fold_in(own_key, 6)
    for dim, parts in shards:
        steps = jnp.exp(jax.random.uniform(jax.random.fold_in(own, dim), (parts,), jnp.float32, low / len(shards), largest / len(shards)))
        factor_of = factor_of * jnp.repeat(steps, extent[dim] // parts).reshape([-1 if axis == dim else 1 for axis in range(len(extent))])
    return factor_of


def split_up(amount, total, bound, skew):
    weights = [(1 << 20) // math.isqrt(standing ** skew) + 1 for standing in range(2, amount + 1)]
    spare, counts = total - bound - (amount - 1), [1] * (amount - 1)
    while spare > 0:
        movable = [i for i in range(amount - 1) if counts[i] < bound]
        mass, budget = sum([weights[i] for i in movable]), spare
        for i in movable:
            more = min(bound - counts[i], max(1, budget * weights[i] // mass), spare)
            counts[i] = counts[i] + more
            spare = spare - more
    return np.array([bound] + counts)


def ragged(key, number_of, total, reach, slope):
    if number_of == 2:
        one = jax.random.randint(key, (), max(1, total - reach), min(reach, total - 1) + 1)
        return jnp.stack([one, total - one])
    tallies = jnp.asarray(split_up(number_of, total, reach, slope), jnp.int32)
    pairs = (number_of - 1) // 2
    source_of, sink = tallies[1:1 + 2 * pairs:2], tallies[2:2 + 2 * pairs:2]
    slack = jnp.minimum(source_of - 1, reach - sink)
    shifted = jax.random.randint(jax.random.fold_in(key, 1), (pairs,), 0, 1 << 20) % (slack + 1)
    tallies = tallies.at[1:1 + 2 * pairs:2].set(source_of - shifted).at[2:2 + 2 * pairs:2].set(sink + shifted)
    return tallies[jax.random.permutation(jax.random.fold_in(key, 2), number_of)]


def deal_out(stream_key, own, number, rows, amount, top, bound, slope):
    order = jax.random.permutation(stream_key, amount)
    crowded, ordinary = load_shares(amount, rows * top, bound, slope, True), load_shares(amount, rows * top, bound, slope, False)
    places = jnp.arange(amount)

    def named(lengths, turn):
        used = int((lengths > 0).sum())
        fixed = max(1, used // 4)
        passed = fixed + (places - fixed + turn * (used - fixed)) % max(1, amount - fixed)
        return jnp.zeros((amount,), jnp.int32).at[order[jnp.where(places < fixed, places, passed)]].set(jnp.asarray(lengths, jnp.int32))

    lengths = jnp.where(number % 4 == 0, named(crowded, number // 4), named(ordinary, number - number // 4 - 1))
    mixed = jax.random.permutation(jax.random.fold_in(own, 3), amount)
    donor, sink = mixed[0:amount // 2 * 2:2], mixed[1:amount // 2 * 2:2]
    room = jnp.minimum(lengths[donor] - 1, bound - lengths[sink]) // 2
    room = jnp.where((donor == order[0]) | (sink == order[0]) | (lengths[sink] == 0), 0, jnp.maximum(room, 0))
    passed = jax.random.randint(jax.random.fold_in(own, 4), (amount // 2,), 0, 1 << 20) % (room + 1)
    lengths = lengths.at[donor].add(-passed).at[sink].add(passed)
    members = jnp.searchsorted(jnp.cumsum(lengths), jnp.arange(rows * top), side="right").astype(jnp.int32)
    table = members.reshape(top, rows).T
    table = table[jax.random.permutation(jax.random.fold_in(own, 1), rows)]
    turn = jax.random.randint(jax.random.fold_in(own, 2), (rows, 1), 0, top)
    return jnp.take_along_axis(table, (jnp.arange(top)[None, :] + turn) % top, axis=1)


def load_shares(count, total, most, slope, full):
    weights = [(1 << 20) // math.isqrt(standing ** slope) + 1 for standing in range(1, count + 1)]
    largest = most if full else min(most, max(-(-total // count), total * weights[0] // sum(weights)))
    least = 1 if total - largest >= count - 1 else 0
    holding, rest = [largest] + [least] * (count - 1), total - largest - least * (count - 1)
    while rest > 0:
        free = [i for i in range(1, count) if holding[i] < largest] or [i for i in range(1, count) if holding[i] < most]
        pool, budget = sum([weights[i] for i in free]), rest
        for i in free:
            addition = min(most - holding[i], max(1, budget * weights[i] // pool), rest)
            holding[i] = holding[i] + addition
            rest = rest - addition
    return np.array(holding)


def scatter_about(stream_key, shape, scale, limit, split=(), held_as=jnp.bfloat16):
    drawn = jax.random.normal(stream_key, shape, jnp.float32) * scale
    if len(split) > 0:
        drawn = block_scale(stream_key, shape, split, -0.22, 0.18) * drawn
    return jnp.clip(drawn, min=-limit, max=limit).astype(held_as)


def setup_inputs(seed: int = 0) -> dict:
    streams_of = jax.random.split(jax.random.key(seed), 12)
    tokens = scatter_about(streams_of[0], (TOKENS, D), 1.0, 6.0, ((0, 32),))
    segment_ids = jax.vmap(lambda own: jnp.searchsorted(jnp.cumsum(ragged(own, SEGS, TOK_DEV, TOK_DEV // 2, 0)), jnp.arange(TOK_DEV), side="right"))(jax.random.split(streams_of[1], SEQS)).reshape((SEQS, TOK_DEV)).astype(jnp.int32)
    token_expert_keys = jax.random.split(jax.random.fold_in(streams_of[2], 1), TOKENS // TOK_DEV)
    token_expert_turns = jax.random.permutation(jax.random.fold_in(streams_of[2], 3), TOKENS // TOK_DEV)
    token_expert = jax.vmap(lambda own, number: deal_out(jax.random.fold_in(streams_of[2], 2), own, number, TOK_DEV, EXPERTS, 1, CAP, 1))(token_expert_keys, token_expert_turns).reshape((TOKENS, 1))
    gates = jnp.clip(0.3 + 0.7 * jax.random.uniform(streams_of[3], (TOKENS,), jnp.float32) ** block_scale(streams_of[3], (TOKENS,), ((0, 32),), -0.2, 0.2), 0.3, 1.0)
    ln1_gain = jnp.clip(1.0 + 0.18 * jax.random.normal(streams_of[4], (D,), jnp.float32), 0.1, 1.9)
    w_qkv = scatter_about(streams_of[5], (D, 3 * D), D ** -0.5, 0.21875)
    w_out = scatter_about(streams_of[6], (D, D), (D // 32) ** -0.5, 1.25)
    ln2_gain = jnp.clip(1.0 + 0.18 * jax.random.normal(streams_of[7], (D,), jnp.float32), 0.1, 1.9)
    expert_in = scatter_about(streams_of[8], (EXPERTS, D, FF), D ** -0.5, 0.21875, ((0, 8),))
    expert_out = scatter_about(streams_of[9], (EXPERTS, FF, D), FF ** -0.5, 0.109375, ((0, 8),))
    cotangent = scatter_about(streams_of[10], (TOKENS, D), 1.0, 6.0, ((0, 32),))
    return dict(tokens=tokens, segment_ids=segment_ids, token_expert=token_expert, gates=gates, ln1_gain=ln1_gain, w_qkv=w_qkv, w_out=w_out, ln2_gain=ln2_gain, expert_in=expert_in, expert_out=expert_out, cotangent=cotangent)


@jax.custom_vjp
def low(v):
    return lax.optimization_barrier(v.astype(jnp.bfloat16)).astype(jnp.float32)

@jax.custom_vjp
def low_back(v):
    return v

def low_keep(v):
    return (low(v), None)

def low_pass(kept, grad):
    return (grad,)

def back_keep(v):
    return (v, None)

def back_low(kept, grad):
    return (low(grad),)
low.defvjp(low_keep, low_pass)
low_back.defvjp(back_keep, back_low)
HIGH = lax.Precision.HIGHEST
EPSILON = 1e-05
NEG_LARGE = -1e+30

def norm_apply(hidden, gain):
    centre = hidden - lax.optimization_barrier(jnp.mean(hidden, axis=-1, keepdims=True))
    spread = lax.optimization_barrier(jnp.mean(centre * centre, axis=-1, keepdims=True))
    return centre * lax.rsqrt(spread + EPSILON) * gain

def reference(tokens, segment_ids, token_expert, gates, ln1_gain, w_qkv, w_out, ln2_gain, expert_in, expert_out, cotangent):
    heads = D // HEAD_DIM
    scale = HEAD_DIM ** (-0.5)
    length = TOK_DEV
    group = math.gcd(SEQS, max(1, 4096 // length))
    ngroups = SEQS // group
    num_dev = N_DP * N_EXPERT
    per_dev = token_expert[:, 0].reshape(num_dev, TOK_DEV)
    onehot = (per_dev[:, :, None] == jnp.arange(EXPERTS, dtype=jnp.int32)[None, None, :]).astype(jnp.int32)
    ranking = lax.optimization_barrier(jnp.sum((jnp.cumsum(onehot, axis=1) - onehot) * onehot, axis=2))
    device_ids = jnp.arange(num_dev, dtype=jnp.int32)[:, None]
    slot_index = ((per_dev * num_dev + device_ids) * CAP + ranking).reshape(-1).astype(jnp.int32)
    segs = segment_ids.reshape(ngroups, group, length)
    positions = jnp.arange(length, dtype=jnp.int32)
    causal = positions[:, None] >= positions[None, :]

    def attend_group(args):
        qkv_group, seg_group = args
        queries = qkv_group[..., :D].reshape(group, length, heads, HEAD_DIM)
        keys_all = qkv_group[..., D:2 * D].reshape(group, length, heads, HEAD_DIM)
        values_all = qkv_group[..., 2 * D:].reshape(group, length, heads, HEAD_DIM)
        raw = jnp.einsum('gqhd,gkhd->ghqk', queries, keys_all, precision=HIGH)
        scores = low_back(raw) * scale
        allowed = causal[None] & (seg_group[:, :, None] == seg_group[:, None, :])
        scores = jnp.where(allowed[:, None], scores, NEG_LARGE)
        peak = lax.optimization_barrier(jnp.max(scores, axis=-1, keepdims=True))
        weights = jnp.exp(scores - peak)
        probs = weights / lax.optimization_barrier(jnp.sum(weights, axis=-1, keepdims=True))
        attended = jnp.einsum('ghqk,gkhd->gqhd', low(probs), values_all, precision=HIGH)
        return attended.reshape(group, length, D)

    def expert_apply(args):
        rows_in, weight_up, weight_down = args
        pre = low_back(jnp.dot(rows_in, weight_up, precision=HIGH))
        act = low(jax.nn.gelu(pre, approximate=False))
        return low(low_back(jnp.dot(act, weight_down, precision=HIGH)))

    def forward(x_in, gain_one, weight_qkv, weight_mix, gain_two, weight_up, weight_down):
        normed = low(norm_apply(x_in, gain_one))
        qkv = low(low_back(jnp.dot(normed, weight_qkv, precision=HIGH)))
        qkv_groups = qkv.reshape(ngroups, group, length, 3 * D)
        attended = lax.map(jax.checkpoint(attend_group), (qkv_groups, segs)).reshape(TOKENS, D)
        attended = low(low_back(attended))
        mixed = low_back(jnp.dot(attended, weight_mix, precision=HIGH))
        resid = x_in + mixed
        sent = low(low_back(norm_apply(resid, gain_two)))
        buffer = jnp.zeros((EXPERTS * num_dev * CAP, D), jnp.float32).at[slot_index].set(sent)
        buffer = buffer.reshape(EXPERTS, num_dev * CAP, D)
        produced = lax.map(jax.checkpoint(expert_apply), (buffer, weight_up, weight_down))
        expert_rows = produced.reshape(EXPERTS * num_dev * CAP, D)[slot_index]
        return resid + gates[:, None] * expert_rows
    x_in = tokens.astype(jnp.float32)
    result, back_fn = jax.vjp(forward, x_in, ln1_gain, w_qkv.astype(jnp.float32), w_out.astype(jnp.float32), ln2_gain, expert_in.astype(jnp.float32), expert_out.astype(jnp.float32))
    grad_x, grad_g1, grad_wqkv, grad_wmix, grad_g2, grad_up, grad_down = back_fn(cotangent.astype(jnp.float32))
    return (result.astype(jnp.bfloat16), grad_x.astype(jnp.bfloat16), grad_g1, grad_wqkv, grad_wmix, grad_g2, grad_up, grad_down)
```

```python
import jax
import jax.numpy as jnp
from jax import lax
from jax.sharding import PartitionSpec as P

HEAD_DIM = 64


EPSILON = 1e-05
NEG_LARGE = -1e30


def norm_apply(hidden, gain):
    centre = hidden - jnp.mean(hidden, axis=-1, keepdims=True)
    spread = jnp.mean(centre * centre, axis=-1, keepdims=True)
    return centre * lax.rsqrt(spread + EPSILON) * gain


def gelu_exact(values):
    return jax.nn.gelu(values, approximate=False)


def slot_places(experts_local, num_experts, capacity):
    position = jnp.arange(experts_local.shape[0], dtype=jnp.int32)
    earlier = (experts_local[:, None] == experts_local[None, :]) & (
        position[:, None] > position[None, :]
    )
    ranking = jnp.sum(earlier.astype(jnp.int32), axis=1)
    return experts_local * capacity + ranking


def allowed_block(start, block, segments):
    row_pos = start + jnp.arange(block, dtype=jnp.int32)
    col_pos = jnp.arange(segments.shape[0], dtype=jnp.int32)
    causal = row_pos[:, None] >= col_pos[None, :]
    same_doc = segments[:, None] == segments[None, :]
    return causal & same_doc


def block_scores(query_block, keys_all, allowed, scale):
    raw = jnp.einsum("qhd,khd->hqk", query_block, keys_all, preferred_element_type=jnp.float32)
    return jnp.where(allowed[None], raw * scale, NEG_LARGE)


def shards(
    tokens,
    segment_ids,
    token_expert,
    gates,
    ln1_gain,
    w_qkv,
    w_out,
    ln2_gain,
    expert_in,
    expert_out,
    cotangent,
):
    rows, width = tokens.shape
    heads = width // HEAD_DIM
    groups = lax.axis_size("expert")
    local_experts = expert_in.shape[0]
    num_experts = groups * local_experts
    capacity = 2 * rows // num_experts
    scale = HEAD_DIM ** (-0.5)
    block = min(rows, 512)
    segments = segment_ids[0]
    token_values = tokens.astype(jnp.float32)
    normed_low = norm_apply(token_values, ln1_gain).astype(jnp.bfloat16)
    qkv_low = jnp.dot(normed_low, w_qkv, preferred_element_type=jnp.float32).astype(jnp.bfloat16)
    queries = qkv_low[:, :width].reshape(rows, heads, HEAD_DIM)
    keys_all = qkv_low[:, width : 2 * width].reshape(rows, heads, HEAD_DIM)
    values_all = qkv_low[:, 2 * width :].reshape(rows, heads, HEAD_DIM)
    index = 0
    start = index * block
    allowed = allowed_block(start, block, segments)
    scores = block_scores(queries, keys_all, allowed, scale)
    peak = jnp.max(scores, axis=-1, keepdims=True)
    weights = jnp.exp(scores - peak)
    totals = jnp.sum(weights, axis=-1, keepdims=True)
    probs = weights / totals
    log_totals = [peak + jnp.log(totals)]
    attended_parts = jnp.einsum(
        "hqk,khd->qhd", probs.astype(jnp.bfloat16), values_all, preferred_element_type=jnp.float32
    )
    attended_low = attended_parts.reshape(rows, width).astype(jnp.bfloat16)
    mixed = jnp.dot(attended_low, w_out, preferred_element_type=jnp.float32)
    residual_one = token_values + mixed
    sent_low = norm_apply(residual_one, ln2_gain).astype(jnp.bfloat16)
    slot_index = slot_places(token_expert[:, 0], num_experts, capacity)
    place = (
        jnp.arange(num_experts * capacity, dtype=jnp.int32)[:, None] == slot_index[None, :]
    ).astype(jnp.bfloat16)
    dispatch_buffer = jnp.dot(place, sent_low, preferred_element_type=jnp.float32).astype(
        jnp.bfloat16
    )
    dispatch_buffer = dispatch_buffer.reshape(num_experts, capacity, width)
    arrived = lax.all_to_all(dispatch_buffer, "expert", split_axis=0, concat_axis=0, tiled=True)
    count = arrived.shape[1]
    grouped = arrived.reshape(groups, local_experts, count, width)
    hidden_pre = jnp.einsum(
        "nekd,edf->nekf", grouped, expert_in, preferred_element_type=jnp.float32
    )
    phi_big = 0.5 * (1.0 + lax.erf(hidden_pre * (0.5**0.5)))
    slope = phi_big + hidden_pre * jnp.exp(-0.5 * hidden_pre * hidden_pre) * 0.3989422804014327
    activated, slope = lax.optimization_barrier(
        ((hidden_pre * phi_big).astype(jnp.bfloat16), slope.astype(jnp.bfloat16))
    )
    produced = jnp.einsum(
        "nekf,efd->nekd", activated, expert_out, preferred_element_type=jnp.float32
    ).astype(jnp.bfloat16)
    produced, kept_pre, arrived_rows = (
        produced.reshape(num_experts, count, width),
        None,
        arrived,
    )
    returned = lax.all_to_all(produced, "expert", split_axis=0, concat_axis=0, tiled=True)
    expert_rows = jnp.einsum(
        "st,sd->td",
        place,
        returned.reshape(num_experts * capacity, width),
        preferred_element_type=jnp.float32,
    )
    gate_col = gates[:, None]
    block_out = (residual_one + gate_col * expert_rows).astype(jnp.bfloat16)
    upstream = cotangent.astype(jnp.float32)
    grad_send = (gate_col * upstream).astype(jnp.bfloat16)
    grad_buffer = jnp.dot(place, grad_send, preferred_element_type=jnp.float32).astype(
        jnp.bfloat16
    )
    grad_buffer = grad_buffer.reshape(num_experts, capacity, width)
    grad_arrived = lax.all_to_all(
        grad_buffer, "expert", split_axis=0, concat_axis=0, tiled=True
    ).reshape(groups, local_experts, capacity, width)
    arrived_group = arrived_rows.reshape(groups, local_experts, capacity, width)
    grad_w_down = jnp.einsum(
        "nekf,nekd->efd", activated, grad_arrived, preferred_element_type=jnp.float32
    )
    grad_act = jnp.einsum(
        "nekd,efd->nekf", grad_arrived, expert_out, preferred_element_type=jnp.float32
    )
    grad_pre = (grad_act * slope.astype(jnp.float32)).astype(jnp.bfloat16)
    grad_w_up = jnp.einsum(
        "nekd,nekf->edf", arrived_group, grad_pre, preferred_element_type=jnp.float32
    )
    grad_rows = jnp.einsum(
        "nekf,edf->nekd", grad_pre, expert_in, preferred_element_type=jnp.float32
    ).astype(jnp.bfloat16)
    grad_rows = grad_rows.reshape(num_experts, capacity, width)
    grad_back = lax.all_to_all(grad_rows, "expert", split_axis=0, concat_axis=0, tiled=True)
    grad_normed_two = jnp.einsum(
        "st,sd->td",
        place,
        grad_back.reshape(num_experts * capacity, width),
        preferred_element_type=jnp.float32,
    )
    down_share = lax.psum_scatter(
        grad_w_down.astype(jnp.bfloat16), "dp", scatter_dimension=1, tiled=True
    ).astype(jnp.float32)
    up_share = lax.psum_scatter(
        grad_w_up.astype(jnp.bfloat16), "dp", scatter_dimension=1, tiled=True
    ).astype(jnp.float32)
    norm_two_value, norm_two_back = jax.vjp(norm_apply, residual_one, ln2_gain)
    grad_resid_part, grad_gain_two = norm_two_back(grad_normed_two)
    grad_residual = upstream + grad_resid_part
    grad_mixed_low = grad_residual.astype(jnp.bfloat16)
    grad_w_mix = jnp.einsum(
        "td,te->de", attended_low, grad_mixed_low, preferred_element_type=jnp.float32
    )
    grad_attended = jnp.einsum(
        "te,de->td", grad_mixed_low, w_out, preferred_element_type=jnp.float32
    )
    grad_attended = grad_attended.astype(jnp.bfloat16).reshape(rows, heads, HEAD_DIM)
    index = 0
    start = index * block
    allowed = allowed_block(start, block, segments)
    scores = block_scores(queries, keys_all, allowed, scale)
    probs = jnp.exp(scores - log_totals[index])
    grad_values = jnp.einsum(
        "hqk,qhd->khd",
        probs.astype(jnp.bfloat16),
        grad_attended,
        preferred_element_type=jnp.float32,
    )
    grad_probs = jnp.einsum(
        "qhd,khd->hqk", grad_attended, values_all, preferred_element_type=jnp.float32
    )
    centre = jnp.sum(probs * grad_probs, axis=-1, keepdims=True)
    grad_scores = (probs * (grad_probs - centre) * scale).astype(jnp.bfloat16)
    grad_query_parts = jnp.einsum(
        "hqk,khd->qhd", grad_scores, keys_all, preferred_element_type=jnp.float32
    )
    grad_keys = jnp.einsum("hqk,qhd->khd", grad_scores, queries, preferred_element_type=jnp.float32)
    grad_qkv_low = jnp.concatenate(
        [
            grad_query_parts.reshape(rows, width),
            grad_keys.reshape(rows, width),
            grad_values.reshape(rows, width),
        ],
        axis=1,
    ).astype(jnp.bfloat16)
    grad_w_qkv = jnp.einsum(
        "td,te->de", normed_low, grad_qkv_low, preferred_element_type=jnp.float32
    )
    grad_normed_one = jnp.einsum(
        "te,de->td", grad_qkv_low, w_qkv, preferred_element_type=jnp.float32
    )
    norm_one_value, norm_one_back = jax.vjp(norm_apply, token_values, ln1_gain)
    grad_input_part, grad_gain_one = norm_one_back(grad_normed_one)
    grad_tokens = (grad_residual + grad_input_part).astype(jnp.bfloat16)
    copies = lax.axis_size("dp")
    gains = jnp.stack([grad_gain_one, grad_gain_two], 1)
    both = jnp.concatenate(
        [grad_w_qkv.reshape(width, copies, -1), grad_w_mix.reshape(width, copies, -1)], axis=2
    )
    both = both.astype(jnp.bfloat16).transpose(1, 0, 2)
    part = lax.psum_scatter(both, "expert", scatter_dimension=1, tiled=True)
    part = lax.psum_scatter(part, "dp", scatter_dimension=0, tiled=True)
    whole = lax.all_gather(part[0], "expert", axis=0, tiled=True).astype(jnp.float32)
    replica = lax.axis_index("dp")
    gain_cols = width // copies
    gains = lax.psum(gains, ("dp", "expert"))
    share_gain = lax.dynamic_slice_in_dim(gains, replica * gain_cols, gain_cols, 0)
    share_one, share_two = share_gain[:, 0], share_gain[:, 1]
    qkv_cols = 3 * width // copies
    share_qkv, share_mix = whole[:, :qkv_cols], whole[:, qkv_cols:]
    return (
        block_out,
        grad_tokens,
        share_one,
        share_qkv,
        share_mix,
        share_two,
        up_share,
        down_share,
    )


def solution(mesh):
    return jax.shard_map(
        shards,
        mesh=mesh,
        in_specs=(
            P(("dp", "expert"), None),
            P(("dp", "expert"), None),
            P(("dp", "expert"), None),
            P(("dp", "expert")),
            P(),
            P(),
            P(),
            P(),
            P("expert", None, None),
            P("expert", None, None),
            P(("dp", "expert"), None),
        ),
        out_specs=(
            P(("dp", "expert"), None),
            P(("dp", "expert"), None),
            P("dp"),
            P(None, "dp"),
            P(None, "dp"),
            P("dp"),
            P("expert", "dp", None),
            P("expert", "dp", None),
        ),
        check_vma=False,
    )
```

```python
import functools

import jax
import jax.numpy as jnp
from jax import lax
from jax.experimental import pallas as pl
from jax.experimental.pallas import tpu as pltpu
from jax.sharding import PartitionSpec as P

HEAD_DIM = 64
EPSILON = 1e-05
NEG_LARGE = -1e30
BAND = 128
PAIR = 2 * HEAD_DIM
GROUP = 256
CHUNK = 512
MIB = 2**20
MESH = pl.DeviceIdType.MESH
ANY = pl.BlockSpec(memory_space=pl.ANY)
VMEM = pl.BlockSpec(memory_space=pltpu.VMEM)
f32, bf16 = jnp.float32, jnp.bfloat16


def dot(a, b):
    return jnp.dot(a, b, preferred_element_type=f32)


def dot_nt(a, b):
    return lax.dot_general(a, b, (((1,), (1,)), ((), ())), preferred_element_type=f32)


def dot_tn(a, b):
    return lax.dot_general(a, b, (((0,), (0,)), ((), ())), preferred_element_type=f32)


def flip(index, bits):
    place = 1
    while bits:
        if bits % 2:
            index = index + place * (1 - 2 * ((index // place) % 2))
        bits, place = bits // 2, place * 2
    return index


def rows_at(start, size):
    return pl.ds(pl.multiple_of(start, size), size)


def greet(peers):
    barrier = pltpu.get_barrier_semaphore()
    for peer in peers:
        pl.semaphore_signal(barrier, inc=1, device_id=peer, device_id_type=MESH)
    pl.semaphore_wait(barrier, len(peers))


def band(index):
    first = max(0, index - 2) * BAND
    return first, (index + 1) * BAND - first


def column_of(row):
    size = row.shape[1]
    eye = lax.broadcasted_iota(jnp.int32, (size, size), 0) == lax.broadcasted_iota(
        jnp.int32, (size, size), 1
    )
    return jnp.sum(jnp.where(eye, row, 0.0), axis=1, keepdims=True)


def slot_row(experts, num_experts, capacity):
    rows = experts.shape[1]
    lines = max(16, num_experts)
    onehot = lax.broadcasted_iota(jnp.int32, (lines, rows), 0) == experts
    onehot = jnp.where(onehot, 1.0, 0.0)
    before = lax.broadcasted_iota(jnp.int32, (rows, rows), 0) < lax.broadcasted_iota(
        jnp.int32, (rows, rows), 1
    )
    earlier = dot(onehot.astype(bf16), jnp.where(before, 1.0, 0.0).astype(bf16))
    rank = jnp.sum(onehot * earlier, axis=0, keepdims=True)
    return experts.astype(f32) * float(capacity) + rank


def centred(hidden):
    centre = hidden - jnp.mean(hidden, axis=-1, keepdims=True)
    spread = jnp.mean(centre * centre, axis=-1, keepdims=True)
    return centre, lax.rsqrt(spread + EPSILON)


def gelu_pair(x):
    bell = jnp.exp(-0.5 * x * x)
    t = 1.0 / (1.0 + (0.3275911 * 0.7071067811865476) * jnp.abs(x))
    poly = 0.5 * 1.061405429
    for factor in (-1.453152027, 1.421413741, -0.284496736, 0.254829592):
        poly = poly * t + 0.5 * factor
    tail = poly * t * bell
    phi = jnp.where(x >= 0.0, 1.0 - tail, tail)
    return x * phi, phi + x * (bell * 0.3989422804014327)


def forward_kernel(
    groups, cap, tok_hbm, seg_ref, te_ref, gate_ref, g1_ref, wqkv_hbm, wout_hbm, g2_ref, win_hbm,
    cot_hbm, h1_out, qkv_out, att_out, probs_out, v_out, gy_out, act_out, slope_out, gdown_out,
    tok, cot, wqkv, wout, win, low, qkv, att, probs, bias, h1, place, sent, gy_send, gy_got, v_got,
    act, slope, gdown, load, store, gy_ssem, gy_rsem, v_ssem, v_rsem,
):
    dp, me = lax.axis_index("dp"), lax.axis_index("expert")
    rows, width = tok.shape
    slots, hidden = act.shape
    loads = [
        pltpu.make_async_copy(src, dst, load.at[i])
        for i, (src, dst) in enumerate(
            ((cot_hbm, cot), (tok_hbm, tok), (wqkv_hbm, wqkv), (wout_hbm, wout), (win_hbm, win))
        )
    ]
    for one in loads:
        one.start()
    greet([(dp, flip(me, k)) for k in range(1, groups)])

    def exchange(source, target, send, receive, k):
        peer = flip(me, k)
        return pltpu.make_async_remote_copy(
            src_ref=source.at[rows_at(peer * cap, cap)],
            dst_ref=target.at[rows_at(me * cap, cap)],
            send_sem=send.at[k],
            recv_sem=receive.at[k],
            device_id=(dp, peer),
            device_id_type=MESH,
        )

    spot = slot_row(te_ref[...], groups, cap)

    @pl.loop(0, slots // GROUP)
    def _(g):
        here = lax.broadcasted_iota(jnp.int32, (GROUP, rows), 0) + g * GROUP
        place[rows_at(g * GROUP, GROUP)] = jnp.where(here.astype(f32) == spot, 1.0, 0.0).astype(
            bf16
        )

    loads[0].wait()
    gate = column_of(gate_ref[...])
    low[...] = (gate * cot[...].astype(f32)).astype(bf16)

    @pl.loop(0, slots // GROUP)
    def _(g):
        at = rows_at(g * GROUP, GROUP)
        gy_send[at] = dot(place[at], low[...]).astype(bf16)

    gy_copies = [exchange(gy_send, gy_got, gy_ssem, gy_rsem, k) for k in range(1, groups)]
    for one in gy_copies[::-1]:
        one.start()
    mine = rows_at(me * cap, cap)
    gy_got[mine] = gy_send[mine]

    segs = seg_ref[...].astype(f32)
    seg_col = column_of(segs)
    for i in range(rows // BAND):
        first, wide = band(i)
        causal = (lax.broadcasted_iota(jnp.int32, (BAND, wide), 0) + i * BAND) >= (
            lax.broadcasted_iota(jnp.int32, (BAND, wide), 1) + first
        )
        same = seg_col[i * BAND : (i + 1) * BAND] == segs[:, first : first + wide]
        bias[i * BAND : (i + 1) * BAND, 0:wide] = jnp.where(causal & same, 0.0, NEG_LARGE)

    loads[1].wait()

    @pl.loop(0, rows // BAND)
    def _(r):
        at = rows_at(r * BAND, BAND)
        centre, inverse = centred(tok[at].astype(f32))
        low[at] = (centre * inverse * g1_ref[...]).astype(bf16)

    loads[2].wait()

    @pl.loop(0, 3 * width // GROUP)
    def _(c):
        at = rows_at(c * GROUP, GROUP)
        qkv[:, at] = dot(low[...], wqkv[:, at]).astype(bf16)

    left = lax.broadcasted_iota(jnp.int32, (1, PAIR), 1) < HEAD_DIM
    none = jnp.zeros((), bf16)

    @pl.loop(0, width // PAIR)
    def _(h):
        at = rows_at(h * PAIR, PAIR)
        k_at = rows_at(width + h * PAIR, PAIR)
        v_at = rows_at(2 * width + h * PAIR, PAIR)
        for i in range(rows // BAND):
            first, wide = band(i)
            mine = slice(i * BAND, (i + 1) * BAND)
            keys = qkv[first : first + wide, k_at]
            values = qkv[first : first + wide, v_at]
            query = qkv[mine, at] * jnp.asarray(HEAD_DIM**-0.5, bf16)
            both = []
            for side in range(2):
                part = jnp.where(left, query, none) if side == 0 else jnp.where(left, none, query)
                scores = dot_nt(part, keys) + bias[mine, 0:wide]
                weights = jnp.exp(scores - jnp.max(scores, axis=-1, keepdims=True))
                share = weights * (1.0 / jnp.sum(weights, axis=-1, keepdims=True))
                share = share.astype(bf16)
                probs[2 * h + side, mine, 0:wide] = share
                both.append(dot(share, values))
            att[mine, at] = jnp.where(left, both[0], both[1]).astype(bf16)

    stores = [
        pltpu.make_async_copy(src, dst, store.at[i])
        for i, (src, dst) in enumerate(
            (
                (qkv, qkv_out), (probs, probs_out), (att, att_out), (h1, h1_out), (gy_got, gy_out),
                (v_got, v_out), (act, act_out), (slope, slope_out), (gdown, gdown_out),
            )
        )
    ]
    for i in range(3):
        stores[i].start()
    loads[3].wait()

    @pl.loop(0, rows // BAND)
    def _(r):
        at = rows_at(r * BAND, BAND)
        resid = tok[at].astype(f32) + dot(att[at], wout[...])
        h1[at] = resid
        centre, inverse = centred(resid)
        low[at] = (centre * inverse * g2_ref[...]).astype(bf16)

    stores[3].start()

    @pl.loop(0, slots // GROUP)
    def _(g):
        at = rows_at(g * GROUP, GROUP)
        sent[at] = dot(place[at], low[...]).astype(bf16)

    v_copies = [exchange(sent, v_got, v_ssem, v_rsem, k) for k in range(1, groups)]
    for one in v_copies[::-1]:
        one.start()
    v_got[mine] = sent[mine]
    loads[4].wait()

    many = GROUP // cap
    for g in range(slots // GROUP):
        for k in range(g * many, (g + 1) * many):
            if k:
                v_copies[k - 1].wait_recv()
        at = rows_at(flip(me // many, g) * GROUP, GROUP)

        @pl.loop(0, hidden // CHUNK)
        def _(c):
            cols = rows_at(c * CHUNK, CHUNK)
            value, back = gelu_pair(dot(v_got[at], win[:, cols]))
            act[at, cols] = value.astype(bf16)
            slope[at, cols] = back.astype(bf16)

    for one in gy_copies:
        one.wait_recv()
    for i in range(4, 8):
        stores[i].start()

    @pl.loop(0, hidden // GROUP)
    def _(c):
        at = rows_at(c * GROUP, GROUP)
        gdown[at] = dot_tn(act[:, at], gy_got[...]).astype(bf16)

    stores[8].start()
    for one in gy_copies + v_copies:
        one.wait_send()
    for one in stores:
        one.wait()


def forward(groups, cap, tokens, segs, experts, gates, g1, w_qkv, w_out, g2, w_in, cot):
    rows, width = tokens.shape
    hidden = w_in.shape[1]
    slots = groups * cap
    heads = width // HEAD_DIM
    wide = 3 * BAND
    shapes = dict(
        h1=((rows, width), f32), qkv=((rows, 3 * width), bf16), att=((rows, width), bf16),
        probs=((heads, rows, wide), bf16), v=((slots, width), bf16), gy=((slots, width), bf16),
        act=((slots, hidden), bf16), slope=((slots, hidden), bf16), gdown=((hidden, width), bf16),
    )
    sems = pltpu.SemaphoreType.DMA
    return pl.pallas_call(
        functools.partial(forward_kernel, groups, cap),
        out_shape=[jax.ShapeDtypeStruct(*one) for one in shapes.values()],
        in_specs=[ANY, VMEM, VMEM, VMEM, VMEM, ANY, ANY, VMEM, ANY, ANY],
        out_specs=[ANY] * len(shapes),
        scratch_shapes=[
            pltpu.VMEM((rows, width), bf16), pltpu.VMEM((rows, width), bf16),
            pltpu.VMEM(w_qkv.shape, bf16), pltpu.VMEM(w_out.shape, bf16),
            pltpu.VMEM(w_in.shape, bf16), pltpu.VMEM((rows, width), bf16),
            pltpu.VMEM((rows, 3 * width), bf16), pltpu.VMEM((rows, width), bf16),
            pltpu.VMEM((heads, rows, wide), bf16), pltpu.VMEM((rows, wide), f32),
            pltpu.VMEM((rows, width), f32), pltpu.VMEM((slots, rows), bf16),
            pltpu.VMEM((slots, width), bf16), pltpu.VMEM((slots, width), bf16),
            pltpu.VMEM((slots, width), bf16), pltpu.VMEM((slots, width), bf16),
            pltpu.VMEM((slots, hidden), bf16), pltpu.VMEM((slots, hidden), bf16),
            pltpu.VMEM((hidden, width), bf16),
            sems((5,)), sems((9,)), sems((groups,)), sems((groups,)), sems((groups,)),
            sems((groups,)),
        ],
        compiler_params=pltpu.CompilerParams(
            collective_id=0, has_side_effects=True, vmem_limit_bytes=60 * MIB
        ),
        cost_estimate=pl.CostEstimate(
            flops=20 * 10**9, bytes_accessed=40 * 10**6, transcendentals=10**7
        ),
        name="forward",
    )(tokens, segs, experts, gates, g1, w_qkv, w_out, g2, w_in, cot)


def expert_kernel(
    groups, cap, v_hbm, gy_hbm, act_hbm, slope_hbm, win_hbm, wout_hbm, gup_out, gv_out, y_out,
    v, gy, act, slope, win, wout, turned, gpre, gup, gv_send, y_send, gv_got, y_got,
    load, store, gv_ssem, gv_rsem, y_ssem, y_rsem,
):
    dp, me = lax.axis_index("dp"), lax.axis_index("expert")
    slots, width = v.shape
    hidden = act.shape[1]
    loads = [
        pltpu.make_async_copy(src, dst, load.at[i])
        for i, (src, dst) in enumerate(
            (
                (gy_hbm, gy), (wout_hbm, wout), (slope_hbm, slope), (win_hbm, win), (act_hbm, act),
                (v_hbm, v),
            )
        )
    ]
    for one in loads:
        one.start()
    greet([(dp, flip(me, k)) for k in range(1, groups)])

    def exchange(source, target, send, receive, k):
        peer = flip(me, k)
        return pltpu.make_async_remote_copy(
            src_ref=source.at[rows_at(peer * cap, cap)],
            dst_ref=target.at[rows_at(me * cap, cap)],
            send_sem=send.at[k],
            recv_sem=receive.at[k],
            device_id=(dp, peer),
            device_id_type=MESH,
        )

    mine = rows_at(me * cap, cap)
    many = GROUP // cap
    last = slots // GROUP - 1
    gv_copies = [exchange(gv_send, gv_got, gv_ssem, gv_rsem, k) for k in range(1, groups)]
    y_copies = [exchange(y_send, y_got, y_ssem, y_rsem, k) for k in range(1, groups)]
    for i in range(3):
        loads[i].wait()
    for g in range(last, -1, -1):
        at = rows_at(flip(me // many, g) * GROUP, GROUP)

        @pl.loop(0, hidden // CHUNK)
        def _(c):
            cols = rows_at(c * CHUNK, CHUNK)
            up = dot_nt(gy[at], wout[cols])
            gpre[at, cols] = (up * slope[at, cols].astype(f32)).astype(bf16)

        if g == last:
            loads[3].wait()

        @pl.loop(0, width // GROUP)
        def _(n):
            cols = rows_at(n * GROUP, GROUP)
            gv_send[at, cols] = dot_nt(gpre[at], win[cols]).astype(bf16)

        for k in range(g * many, (g + 1) * many):
            if k:
                gv_copies[k - 1].start()
    gv_got[mine] = gv_send[mine]
    loads[4].wait()
    for g in range(last, -1, -1):
        at = rows_at(flip(me // many, g) * GROUP, GROUP)

        @pl.loop(0, width // GROUP)
        def _(n):
            cols = rows_at(n * GROUP, GROUP)
            y_send[at, cols] = dot(act[at], wout[:, cols]).astype(bf16)

        for k in range(g * many, (g + 1) * many):
            if k:
                y_copies[k - 1].start()
    y_got[mine] = y_send[mine]
    loads[5].wait()
    turned[...] = v[...].T

    @pl.loop(0, hidden // GROUP)
    def _(c):
        cols = rows_at(c * GROUP, GROUP)
        gup[:, cols] = dot(turned[...], gpre[:, cols]).astype(bf16)

    outs = [pltpu.make_async_copy(gup, gup_out, store.at[0])]
    outs[0].start()
    for one in gv_copies:
        one.wait_recv()
    outs.append(pltpu.make_async_copy(gv_got, gv_out, store.at[1]))
    outs[1].start()
    for one in y_copies:
        one.wait_recv()
    outs.append(pltpu.make_async_copy(y_got, y_out, store.at[2]))
    outs[2].start()
    for one in gv_copies + y_copies:
        one.wait_send()
    for one in outs:
        one.wait()


def experts_back(groups, cap, v, gy, act, slope, w_in, w_out):
    slots, width = v.shape
    hidden = act.shape[1]
    sems = pltpu.SemaphoreType.DMA
    return pl.pallas_call(
        functools.partial(expert_kernel, groups, cap),
        out_shape=[
            jax.ShapeDtypeStruct((width, hidden), bf16),
            jax.ShapeDtypeStruct((slots, width), bf16),
            jax.ShapeDtypeStruct((slots, width), bf16),
        ],
        in_specs=[ANY] * 6,
        out_specs=[ANY] * 3,
        scratch_shapes=[
            pltpu.VMEM((slots, width), bf16), pltpu.VMEM((slots, width), bf16),
            pltpu.VMEM((slots, hidden), bf16), pltpu.VMEM((slots, hidden), bf16),
            pltpu.VMEM((width, hidden), bf16), pltpu.VMEM((hidden, width), bf16),
            pltpu.VMEM((width, slots), bf16), pltpu.VMEM((slots, hidden), bf16),
            pltpu.VMEM((width, hidden), bf16),
            pltpu.VMEM((slots, width), bf16), pltpu.VMEM((slots, width), bf16),
            pltpu.VMEM((slots, width), bf16), pltpu.VMEM((slots, width), bf16),
            sems((6,)), sems((3,)), sems((groups,)), sems((groups,)), sems((groups,)),
            sems((groups,)),
        ],
        compiler_params=pltpu.CompilerParams(
            collective_id=1, has_side_effects=True, vmem_limit_bytes=60 * MIB
        ),
        cost_estimate=pl.CostEstimate(
            flops=20 * 10**9, bytes_accessed=40 * 10**6, transcendentals=0
        ),
        name="experts_back",
    )(v, gy, act, slope, w_in, w_out)


def dense_kernel(
    groups, cap, gvr_hbm, yr_hbm, te_ref, gate_ref, h1_hbm, cot_hbm, tok_hbm, g1_ref, g2_ref,
    att_hbm, probs_hbm, qkv_hbm, wqkv_hbm, wout_hbm, block_out, gtok_out, dense_out, gains_out,
    gvr, yr, h1, cot, tok, att, probs, qkv, wqkv, wout, place, gh1, low, gatt, gqkv, turned,
    gk, gvv, dense, outv, load, store,
):
    rows, width = tok.shape
    slots = gvr.shape[0]
    loads = [
        pltpu.make_async_copy(src, dst, load.at[i])
        for i, (src, dst) in enumerate(
            (
                (gvr_hbm, gvr), (h1_hbm, h1), (cot_hbm, cot), (yr_hbm, yr), (att_hbm, att),
                (wout_hbm, wout), (qkv_hbm, qkv), (probs_hbm, probs), (tok_hbm, tok),
                (wqkv_hbm, wqkv),
            )
        )
    ]
    for one in loads:
        one.start()
    spot = column_of(slot_row(te_ref[...], groups, cap))
    for r in range(rows // BAND):
        at = slice(r * BAND, (r + 1) * BAND)
        here = lax.broadcasted_iota(jnp.int32, (BAND, slots), 1).astype(f32)
        place[at] = jnp.where(here == spot[at], 1.0, 0.0).astype(bf16)
    gate = column_of(gate_ref[...])
    for i in range(4):
        loads[i].wait()
    gains_out[...] = jnp.zeros_like(gains_out)
    for r in range(rows // BAND):
        at = slice(r * BAND, (r + 1) * BAND)
        back = dot(place[at], gvr[...])
        resid = h1[at]
        centre, inverse = centred(resid)
        unit = centre * inverse
        gains_out[1:2] += jnp.sum(back * unit, axis=0, keepdims=True)
        slant = back * g2_ref[...]
        inner = slant - jnp.mean(slant, axis=-1, keepdims=True)
        inner = inner - unit * jnp.mean(slant * unit, axis=-1, keepdims=True)
        grad = cot[at].astype(f32) + inverse * inner
        gh1[at] = grad
        low[at] = grad.astype(bf16)
        outv[at] = (resid + gate[at] * dot(place[at], yr[...])).astype(bf16)
    out_one = pltpu.make_async_copy(outv, block_out, store.at[0])
    out_one.start()
    loads[4].wait()
    loads[5].wait()

    @pl.loop(0, width // GROUP)
    def _(n):
        cols = rows_at(n * GROUP, GROUP)
        gatt[:, cols] = dot_nt(low[...], wout[cols]).astype(bf16)

    turned[...] = att[...].T

    @pl.loop(0, width // GROUP)
    def _(n):
        cols = rows_at(n * GROUP, GROUP)
        dense[0:width, rows_at(3 * width + n * GROUP, GROUP)] = dot(
            turned[...], low[:, cols]
        ).astype(bf16)

    loads[6].wait()
    loads[7].wait()
    left = lax.broadcasted_iota(jnp.int32, (1, PAIR), 1) < HEAD_DIM
    none = jnp.zeros((), bf16)

    def halves(block):
        return jnp.concatenate([jnp.where(left, block, none), jnp.where(left, none, block)], axis=0)

    @pl.loop(0, width // PAIR)
    def _(h):
        at = rows_at(h * PAIR, PAIR)
        k_at = rows_at(width + h * PAIR, PAIR)
        v_at = rows_at(2 * width + h * PAIR, PAIR)
        gk[...] = jnp.zeros_like(gk)
        gvv[...] = jnp.zeros_like(gvv)
        for i in range(rows // BAND):
            first, wide = band(i)
            mine, seen = slice(i * BAND, (i + 1) * BAND), slice(first, first + wide)
            keys, values = qkv[seen, k_at], qkv[seen, v_at]
            query, grad = halves(qkv[mine, at]), halves(gatt[mine, at])
            share = jnp.concatenate(
                [probs[2 * h, mine, 0:wide], probs[2 * h + 1, mine, 0:wide]], axis=0
            )
            gprobs = dot_nt(grad, values)
            wider = share.astype(f32)
            middle = jnp.sum(wider * gprobs, axis=-1, keepdims=True)
            graw = (wider * (gprobs - middle) * HEAD_DIM**-0.5).astype(bf16)
            gquery = dot(graw, keys)
            gqkv[mine, at] = jnp.where(left, gquery[0:BAND], gquery[BAND:]).astype(bf16)
            gk[seen] += dot_tn(graw, query)
            gvv[seen] += dot_tn(share, grad)
        gqkv[:, k_at] = gk[...].astype(bf16)
        gqkv[:, v_at] = gvv[...].astype(bf16)

    loads[8].wait()
    loads[9].wait()
    for r in range(rows // BAND):
        at = slice(r * BAND, (r + 1) * BAND)
        centre, inverse = centred(tok[at].astype(f32))
        low[at] = (centre * inverse * g1_ref[...]).astype(bf16)
    turned[...] = low[...].T

    @pl.loop(0, 3 * width // GROUP)
    def _(n):
        cols = rows_at(n * GROUP, GROUP)
        dense[0:width, cols] = dot(turned[...], gqkv[:, cols]).astype(bf16)

    out_two = pltpu.make_async_copy(dense, dense_out, store.at[1])
    out_two.start()
    out_one.wait()
    for r in range(rows // BAND):
        at = slice(r * BAND, (r + 1) * BAND)
        back = dot_nt(gqkv[at], wqkv[...])
        centre, inverse = centred(tok[at].astype(f32))
        unit = centre * inverse
        gains_out[0:1] += jnp.sum(back * unit, axis=0, keepdims=True)
        slant = back * g1_ref[...]
        inner = slant - jnp.mean(slant, axis=-1, keepdims=True)
        inner = inner - unit * jnp.mean(slant * unit, axis=-1, keepdims=True)
        outv[at] = (gh1[at] + inverse * inner).astype(bf16)
    out_three = pltpu.make_async_copy(outv, gtok_out, store.at[0])
    out_three.start()
    out_two.wait()
    out_three.wait()


def dense_back(groups, cap, per, gvr, yr, experts, gates, h1, cot, tok, g1, g2, att, probs, qkv, w_qkv, w_out):
    rows, width = tok.shape
    slots = gvr.shape[0]
    sems = pltpu.SemaphoreType.DMA
    return pl.pallas_call(
        functools.partial(dense_kernel, groups, cap),
        out_shape=[
            jax.ShapeDtypeStruct((rows, width), bf16),
            jax.ShapeDtypeStruct((rows, width), bf16),
            jax.ShapeDtypeStruct((groups * per, 4 * width), bf16),
            jax.ShapeDtypeStruct((8, width), f32),
        ],
        in_specs=[ANY, ANY, VMEM, VMEM, ANY, ANY, ANY, VMEM, VMEM, ANY, ANY, ANY, ANY, ANY],
        out_specs=[ANY, ANY, ANY, VMEM],
        scratch_shapes=[
            pltpu.VMEM((slots, width), bf16), pltpu.VMEM((slots, width), bf16),
            pltpu.VMEM((rows, width), f32), pltpu.VMEM((rows, width), bf16),
            pltpu.VMEM((rows, width), bf16), pltpu.VMEM((rows, width), bf16),
            pltpu.VMEM(probs.shape, bf16), pltpu.VMEM(qkv.shape, bf16),
            pltpu.VMEM(w_qkv.shape, bf16), pltpu.VMEM(w_out.shape, bf16),
            pltpu.VMEM((rows, slots), bf16), pltpu.VMEM((rows, width), f32),
            pltpu.VMEM((rows, width), bf16), pltpu.VMEM((rows, width), bf16),
            pltpu.VMEM((rows, 3 * width), bf16), pltpu.VMEM((width, rows), bf16),
            pltpu.VMEM((rows, PAIR), f32), pltpu.VMEM((rows, PAIR), f32),
            pltpu.VMEM((groups * per, 4 * width), bf16), pltpu.VMEM((rows, width), bf16),
            sems((10,)), sems((2,)),
        ],
        compiler_params=pltpu.CompilerParams(vmem_limit_bytes=60 * MIB),
        cost_estimate=pl.CostEstimate(
            flops=20 * 10**9, bytes_accessed=40 * 10**6, transcendentals=0
        ),
        name="dense_back",
    )(gvr, yr, experts, gates, h1, cot, tok, g1, g2, att, probs, qkv, w_qkv, w_out)


def sum_kernel(
    groups, copies, dense_hbm, gains_ref, out_ref, total_ref,
    own, other, part, got, ring, ring_got, final, gains_pair, gains_chip, gains_part, gains_ring,
    load, s_pair, r_pair, s_chip, r_chip, s_ring, r_ring, s_out, r_out, s_gain, r_gain,
):
    dp, me = lax.axis_index("dp"), lax.axis_index("expert")
    half = groups // 2
    per, wide = got.shape[1:]
    width = wide // 4
    chip, core = me // 2, me % 2
    there = flip(me, 1)
    chips = [flip(chip, k) for k in range(half)]
    rounds = [lax.rem(dp + k, copies) for k in range(copies)]
    keep = pltpu.make_async_copy(
        dense_hbm.at[rows_at(core * (half * per), half * per)], own, load.at[0]
    )
    keep.start()
    greet(
        [(dp, flip(me, k)) for k in range(1, groups)] + [(one, me) for one in rounds[1:]]
    )

    def send(source, target, ssem, rsem, device):
        return pltpu.make_async_remote_copy(
            src_ref=source, dst_ref=target, send_sem=ssem, recv_sem=rsem, device_id=device,
            device_id_type=MESH,
        )

    started = []

    def go(copy):
        copy.start()
        started.append(copy)
        return copy

    pair = []
    for k in range(half - 1, -1, -1):
        block = chips[k]
        pair.append(
            go(
                send(
                    dense_hbm.at[rows_at(((1 - core) * half + block) * per, per)],
                    other.at[rows_at(block * per, per)],
                    s_pair.at[k], r_pair.at[k], (dp, there),
                )
            )
        )
    gain_pair = go(send(gains_ref, gains_pair, s_gain.at[0], r_gain.at[0], (dp, there)))
    keep.wait()
    far = {}
    for i, k in enumerate(range(half - 1, -1, -1)):
        at = rows_at(chips[k] * per, per)
        pair[i].wait_recv()
        part[at] = (own[at].astype(f32) + other[at].astype(f32)).astype(bf16)
        if k:
            far[k] = go(
                send(part.at[at], got.at[k], s_chip.at[k], r_chip.at[k], (dp, chips[k] * 2 + core))
            )
    gain_pair.wait_recv()
    gains_part[0] = gains_ref[...] + gains_pair[...]
    gain_far = [
        go(
            send(
                gains_part.at[0], gains_chip.at[k], s_gain.at[k], r_gain.at[k],
                (dp, chips[k] * 2 + core),
            )
        )
        for k in range(1, half)
    ]
    total = part[rows_at(chip * per, per)].astype(f32)
    for k in range(1, half):
        far[k].wait_recv()
        total = total + got[k].astype(f32)
    share = 3 * width // copies
    thin = width // copies
    for d in range(copies):
        ring[d] = jnp.concatenate(
            [
                total[:, d * share : (d + 1) * share],
                total[:, 3 * width + d * thin : 3 * width + (d + 1) * thin],
            ],
            axis=1,
        ).astype(bf16)
    around = [
        go(send(ring.at[rounds[k]], ring_got.at[k], s_ring.at[k], r_ring.at[k], (rounds[k], me)))
        for k in range(1, copies)
    ]
    gains = gains_part[0]
    for k in range(1, half):
        gain_far[k - 1].wait_recv()
        gains = gains + gains_chip[k]
    gains_part[1] = gains
    gain_around = [
        go(
            send(
                gains_part.at[1], gains_ring.at[k], s_gain.at[half + k], r_gain.at[half + k],
                (rounds[k], me),
            )
        )
        for k in range(1, copies)
    ]
    summed = ring[dp].astype(f32)
    for k in range(1, copies):
        around[k - 1].wait_recv()
        summed = summed + ring_got[k].astype(f32)
    place = rows_at((core * half + chip) * per, per)
    final[...] = summed.astype(bf16)
    out_ref[place] = final[...]
    spread = [
        go(send(final, out_ref.at[place], s_out.at[k], r_out.at[k], (dp, flip(me, k))))
        for k in range(groups - 1, 0, -1)
    ]
    for k in range(1, copies):
        gain_around[k - 1].wait_recv()
        gains = gains + gains_ring[k]
    total_ref[...] = gains
    for one in spread:
        one.wait_recv()
    for one in started:
        one.wait_send()


def dense_sum(groups, copies, dense, gains):
    wide = dense.shape[1]
    per = dense.shape[0] // groups
    half = groups // 2
    thin = wide // copies
    sems = pltpu.SemaphoreType.DMA
    tile = gains.shape
    return pl.pallas_call(
        functools.partial(sum_kernel, groups, copies),
        out_shape=[
            jax.ShapeDtypeStruct((groups * per, thin), bf16),
            jax.ShapeDtypeStruct(tile, f32),
        ],
        in_specs=[ANY, VMEM],
        out_specs=[VMEM, VMEM],
        scratch_shapes=[
            pltpu.VMEM((half * per, wide), bf16), pltpu.VMEM((half * per, wide), bf16),
            pltpu.VMEM((half * per, wide), bf16), pltpu.VMEM((half, per, wide), bf16),
            pltpu.VMEM((copies, per, thin), bf16), pltpu.VMEM((copies, per, thin), bf16),
            pltpu.VMEM((per, thin), bf16),
            pltpu.VMEM(tile, f32), pltpu.VMEM((half, *tile), f32), pltpu.VMEM((2, *tile), f32),
            pltpu.VMEM((copies, *tile), f32),
            sems((1,)), sems((half,)), sems((half,)), sems((half,)), sems((half,)),
            sems((copies,)), sems((copies,)), sems((groups,)), sems((groups,)),
            sems((half + copies,)), sems((half + copies,)),
        ],
        compiler_params=pltpu.CompilerParams(
            collective_id=2, has_side_effects=True, vmem_limit_bytes=40 * MIB
        ),
        cost_estimate=pl.CostEstimate(
            flops=20 * 10**9, bytes_accessed=100 * 10**6, transcendentals=0
        ),
        name="dense_sum",
    )(dense, gains)


def shards(
    tokens, segment_ids, token_expert, gates, ln1_gain, w_qkv, w_out, ln2_gain, expert_in,
    expert_out, cotangent,
):
    rows, width = tokens.shape
    groups, copies = lax.axis_size("expert"), lax.axis_size("dp")
    cap = 2 * rows // groups
    per = -(-width // (16 * groups)) * 16
    w_in, w_down = expert_in[0], expert_out[0]
    experts, gate_row = token_expert.reshape(1, rows), gates.reshape(1, rows)
    g1, g2 = ln1_gain.reshape(1, width), ln2_gain.reshape(1, width)
    h1, qkv, att, probs, v, gy, act, slope, gdown = forward(
        groups, cap, tokens, segment_ids, experts, gate_row, g1, w_qkv, w_out, g2, w_in, cotangent
    )
    down_share = lax.psum_scatter(gdown[None], "dp", scatter_dimension=1, tiled=True)
    gup, gv_slots, y_slots = experts_back(groups, cap, v, gy, act, slope, w_in, w_down)
    up_share = lax.psum_scatter(gup[None], "dp", scatter_dimension=1, tiled=True)
    block_out, grad_tokens, dense, gains = dense_back(
        groups, cap, per, gv_slots, y_slots, experts, gate_row, h1, cotangent, tokens, g1, g2, att,
        probs, qkv, w_qkv, w_out,
    )
    whole, gains = dense_sum(groups, copies, dense, gains)
    whole = whole[:width].astype(f32)
    share = width // copies
    gains = lax.dynamic_slice_in_dim(gains, lax.axis_index("dp") * share, share, 1)
    return (
        block_out,
        grad_tokens,
        gains[0],
        whole[:, : 3 * share],
        whole[:, 3 * share :],
        gains[1],
        up_share.astype(f32),
        down_share.astype(f32),
    )


def solution(mesh):
    tokens, experts = P(("dp", "expert"), None), P("expert", None, None)
    return jax.shard_map(
        shards,
        mesh=mesh,
        in_specs=(
            tokens, tokens, tokens, P(("dp", "expert")), P(), P(), P(), P(), experts, experts,
            tokens,
        ),
        out_specs=(
            tokens, tokens, P("dp"), P(None, "dp"), P(None, "dp"), P("dp"),
            P("expert", "dp", None), P("expert", "dp", None),
        ),
        check_vma=False,
    )
```

```python
import functools

import jax
import jax.numpy as jnp
from jax import lax
from jax.experimental import pallas as pl
from jax.experimental.pallas import tpu as pltpu
from jax.sharding import PartitionSpec as P

HEAD_DIM = 64
EPSILON = 1e-05
NEG_LARGE = -1e30
BAND = 128
PAIR = 2 * HEAD_DIM
GROUP = 256
CHUNK = 512
MIB = 2**20
MESH = pl.DeviceIdType.MESH
ANY = pl.BlockSpec(memory_space=pl.ANY)
VMEM = pl.BlockSpec(memory_space=pltpu.VMEM)
f32, bf16 = jnp.float32, jnp.bfloat16


def dot(a, b):
    return jnp.dot(a, b, preferred_element_type=f32)


def dot_nt(a, b):
    return lax.dot_general(a, b, (((1,), (1,)), ((), ())), preferred_element_type=f32)


def dot_tn(a, b):
    return lax.dot_general(a, b, (((0,), (0,)), ((), ())), preferred_element_type=f32)


def flip(index, bits):
    place = 1
    while bits:
        if bits % 2:
            index = index + place * (1 - 2 * ((index // place) % 2))
        bits, place = bits // 2, place * 2
    return index


def rows_at(start, size):
    return pl.ds(pl.multiple_of(start, size), size)


def greet(peers):
    barrier = pltpu.get_barrier_semaphore()
    for peer in peers:
        pl.semaphore_signal(barrier, inc=1, device_id=peer, device_id_type=MESH)
    pl.semaphore_wait(barrier, len(peers))


def band(index):
    first = max(0, index - 2) * BAND
    return first, (index + 1) * BAND - first


def column_of(row):
    size = row.shape[1]
    eye = lax.broadcasted_iota(jnp.int32, (size, size), 0) == lax.broadcasted_iota(
        jnp.int32, (size, size), 1
    )
    return jnp.sum(jnp.where(eye, row, 0.0), axis=1, keepdims=True)


def slot_row(experts, num_experts, capacity):
    rows = experts.shape[1]
    lines = max(16, num_experts)
    onehot = lax.broadcasted_iota(jnp.int32, (lines, rows), 0) == experts
    onehot = jnp.where(onehot, 1.0, 0.0)
    before = lax.broadcasted_iota(jnp.int32, (rows, rows), 0) < lax.broadcasted_iota(
        jnp.int32, (rows, rows), 1
    )
    earlier = dot(onehot.astype(bf16), jnp.where(before, 1.0, 0.0).astype(bf16))
    rank = jnp.sum(onehot * earlier, axis=0, keepdims=True)
    return experts.astype(f32) * float(capacity) + rank


def centred(hidden):
    centre = hidden - jnp.mean(hidden, axis=-1, keepdims=True)
    spread = jnp.mean(centre * centre, axis=-1, keepdims=True)
    return centre, lax.rsqrt(spread + EPSILON)


def gelu_pair(x):
    bell = jnp.exp(-0.5 * x * x)
    t = 1.0 / (1.0 + (0.3275911 * 0.7071067811865476) * jnp.abs(x))
    poly = 0.5 * 1.061405429
    for factor in (-1.453152027, 1.421413741, -0.284496736, 0.254829592):
        poly = poly * t + 0.5 * factor
    tail = poly * t * bell
    phi = jnp.where(x >= 0.0, 1.0 - tail, tail)
    return x * phi, phi + x * (bell * 0.3989422804014327)


def forward_kernel(
    groups, cap, tok_hbm, seg_ref, te_ref, gate_ref, g1_ref, wqkv_hbm, wout_hbm, g2_ref, win_hbm,
    wdown_hbm, cot_hbm, h1_out, qkv_out, att_out, inv_out, probs_out, v_out, act_out, gpre_out,
    gdown_out, tok, cot, wqkv, wout, win, wdown, low, qkv, att, inv, probs, bias, h1, place, sent,
    gy_send, gy_got, v_got, act, gpre, gdown, load, store, act_store, gpre_store, down_store,
    gy_ssem, gy_rsem, v_ssem, v_rsem,
):
    dp, me = lax.axis_index("dp"), lax.axis_index("expert")
    rows, width = tok.shape
    slots, hidden = act.shape
    loads = [
        pltpu.make_async_copy(src, dst, load.at[i])
        for i, (src, dst) in enumerate(
            (
                (cot_hbm, cot), (tok_hbm, tok), (wqkv_hbm, wqkv), (wout_hbm, wout),
                (win_hbm, win), (wdown_hbm, wdown),
            )
        )
    ]
    for one in loads:
        one.start()
    greet([(dp, flip(me, k)) for k in range(1, groups)])

    def exchange(source, target, send, receive, k):
        peer = flip(me, k)
        return pltpu.make_async_remote_copy(
            src_ref=source.at[rows_at(peer * cap, cap)],
            dst_ref=target.at[rows_at(me * cap, cap)],
            send_sem=send.at[k],
            recv_sem=receive.at[k],
            device_id=(dp, peer),
            device_id_type=MESH,
        )

    spot = slot_row(te_ref[...], groups, cap)

    @pl.loop(0, slots // GROUP)
    def _(g):
        here = lax.broadcasted_iota(jnp.int32, (GROUP, rows), 0) + g * GROUP
        place[rows_at(g * GROUP, GROUP)] = jnp.where(here.astype(f32) == spot, 1.0, 0.0).astype(
            bf16
        )

    loads[0].wait()
    gate = column_of(gate_ref[...])
    low[...] = (gate * cot[...].astype(f32)).astype(bf16)

    @pl.loop(0, slots // GROUP)
    def _(g):
        at = rows_at(g * GROUP, GROUP)
        gy_send[at] = dot(place[at], low[...]).astype(bf16)

    gy_copies = [exchange(gy_send, gy_got, gy_ssem, gy_rsem, k) for k in range(1, groups)]
    for one in gy_copies:
        one.start()
    mine = rows_at(me * cap, cap)
    gy_got[mine] = gy_send[mine]

    segs = seg_ref[...].astype(f32)
    seg_col = column_of(segs)
    for i in range(rows // BAND):
        first, wide = band(i)
        causal = (lax.broadcasted_iota(jnp.int32, (BAND, wide), 0) + i * BAND) >= (
            lax.broadcasted_iota(jnp.int32, (BAND, wide), 1) + first
        )
        same = seg_col[i * BAND : (i + 1) * BAND] == segs[:, first : first + wide]
        bias[i * BAND : (i + 1) * BAND, 0:wide] = jnp.where(causal & same, 0.0, NEG_LARGE)

    loads[1].wait()

    @pl.loop(0, rows // BAND)
    def _(r):
        at = rows_at(r * BAND, BAND)
        centre, inverse = centred(tok[at].astype(f32))
        low[at] = (centre * inverse * g1_ref[...].reshape(1, width)).astype(bf16)

    loads[2].wait()

    @pl.loop(0, 3 * width // GROUP)
    def _(c):
        at = rows_at(c * GROUP, GROUP)
        qkv[:, at] = dot(low[...], wqkv[:, at]).astype(bf16)

    left = lax.broadcasted_iota(jnp.int32, (1, PAIR), 1) < HEAD_DIM
    none, unit = jnp.zeros((), bf16), jnp.ones((), bf16)

    @pl.loop(0, width // PAIR)
    def _(h):
        at = rows_at(h * PAIR, PAIR)
        k_at = rows_at(width + h * PAIR, PAIR)
        v_at = rows_at(2 * width + h * PAIR, PAIR)
        for i in range(rows // BAND):
            first, wide = band(i)
            mine = slice(i * BAND, (i + 1) * BAND)
            keys = qkv[first : first + wide, k_at]
            values = qkv[first : first + wide, v_at]
            query = qkv[mine, at] * jnp.asarray(HEAD_DIM**-0.5, bf16)
            query = jnp.concatenate(
                [jnp.where(left, query, none), jnp.where(left, none, query)], axis=0
            )
            scores = dot_nt(query, keys).reshape(2, BAND, wide) + bias[mine, 0:wide][None]
            weights = jnp.exp(scores - jnp.max(scores, axis=-1, keepdims=True)).astype(bf16)
            probs[h, 2 * i * BAND : 2 * (i + 1) * BAND, 0:wide] = weights.reshape(2 * BAND, wide)
            one = dot(weights[0], jnp.where(left, values, unit))
            two = dot(weights[1], jnp.where(left, unit, values))
            totals = pltpu.roll(jnp.where(left, two, one), HEAD_DIM, 1)
            scale = 1.0 / totals
            inv[mine, at] = scale
            att[mine, at] = (jnp.where(left, one, two) * scale).astype(bf16)

    stores = [
        pltpu.make_async_copy(src, dst, store.at[i])
        for i, (src, dst) in enumerate(
            (
                (qkv, qkv_out), (probs, probs_out), (att, att_out), (inv, inv_out), (h1, h1_out),
                (v_got, v_out),
            )
        )
    ]
    for i in range(4):
        stores[i].start()
    loads[3].wait()

    @pl.loop(0, rows // BAND)
    def _(r):
        at = rows_at(r * BAND, BAND)
        resid = tok[at].astype(f32) + dot(att[at], wout[...])
        h1[at] = resid
        centre, inverse = centred(resid)
        low[at] = (centre * inverse * g2_ref[...].reshape(1, width)).astype(bf16)

    stores[4].start()

    @pl.loop(0, slots // GROUP)
    def _(g):
        at = rows_at(g * GROUP, GROUP)
        sent[at] = dot(place[at], low[...]).astype(bf16)

    v_copies = [exchange(sent, v_got, v_ssem, v_rsem, k) for k in range(1, groups)]
    for one in v_copies:
        one.start()
    v_got[mine] = sent[mine]
    for i in range(4, 6):
        loads[i].wait()
    for one in gy_copies:
        one.wait_recv()

    @pl.loop(0, hidden // GROUP)
    def _(c):
        at = rows_at(c * GROUP, GROUP)
        gpre[:, at] = dot_nt(gy_got[...], wdown[at]).astype(bf16)

    many = GROUP // cap
    for g in range(slots // GROUP):
        for k in range(g * many, (g + 1) * many):
            if k:
                v_copies[k - 1].wait_recv()
        at = rows_at(flip(me // many, g) * GROUP, GROUP)

        @pl.loop(0, hidden // CHUNK)
        def _(c):
            cols = rows_at(c * CHUNK, CHUNK)
            value, back = gelu_pair(dot(v_got[at], win[:, cols]))
            act[at, cols] = value.astype(bf16)
            gpre[at, cols] = (gpre[at, cols].astype(f32) * back).astype(bf16)

        for source, target, sem in ((act, act_out, act_store), (gpre, gpre_out, gpre_store)):
            stores.append(pltpu.make_async_copy(source.at[at], target.at[at], sem.at[g]))
            stores[-1].start()

    stores[5].start()
    half = hidden // 2
    for part in range(2):

        @pl.loop(part * half // GROUP, (part + 1) * half // GROUP)
        def _(c):
            at = rows_at(c * GROUP, GROUP)
            gdown[at] = dot_tn(act[:, at], gy_got[...]).astype(bf16)

        at = slice(part * half, (part + 1) * half)
        stores.append(pltpu.make_async_copy(gdown.at[at], gdown_out.at[at], down_store.at[part]))
        stores[-1].start()
    for one in gy_copies + v_copies:
        one.wait_send()
    for one in stores:
        one.wait()


def forward(groups, cap, tokens, segs, experts, gates, g1, w_qkv, w_out, g2, w_in, w_down, cot):
    rows, width = tokens.shape
    hidden = w_in.shape[1]
    slots = groups * cap
    pairs = width // PAIR
    wide = 3 * BAND
    shapes = dict(
        h1=((rows, width), f32), qkv=((rows, 3 * width), bf16), att=((rows, width), bf16),
        inv=((rows, width), f32), probs=((pairs, 2 * rows, wide), bf16), v=((slots, width), bf16),
        act=((slots, hidden), bf16), gpre=((slots, hidden), bf16), gdown=((hidden, width), bf16),
    )
    sems = pltpu.SemaphoreType.DMA
    return pl.pallas_call(
        functools.partial(forward_kernel, groups, cap),
        out_shape=[jax.ShapeDtypeStruct(*one) for one in shapes.values()],
        in_specs=[ANY, VMEM, VMEM, VMEM, VMEM, ANY, ANY, VMEM, ANY, ANY, ANY],
        out_specs=[ANY] * len(shapes),
        scratch_shapes=[
            pltpu.VMEM((rows, width), bf16), pltpu.VMEM((rows, width), bf16),
            pltpu.VMEM(w_qkv.shape, bf16), pltpu.VMEM(w_out.shape, bf16),
            pltpu.VMEM(w_in.shape, bf16), pltpu.VMEM(w_down.shape, bf16),
            pltpu.VMEM((rows, width), bf16),
            pltpu.VMEM((rows, 3 * width), bf16), pltpu.VMEM((rows, width), bf16),
            pltpu.VMEM((rows, width), f32),
            pltpu.VMEM((pairs, 2 * rows, wide), bf16), pltpu.VMEM((rows, wide), f32),
            pltpu.VMEM((rows, width), f32), pltpu.VMEM((slots, rows), bf16),
            pltpu.VMEM((slots, width), bf16), pltpu.VMEM((slots, width), bf16),
            pltpu.VMEM((slots, width), bf16), pltpu.VMEM((slots, width), bf16),
            pltpu.VMEM((slots, hidden), bf16), pltpu.VMEM((slots, hidden), bf16),
            pltpu.VMEM((hidden, width), bf16),
            sems((6,)), sems((6,)), sems((slots // GROUP,)), sems((slots // GROUP,)), sems((2,)),
            sems((groups,)), sems((groups,)), sems((groups,)), sems((groups,)),
        ],
        compiler_params=pltpu.CompilerParams(
            collective_id=0, has_side_effects=True, vmem_limit_bytes=60 * MIB
        ),
        cost_estimate=pl.CostEstimate(
            flops=20 * 10**9, bytes_accessed=40 * 10**6, transcendentals=10**7
        ),
        name="forward",
    )(tokens, segs, experts, gates, g1, w_qkv, w_out, g2, w_in, w_down, cot)


def expert_kernel(
    groups, cap, v_hbm, act_hbm, gpre_hbm, win_hbm, wout_hbm, gup_out, gv_out, y_out,
    v, act, gpre, win, wout, turned, gup, gv_send, y_send, gv_got, y_got,
    load, store, gv_ssem, gv_rsem, y_ssem, y_rsem,
):
    dp, me = lax.axis_index("dp"), lax.axis_index("expert")
    slots, width = v.shape
    hidden = act.shape[1]
    loads = [
        pltpu.make_async_copy(src, dst, load.at[i])
        for i, (src, dst) in enumerate(
            (
                (win_hbm, win), (gpre_hbm, gpre), (wout_hbm, wout), (act_hbm, act), (v_hbm, v),
            )
        )
    ]
    for one in loads:
        one.start()
    greet([(dp, flip(me, k)) for k in range(1, groups)])

    def exchange(source, target, send, receive, k):
        peer = flip(me, k)
        return pltpu.make_async_remote_copy(
            src_ref=source.at[rows_at(peer * cap, cap)],
            dst_ref=target.at[rows_at(me * cap, cap)],
            send_sem=send.at[k],
            recv_sem=receive.at[k],
            device_id=(dp, peer),
            device_id_type=MESH,
        )

    mine = rows_at(me * cap, cap)
    many = GROUP // cap
    last = slots // GROUP - 1
    gv_copies = [exchange(gv_send, gv_got, gv_ssem, gv_rsem, k) for k in range(1, groups)]
    y_copies = [exchange(y_send, y_got, y_ssem, y_rsem, k) for k in range(1, groups)]
    for i in range(2):
        loads[i].wait()
    for g in range(last, -1, -1):
        at = rows_at(flip(me // many, g) * GROUP, GROUP)

        @pl.loop(0, width // GROUP)
        def _(n):
            cols = rows_at(n * GROUP, GROUP)
            gv_send[at, cols] = dot_nt(gpre[at], win[cols]).astype(bf16)

        for k in range(g * many, (g + 1) * many):
            if k:
                gv_copies[k - 1].start()
    gv_got[mine] = gv_send[mine]
    for i in range(2, 4):
        loads[i].wait()
    for g in range(last, -1, -1):
        at = rows_at(flip(me // many, g) * GROUP, GROUP)

        @pl.loop(0, width // GROUP)
        def _(n):
            cols = rows_at(n * GROUP, GROUP)
            y_send[at, cols] = dot(act[at], wout[:, cols]).astype(bf16)

        for k in range(g * many, (g + 1) * many):
            if k:
                y_copies[k - 1].start()
    y_got[mine] = y_send[mine]
    loads[4].wait()
    turned[...] = v[...].T

    @pl.loop(0, hidden // GROUP)
    def _(c):
        cols = rows_at(c * GROUP, GROUP)
        gup[:, cols] = dot(turned[...], gpre[:, cols]).astype(bf16)

    outs = [pltpu.make_async_copy(gup, gup_out, store.at[0])]
    outs[0].start()
    for one in gv_copies:
        one.wait_recv()
    outs.append(pltpu.make_async_copy(gv_got, gv_out, store.at[1]))
    outs[1].start()
    for one in y_copies:
        one.wait_recv()
    outs.append(pltpu.make_async_copy(y_got, y_out, store.at[2]))
    outs[2].start()
    for one in gv_copies + y_copies:
        one.wait_send()
    for one in outs:
        one.wait()


def experts_back(groups, cap, v, act, gpre, w_in, w_out):
    slots, width = v.shape
    hidden = act.shape[1]
    sems = pltpu.SemaphoreType.DMA
    return pl.pallas_call(
        functools.partial(expert_kernel, groups, cap),
        out_shape=[
            jax.ShapeDtypeStruct((width, hidden), bf16),
            jax.ShapeDtypeStruct((slots, width), bf16),
            jax.ShapeDtypeStruct((slots, width), bf16),
        ],
        in_specs=[ANY] * 5,
        out_specs=[ANY] * 3,
        scratch_shapes=[
            pltpu.VMEM((slots, width), bf16),
            pltpu.VMEM((slots, hidden), bf16), pltpu.VMEM((slots, hidden), bf16),
            pltpu.VMEM((width, hidden), bf16), pltpu.VMEM((hidden, width), bf16),
            pltpu.VMEM((width, slots), bf16),
            pltpu.VMEM((width, hidden), bf16),
            pltpu.VMEM((slots, width), bf16), pltpu.VMEM((slots, width), bf16),
            pltpu.VMEM((slots, width), bf16), pltpu.VMEM((slots, width), bf16),
            sems((5,)), sems((3,)), sems((groups,)), sems((groups,)), sems((groups,)),
            sems((groups,)),
        ],
        compiler_params=pltpu.CompilerParams(
            collective_id=1, has_side_effects=True, vmem_limit_bytes=60 * MIB
        ),
        cost_estimate=pl.CostEstimate(flops=10**6, bytes_accessed=10**5, transcendentals=0),
        name="experts_back",
    )(v, act, gpre, w_in, w_out)


def dense_kernel(
    groups, cap, gvr_hbm, yr_hbm, te_ref, gate_ref, h1_hbm, cot_hbm, tok_hbm, g1_ref, g2_ref,
    att_hbm, inv_hbm, probs_hbm, qkv_hbm, wqkv_hbm, wout_hbm, block_out, gtok_out, dense_out, gains_out,
    gvr, yr, h1, cot, tok, att, inv, probs, qkv, wqkv, wout, place, gh1, low, gatt, inner_sum, gqkv,
    turned, gk, gvv, dense, outv, load, store,
):
    rows, width = tok.shape
    slots = gvr.shape[0]
    loads = [
        pltpu.make_async_copy(src, dst, load.at[i])
        for i, (src, dst) in enumerate(
            (
                (gvr_hbm, gvr), (h1_hbm, h1), (cot_hbm, cot), (yr_hbm, yr), (att_hbm, att),
                (wout_hbm, wout), (qkv_hbm, qkv), (probs_hbm, probs), (tok_hbm, tok),
                (wqkv_hbm, wqkv), (inv_hbm, inv),
            )
        )
    ]
    for one in loads:
        one.start()
    spot = column_of(slot_row(te_ref[...], groups, cap))
    for r in range(rows // BAND):
        at = slice(r * BAND, (r + 1) * BAND)
        here = lax.broadcasted_iota(jnp.int32, (BAND, slots), 1).astype(f32)
        place[at] = jnp.where(here == spot[at], 1.0, 0.0).astype(bf16)
    gate = column_of(gate_ref[...])
    for i in range(4):
        loads[i].wait()
    gains_out[...] = jnp.zeros_like(gains_out)
    for r in range(rows // BAND):
        at = slice(r * BAND, (r + 1) * BAND)
        back = dot(place[at], gvr[...])
        resid = h1[at]
        centre, inverse = centred(resid)
        unit = centre * inverse
        gains_out[1:2] += jnp.sum(back * unit, axis=0, keepdims=True)
        slant = back * g2_ref[...].reshape(1, width)
        inner = slant - jnp.mean(slant, axis=-1, keepdims=True)
        inner = inner - unit * jnp.mean(slant * unit, axis=-1, keepdims=True)
        grad = cot[at].astype(f32) + inverse * inner
        gh1[at] = grad
        low[at] = grad.astype(bf16)
        outv[at] = (resid + gate[at] * dot(place[at], yr[...])).astype(bf16)
    out_one = pltpu.make_async_copy(outv, block_out, store.at[0])
    out_one.start()
    for i in (4, 5, 10):
        loads[i].wait()

    @pl.loop(0, width // GROUP)
    def _(n):
        cols = rows_at(n * GROUP, GROUP)
        grad = dot_nt(low[...], wout[cols]) * inv[:, cols]
        gatt[:, cols] = grad.astype(bf16)
        inner_sum[:, cols] = grad * att[:, cols].astype(f32) * HEAD_DIM**-0.5

    turned[...] = att[...].T

    @pl.loop(0, width // GROUP)
    def _(n):
        cols = rows_at(n * GROUP, GROUP)
        dense[0:width, rows_at(3 * width + n * GROUP, GROUP)] = dot(
            turned[...], low[:, cols]
        ).astype(bf16)

    loads[6].wait()
    loads[7].wait()
    left = lax.broadcasted_iota(jnp.int32, (1, PAIR), 1) < HEAD_DIM
    none = jnp.zeros((), bf16)

    def halves(block):
        return jnp.concatenate([jnp.where(left, block, none), jnp.where(left, none, block)], axis=0)

    @pl.loop(0, width // PAIR)
    def _(h):
        at = rows_at(h * PAIR, PAIR)
        k_at = rows_at(width + h * PAIR, PAIR)
        v_at = rows_at(2 * width + h * PAIR, PAIR)
        gk[...] = jnp.zeros_like(gk)
        gvv[...] = jnp.zeros_like(gvv)
        for i in range(rows // BAND):
            first, wide = band(i)
            mine, seen = slice(i * BAND, (i + 1) * BAND), slice(first, first + wide)
            keys = qkv[seen, k_at]
            values = qkv[seen, v_at] * jnp.asarray(HEAD_DIM**-0.5, bf16)
            query, grad = halves(qkv[mine, at]), halves(gatt[mine, at])
            share = probs[h, 2 * i * BAND : 2 * (i + 1) * BAND, 0:wide]
            inner = inner_sum[mine, at]
            middle = jnp.concatenate(
                [
                    jnp.sum(jnp.where(left, inner, 0.0), axis=-1, keepdims=True),
                    jnp.sum(jnp.where(left, 0.0, inner), axis=-1, keepdims=True),
                ],
                axis=0,
            )
            graw = (share.astype(f32) * (dot_nt(grad, values) - middle)).astype(bf16)
            gquery = dot(graw, keys)
            gqkv[mine, at] = jnp.where(left, gquery[0:BAND], gquery[BAND:]).astype(bf16)
            gk[seen] += dot_tn(graw, query)
            gvv[seen] += dot_tn(share, grad)
        gqkv[:, k_at] = gk[...].astype(bf16)
        gqkv[:, v_at] = gvv[...].astype(bf16)

    loads[8].wait()
    loads[9].wait()
    for r in range(rows // BAND):
        at = slice(r * BAND, (r + 1) * BAND)
        centre, inverse = centred(tok[at].astype(f32))
        low[at] = (centre * inverse * g1_ref[...].reshape(1, width)).astype(bf16)
    turned[...] = low[...].T

    @pl.loop(0, 3 * width // GROUP)
    def _(n):
        cols = rows_at(n * GROUP, GROUP)
        dense[0:width, cols] = dot(turned[...], gqkv[:, cols]).astype(bf16)

    out_two = pltpu.make_async_copy(dense, dense_out, store.at[1])
    out_two.start()
    out_one.wait()
    for r in range(rows // BAND):
        at = slice(r * BAND, (r + 1) * BAND)
        back = dot_nt(gqkv[at], wqkv[...])
        centre, inverse = centred(tok[at].astype(f32))
        unit = centre * inverse
        gains_out[0:1] += jnp.sum(back * unit, axis=0, keepdims=True)
        slant = back * g1_ref[...].reshape(1, width)
        inner = slant - jnp.mean(slant, axis=-1, keepdims=True)
        inner = inner - unit * jnp.mean(slant * unit, axis=-1, keepdims=True)
        outv[at] = (gh1[at] + inverse * inner).astype(bf16)
    out_three = pltpu.make_async_copy(outv, gtok_out, store.at[0])
    out_three.start()
    out_two.wait()
    out_three.wait()


def dense_back(
    groups, cap, per, gvr, yr, experts, gates, h1, cot, tok, g1, g2, att, inv,
    probs, qkv, w_qkv, w_out,
):
    rows, width = tok.shape
    slots = gvr.shape[0]
    sems = pltpu.SemaphoreType.DMA
    return pl.pallas_call(
        functools.partial(dense_kernel, groups, cap),
        out_shape=[
            jax.ShapeDtypeStruct((rows, width), bf16),
            jax.ShapeDtypeStruct((rows, width), bf16),
            jax.ShapeDtypeStruct((groups * per, 4 * width), bf16),
            jax.ShapeDtypeStruct((8, width), f32),
        ],
        in_specs=[ANY, ANY, VMEM, VMEM, ANY, ANY, ANY, VMEM, VMEM] + [ANY] * 6,
        out_specs=[ANY, ANY, ANY, VMEM],
        scratch_shapes=[
            pltpu.VMEM((slots, width), bf16), pltpu.VMEM((slots, width), bf16),
            pltpu.VMEM((rows, width), f32), pltpu.VMEM((rows, width), bf16),
            pltpu.VMEM((rows, width), bf16), pltpu.VMEM((rows, width), bf16),
            pltpu.VMEM((rows, width), f32),
            pltpu.VMEM(probs.shape, bf16), pltpu.VMEM(qkv.shape, bf16),
            pltpu.VMEM(w_qkv.shape, bf16), pltpu.VMEM(w_out.shape, bf16),
            pltpu.VMEM((rows, slots), bf16), pltpu.VMEM((rows, width), f32),
            pltpu.VMEM((rows, width), bf16), pltpu.VMEM((rows, width), bf16),
            pltpu.VMEM((rows, width), f32),
            pltpu.VMEM((rows, 3 * width), bf16), pltpu.VMEM((width, rows), bf16),
            pltpu.VMEM((rows, PAIR), f32), pltpu.VMEM((rows, PAIR), f32),
            pltpu.VMEM((groups * per, 4 * width), bf16), pltpu.VMEM((rows, width), bf16),
            sems((11,)), sems((2,)),
        ],
        compiler_params=pltpu.CompilerParams(vmem_limit_bytes=60 * MIB),
        cost_estimate=pl.CostEstimate(flops=10**6, bytes_accessed=10**5, transcendentals=0),
        name="dense_back",
    )(gvr, yr, experts, gates, h1, cot, tok, g1, g2, att, inv, probs, qkv, w_qkv, w_out)


def sum_kernel(
    groups, copies, dense_hbm, gains_ref, out_ref, total_ref,
    own, other, part, got, ring, ring_got, final, gains_pair, gains_chip, gains_part, gains_ring,
    load, s_pair, r_pair, s_chip, r_chip, s_ring, r_ring, s_out, r_out, s_gain, r_gain,
):
    dp, me = lax.axis_index("dp"), lax.axis_index("expert")
    half = groups // 2
    per, wide = got.shape[1:]
    width = wide // 4
    chip, core = me // 2, me % 2
    there = flip(me, 1)
    chips = [flip(chip, k) for k in range(half)]
    rounds = [lax.rem(dp + k, copies) for k in range(copies)]
    keep = pltpu.make_async_copy(
        dense_hbm.at[rows_at(core * (half * per), half * per)], own, load.at[0]
    )
    keep.start()
    greet(
        [(dp, flip(me, k)) for k in range(1, groups)] + [(one, me) for one in rounds[1:]]
    )

    def send(source, target, ssem, rsem, device):
        return pltpu.make_async_remote_copy(
            src_ref=source, dst_ref=target, send_sem=ssem, recv_sem=rsem, device_id=device,
            device_id_type=MESH,
        )

    started = []

    def go(copy):
        copy.start()
        started.append(copy)
        return copy

    pair = []
    for k in range(half - 1, -1, -1):
        block = chips[k]
        pair.append(
            go(
                send(
                    dense_hbm.at[rows_at(((1 - core) * half + block) * per, per)],
                    other.at[rows_at(block * per, per)],
                    s_pair.at[k], r_pair.at[k], (dp, there),
                )
            )
        )
    gain_pair = go(send(gains_ref, gains_pair, s_gain.at[0], r_gain.at[0], (dp, there)))
    keep.wait()
    far = {}
    for i, k in enumerate(range(half - 1, -1, -1)):
        at = rows_at(chips[k] * per, per)
        pair[i].wait_recv()
        part[at] = (own[at].astype(f32) + other[at].astype(f32)).astype(bf16)
        if k:
            far[k] = go(
                send(part.at[at], got.at[k], s_chip.at[k], r_chip.at[k], (dp, chips[k] * 2 + core))
            )
    gain_pair.wait_recv()
    gains_part[0] = gains_ref[...] + gains_pair[...]
    gain_far = [
        go(
            send(
                gains_part.at[0], gains_chip.at[k], s_gain.at[k], r_gain.at[k],
                (dp, chips[k] * 2 + core),
            )
        )
        for k in range(1, half)
    ]
    total = part[rows_at(chip * per, per)].astype(f32)
    for k in range(1, half):
        far[k].wait_recv()
        total = total + got[k].astype(f32)
    share = 3 * width // copies
    thin = width // copies
    for d in range(copies):
        ring[d] = jnp.concatenate(
            [
                total[:, d * share : (d + 1) * share],
                total[:, 3 * width + d * thin : 3 * width + (d + 1) * thin],
            ],
            axis=1,
        ).astype(bf16)
    around = [
        go(send(ring.at[rounds[k]], ring_got.at[k], s_ring.at[k], r_ring.at[k], (rounds[k], me)))
        for k in range(1, copies)
    ]
    gains = gains_part[0]
    for k in range(1, half):
        gain_far[k - 1].wait_recv()
        gains = gains + gains_chip[k]
    gains_part[1] = gains
    gain_around = [
        go(
            send(
                gains_part.at[1], gains_ring.at[k], s_gain.at[half + k], r_gain.at[half + k],
                (rounds[k], me),
            )
        )
        for k in range(1, copies)
    ]
    summed = ring[dp].astype(f32)
    for k in range(1, copies):
        around[k - 1].wait_recv()
        summed = summed + ring_got[k].astype(f32)
    place = rows_at((core * half + chip) * per, per)
    final[...] = summed.astype(bf16)
    out_ref[place] = final[...]
    spread = [
        go(send(final, out_ref.at[place], s_out.at[k], r_out.at[k], (dp, flip(me, k))))
        for k in range(groups - 1, 0, -1)
    ]
    for k in range(1, copies):
        gain_around[k - 1].wait_recv()
        gains = gains + gains_ring[k]
    total_ref[...] = gains
    for one in spread:
        one.wait_recv()
    for one in started:
        one.wait_send()


def dense_sum(groups, copies, dense, gains):
    wide = dense.shape[1]
    per = dense.shape[0] // groups
    half = groups // 2
    thin = wide // copies
    sems = pltpu.SemaphoreType.DMA
    tile = gains.shape
    return pl.pallas_call(
        functools.partial(sum_kernel, groups, copies),
        out_shape=[
            jax.ShapeDtypeStruct((groups * per, thin), bf16),
            jax.ShapeDtypeStruct(tile, f32),
        ],
        in_specs=[ANY, VMEM],
        out_specs=[VMEM, VMEM],
        scratch_shapes=[
            pltpu.VMEM((half * per, wide), bf16), pltpu.VMEM((half * per, wide), bf16),
            pltpu.VMEM((half * per, wide), bf16), pltpu.VMEM((half, per, wide), bf16),
            pltpu.VMEM((copies, per, thin), bf16), pltpu.VMEM((copies, per, thin), bf16),
            pltpu.VMEM((per, thin), bf16),
            pltpu.VMEM(tile, f32), pltpu.VMEM((half, *tile), f32), pltpu.VMEM((2, *tile), f32),
            pltpu.VMEM((copies, *tile), f32),
            sems((1,)), sems((half,)), sems((half,)), sems((half,)), sems((half,)),
            sems((copies,)), sems((copies,)), sems((groups,)), sems((groups,)),
            sems((half + copies,)), sems((half + copies,)),
        ],
        compiler_params=pltpu.CompilerParams(
            collective_id=2, has_side_effects=True, vmem_limit_bytes=40 * MIB
        ),
        cost_estimate=pl.CostEstimate(flops=10**6, bytes_accessed=10**5, transcendentals=0),
        name="dense_sum",
    )(dense, gains)


def shards(
    tokens, segment_ids, token_expert, gates, ln1_gain, w_qkv, w_out, ln2_gain, expert_in,
    expert_out, cotangent,
):
    rows, width = tokens.shape
    groups, copies = lax.axis_size("expert"), lax.axis_size("dp")
    cap = 2 * rows // groups
    per = -(-width // (16 * groups)) * 16
    w_in, w_down = expert_in[0], expert_out[0]
    experts, gate_row = token_expert.reshape(1, rows), gates.reshape(1, rows)
    h1, qkv, att, inv, probs, v, act, gpre, gdown = forward(
        groups, cap, tokens, segment_ids, experts, gate_row, ln1_gain, w_qkv, w_out, ln2_gain, w_in,
        w_down, cotangent,
    )
    down_share = lax.psum_scatter(gdown[None], "dp", scatter_dimension=1, tiled=True)
    gup, gv_slots, y_slots = experts_back(groups, cap, v, act, gpre, w_in, w_down)
    up_share = lax.psum_scatter(gup[None], "dp", scatter_dimension=1, tiled=True)
    block_out, grad_tokens, dense, gains = dense_back(
        groups, cap, per, gv_slots, y_slots, experts, gate_row, h1, cotangent, tokens, ln1_gain,
        ln2_gain, att,
        inv, probs, qkv, w_qkv, w_out,
    )
    dense, down_share = lax.optimization_barrier((dense, down_share))
    whole, gains = dense_sum(groups, copies, dense, gains)
    whole = whole[:width].astype(f32)
    share = width // copies
    gains = lax.dynamic_slice_in_dim(gains, lax.axis_index("dp") * share, share, 1)
    return (
        block_out,
        grad_tokens,
        gains[0],
        whole[:, : 3 * share],
        whole[:, 3 * share :],
        gains[1],
        up_share.astype(f32),
        down_share.astype(f32),
    )


def solution(mesh):
    tokens, experts = P(("dp", "expert"), None), P("expert", None, None)
    return jax.shard_map(
        shards,
        mesh=mesh,
        in_specs=(
            tokens, tokens, tokens, P(("dp", "expert")), P(), P(), P(), P(), experts, experts,
            tokens,
        ),
        out_specs=(
            tokens, tokens, P("dp"), P(None, "dp"), P(None, "dp"), P("dp"),
            P("expert", "dp", None), P("expert", "dp", None),
        ),
        check_vma=False,
    )
```

```python
import functools

import jax
import jax.numpy as jnp
from jax import lax
from jax.experimental import pallas as pl
from jax.experimental.pallas import tpu as pltpu
from jax.sharding import PartitionSpec as P

HEAD_DIM = 64
EPSILON = 1e-05
NEG_LARGE = -1e30
BAND = 128
PAIR = 2 * HEAD_DIM
GROUP = 256
CHUNK = 512
MIB = 2**20
MESH = pl.DeviceIdType.MESH
ANY = pl.BlockSpec(memory_space=pl.ANY)
VMEM = pl.BlockSpec(memory_space=pltpu.VMEM)
f32, bf16 = jnp.float32, jnp.bfloat16


def dot(a, b):
    return jnp.dot(a, b, preferred_element_type=f32)


def dot_nt(a, b):
    return lax.dot_general(a, b, (((1,), (1,)), ((), ())), preferred_element_type=f32)


def dot_tn(a, b):
    return lax.dot_general(a, b, (((0,), (0,)), ((), ())), preferred_element_type=f32)


def flip(index, bits):
    place = 1
    while bits:
        if bits % 2:
            index = index + place * (1 - 2 * ((index // place) % 2))
        bits, place = bits // 2, place * 2
    return index


def add(a, b):
    return (a.astype(f32) + b.astype(f32)).astype(bf16)


def rows_at(start, size):
    return pl.ds(pl.multiple_of(start, size), size)


def greet(peers):
    barrier = pltpu.get_barrier_semaphore()
    for peer in peers:
        pl.semaphore_signal(barrier, inc=1, device_id=peer, device_id_type=MESH)
    pl.semaphore_wait(barrier, len(peers))


def sides(dp):
    side = dp // 2
    return flip(dp, 1), 3 - dp, [3 * (1 - side), 2 - side, 3 * side, 1 + side]


class Relay:
    def __init__(self, dp, me, moves, ssem, rsem):
        self.outer = (dp == 0) | (dp == 3)
        self.inner = jnp.logical_not(self.outer)
        beside, across, _ = sides(dp)
        self.moves = []
        for i, (kind, source, target) in enumerate(moves):
            plane = across if kind == "across" else beside
            copy = pltpu.make_async_remote_copy(
                src_ref=source, dst_ref=target, send_sem=ssem.at[i], recv_sem=rsem.at[i],
                device_id=(plane, me), device_id_type=MESH,
            )
            sender = self.outer if kind == "inward" else self.inner
            receiver = self.outer if kind == "outward" else self.inner
            self.moves.append((copy, sender, receiver))

    def start(self, *which):
        for i in which:
            copy, sender, _ = self.moves[i]
            pl.when(sender)(copy.start)

    def sent(self, i):
        pl.when(self.moves[i][1])(self.moves[i][0].wait_send)

    def landed(self, i):
        pl.when(self.moves[i][2])(self.moves[i][0].wait_recv)

    def merged(self, first, second, total, spare, sem):
        @pl.when(self.inner)
        def _():
            loads = [
                pltpu.make_async_copy(first, total, sem.at[0]),
                pltpu.make_async_copy(second, spare, sem.at[1]),
            ]
            for one in loads:
                one.start()
            for one in loads:
                one.wait()
            lines = total.shape[0] // 12

            @pl.loop(0, 12)
            def _(r):
                at = rows_at(r * lines, lines)
                total[at] = add(total[at], spare[at])


def band(index):
    first = max(0, index - 2) * BAND
    return first, (index + 1) * BAND - first


def column_of(row):
    size = row.shape[1]
    eye = lax.broadcasted_iota(jnp.int32, (size, size), 0) == lax.broadcasted_iota(
        jnp.int32, (size, size), 1
    )
    return jnp.sum(jnp.where(eye, row, 0.0), axis=1, keepdims=True)


def slot_row(experts, num_experts, capacity):
    rows = experts.shape[1]
    lines = max(16, num_experts)
    onehot = lax.broadcasted_iota(jnp.int32, (lines, rows), 0) == experts
    onehot = jnp.where(onehot, 1.0, 0.0)
    before = lax.broadcasted_iota(jnp.int32, (rows, rows), 0) < lax.broadcasted_iota(
        jnp.int32, (rows, rows), 1
    )
    earlier = dot(onehot.astype(bf16), jnp.where(before, 1.0, 0.0).astype(bf16))
    rank = jnp.sum(onehot * earlier, axis=0, keepdims=True)
    return experts.astype(f32) * float(capacity) + rank


def centred(hidden):
    centre = hidden - jnp.mean(hidden, axis=-1, keepdims=True)
    spread = jnp.mean(centre * centre, axis=-1, keepdims=True)
    return centre, lax.rsqrt(spread + EPSILON)


def gelu_pair(x):
    bell = jnp.exp(-0.5 * x * x)
    t = 1.0 / (1.0 + (0.3275911 * 0.7071067811865476) * jnp.abs(x))
    poly = 0.5 * 1.061405429
    for factor in (-1.453152027, 1.421413741, -0.284496736, 0.254829592):
        poly = poly * t + 0.5 * factor
    tail = poly * t * bell
    phi = jnp.where(x >= 0.0, 1.0 - tail, tail)
    return x * phi, phi + x * (bell * 0.3989422804014327)


def gelu(x):
    return gelu_pair(x)[0]


def forward_kernel(groups, cap, ends, *refs):
    (
        tok_hbm, seg_ref, te_ref, gate_ref, g1_ref, wqkv_hbm, wout_hbm, g2_ref, win_hbm, wdown_hbm,
        cot_hbm, h1_out, qkv_out, att_out, inv_out, probs_out, act_out, gpre_out,
    ) = refs[:18]
    count = 4 if ends else 1
    ups, downs = refs[18 : 18 + count], refs[18 + count : 18 + 2 * count]
    up_land = refs[18 + 2 * count : 18 + 2 * count + ends]
    (
        tok, cot, win, wdown, low, h1, place, sent, gy_send, gy_got, v_got, gy_low, spot_own, gy_line,
        v_line, spot_far, gy_fsend, far_send, gy_far, v_far, act,
        gpre, load, store, act_store, gpre_store, gy_ssem, gy_rsem, v_ssem, v_rsem, gy_fssem,
        gy_frsem, v_fssem, v_frsem, line_ssem, line_rsem, rel_s, rel_r,
    ) = refs[18 + 2 * count + ends :]
    dp, me = lax.axis_index("dp"), lax.axis_index("expert")
    rows, width = tok.shape
    slots, hidden = act.shape
    pairs = width // PAIR
    outer = (dp == 0) | (dp == 3)
    inner = jnp.logical_not(outer)
    first_loads = [
        pltpu.make_async_copy(src, dst, load.at[i])
        for i, (src, dst) in enumerate(
            ((cot_hbm, cot), (tok_hbm, tok), (win_hbm, win), (wdown_hbm, wdown))
        )
    ]
    first_loads[0].start()
    first_loads[1].start()
    beside = [(flip(dp, 1), me)] if ends else []
    greet([(dp, flip(me, k)) for k in range(1, groups)] + beside)

    def exchange(source, target, send, receive, k):
        peer = flip(me, k)
        return pltpu.make_async_remote_copy(
            src_ref=source.at[rows_at(peer * cap, cap)],
            dst_ref=target.at[rows_at(me * cap, cap)],
            send_sem=send.at[k],
            recv_sem=receive.at[k],
            device_id=(dp, peer),
            device_id_type=MESH,
        )

    gy_copies = [exchange(gy_send, gy_got, gy_ssem, gy_rsem, k) for k in range(1, groups)]
    v_copies = [exchange(sent, v_got, v_ssem, v_rsem, k) for k in range(1, groups)]
    far_groups = groups if ends else 0
    gy_fars = [exchange(gy_fsend, gy_far, gy_fssem, gy_frsem, k) for k in range(1, far_groups)]
    v_fars = [exchange(far_send, v_far, v_fssem, v_frsem, k) for k in range(1, far_groups)]
    lines = ends and [
        pltpu.make_async_remote_copy(
            src_ref=source, dst_ref=target, send_sem=line_ssem.at[i], recv_sem=line_rsem.at[i],
            device_id=(flip(dp, 1), me), device_id_type=MESH,
        )
        for i, (source, target) in enumerate(
            ((spot_own, spot_far), (gy_low, gy_line), (low, v_line))
        )
    ]

    def when(condition, action):
        if ends:
            pl.when(condition)(action)

    def placed(line, target):
        @pl.loop(0, slots // GROUP)
        def _(g):
            at = rows_at(g * GROUP, GROUP)
            here = lax.broadcasted_iota(jnp.int32, (GROUP, rows), 0) + g * GROUP
            there = jnp.where(here.astype(f32) == spot_far[0:1], 1.0, 0.0).astype(bf16)
            target[at] = dot(there, line[...]).astype(bf16)

    def far_gy():
        lines[0].wait_recv()
        lines[1].wait_recv()
        placed(gy_line, gy_fsend)
        for one in gy_fars:
            one.start()
        gy_far[mine] = gy_fsend[mine]

    def far_v():
        lines[2].wait_recv()
        placed(v_line, far_send)
        for one in v_fars:
            one.start()
        v_far[mine] = far_send[mine]

    mine = rows_at(me * cap, cap)

    def attention(wqkv, wout, qkv, att, inv, probs, bias):
        loads = [
            pltpu.make_async_copy(wqkv_hbm, wqkv, load.at[4]),
            pltpu.make_async_copy(wout_hbm, wout, load.at[5]),
        ]
        for one in loads + first_loads[2:]:
            one.start()
        spot = slot_row(te_ref[...], groups, cap)

        @pl.loop(0, slots // GROUP)
        def _(g):
            here = lax.broadcasted_iota(jnp.int32, (GROUP, rows), 0) + g * GROUP
            there = jnp.where(here.astype(f32) == spot, 1.0, 0.0)
            place[rows_at(g * GROUP, GROUP)] = there.astype(bf16)

        first_loads[0].wait()
        gate = column_of(gate_ref[...])
        gy_low[...] = (gate * cot[...].astype(f32)).astype(bf16)
        if ends:
            spot_own[...] = jnp.broadcast_to(spot, spot_own.shape)

            @pl.when(outer)
            def _():
                lines[0].start()
                lines[1].start()

        @pl.loop(0, slots // GROUP)
        def _(g):
            at = rows_at(g * GROUP, GROUP)
            gy_send[at] = dot(place[at], gy_low[...]).astype(bf16)

        for one in gy_copies:
            one.start()
        gy_got[mine] = gy_send[mine]
        segs = seg_ref[...].astype(f32)
        seg_col = column_of(segs)
        for i in range(rows // BAND):
            first, wide = band(i)
            causal = (lax.broadcasted_iota(jnp.int32, (BAND, wide), 0) + i * BAND) >= (
                lax.broadcasted_iota(jnp.int32, (BAND, wide), 1) + first
            )
            same = seg_col[i * BAND : (i + 1) * BAND] == segs[:, first : first + wide]
            bias[i * BAND : (i + 1) * BAND, 0:wide] = jnp.where(causal & same, 0.0, NEG_LARGE)

        first_loads[1].wait()

        @pl.loop(0, rows // BAND)
        def _(r):
            at = rows_at(r * BAND, BAND)
            centre, inverse = centred(tok[at].astype(f32))
            low[at] = (centre * inverse * g1_ref[...].reshape(1, width)).astype(bf16)

        loads[0].wait()

        @pl.loop(0, 3 * width // GROUP)
        def _(c):
            at = rows_at(c * GROUP, GROUP)
            qkv[:, at] = dot(low[...], wqkv[:, at]).astype(bf16)

        left = lax.broadcasted_iota(jnp.int32, (1, PAIR), 1) < HEAD_DIM
        none, unit = jnp.zeros((), bf16), jnp.ones((), bf16)

        def attend(h):
            at = rows_at(h * PAIR, PAIR)
            k_at = rows_at(width + h * PAIR, PAIR)
            v_at = rows_at(2 * width + h * PAIR, PAIR)
            for i in range(rows // BAND):
                first, wide = band(i)
                here = slice(i * BAND, (i + 1) * BAND)
                keys = qkv[first : first + wide, k_at]
                values = qkv[first : first + wide, v_at]
                query = qkv[here, at] * jnp.asarray(HEAD_DIM**-0.5, bf16)
                query = jnp.concatenate(
                    [jnp.where(left, query, none), jnp.where(left, none, query)], axis=0
                )
                scores = dot_nt(query, keys).reshape(2, BAND, wide) + bias[here, 0:wide][None]
                weights = jnp.exp(scores - jnp.max(scores, axis=-1, keepdims=True)).astype(bf16)
                probs[h, 2 * i * BAND : 2 * (i + 1) * BAND, 0:wide] = weights.reshape(
                    2 * BAND, wide
                )
                one = dot(weights[0], jnp.where(left, values, unit))
                two = dot(weights[1], jnp.where(left, unit, values))
                scale = 1.0 / pltpu.roll(jnp.where(left, two, one), HEAD_DIM, 1)
                inv[here, at] = scale
                att[here, at] = (jnp.where(left, one, two) * scale).astype(bf16)

        pl.loop(0, pairs)(attend)
        when(inner, far_gy)
        stores = [
            pltpu.make_async_copy(src, dst, store.at[i])
            for i, (src, dst) in enumerate(
                ((qkv, qkv_out), (probs, probs_out), (att, att_out), (inv, inv_out))
            )
        ]
        for one in stores:
            one.start()
        loads[1].wait()

        @pl.loop(0, rows // BAND)
        def _(r):
            at = rows_at(r * BAND, BAND)
            resid = tok[at].astype(f32) + dot(att[at], wout[...])
            h1[at] = resid
            centre, inverse = centred(resid)
            low[at] = (centre * inverse * g2_ref[...].reshape(1, width)).astype(bf16)

        when(outer, lambda: lines[2].start())

        @pl.loop(0, slots // GROUP)
        def _(g):
            at = rows_at(g * GROUP, GROUP)
            sent[at] = dot(place[at], low[...]).astype(bf16)

        for one in v_copies:
            one.start()
        v_got[mine] = sent[mine]
        for one in stores:
            one.wait()

    pl.run_scoped(
        attention,
        pltpu.VMEM((width, 3 * width), bf16), pltpu.VMEM((width, width), bf16),
        pltpu.VMEM((rows, 3 * width), bf16), pltpu.VMEM((rows, width), bf16),
        pltpu.VMEM((rows, width), f32), pltpu.VMEM((pairs, 2 * rows, 3 * BAND), bf16),
        pltpu.VMEM((rows, 3 * BAND), f32),
    )

    def experts(act_far, gdown, gup, turned):
        stores = [pltpu.make_async_copy(h1, h1_out, store.at[4])]
        stores[0].start()
        for one in first_loads[2:]:
            one.wait()
        for one in gy_copies:
            one.wait_recv()

        @pl.loop(0, hidden // GROUP)
        def _(c):
            at = rows_at(c * GROUP, GROUP)
            gpre[:, at] = dot_nt(gy_got[...], wdown[at]).astype(bf16)

        many = GROUP // cap
        for g in range(slots // GROUP):
            for k in range(g * many, (g + 1) * many):
                if k:
                    v_copies[k - 1].wait_recv()
            at = rows_at(flip(me // many, g) * GROUP, GROUP)

            @pl.loop(0, hidden // CHUNK)
            def _(c):
                cols = rows_at(c * CHUNK, CHUNK)
                value, back = gelu_pair(dot(v_got[at], win[:, cols]))
                act[at, cols] = value.astype(bf16)
                gpre[at, cols] = (gpre[at, cols].astype(f32) * back).astype(bf16)

            for source, target, sem in ((act, act_out, act_store), (gpre, gpre_out, gpre_store)):
                stores.append(pltpu.make_async_copy(source.at[at], target.at[at], sem.at[g]))
                stores[-1].start()
            if g == 1:
                when(inner, far_v)

        turned[...] = v_got[...].T

        @pl.loop(0, hidden // GROUP)
        def _(c):
            cols = rows_at(c * GROUP, GROUP)
            gup[:, cols] = dot(turned[...], gpre[:, cols]).astype(bf16)

        shares = sides(dp)[2] if ends else [0]
        size, share = width // count, hidden // count
        for i, (one, part) in enumerate(zip(shares, ups)):
            source = gup.at[rows_at(one * size, size)]
            stores.append(pltpu.make_async_copy(source, part, store.at[5 + i]))
            stores[-1].start()
        if ends:
            relay = Relay(
                dp, me, [("inward", gup.at[rows_at(shares[0] * size, size)], up_land[0])],
                rel_s, rel_r,
            )
            relay.start(0)

        def down(kept, shared):
            for i in kept:

                @pl.loop(0, share // GROUP)
                def _(c):
                    cols = pl.ds(pl.multiple_of(shares[i] * share + c * GROUP, GROUP), GROUP)
                    at = pl.ds(pl.multiple_of(i * share + c * GROUP, GROUP), GROUP)
                    total = dot_tn(act[:, cols], gy_got[...])
                    if shared:
                        total = total + dot_tn(act_far[:, at], gy_far[...])
                    gdown[at] = total.astype(bf16)

            for i in kept:
                at = slice(i * share, (i + 1) * share)
                pltpu.make_async_copy(gdown.at[at], downs[i], store.at[9 + i]).start()

        def taken(kept):
            for i in kept:
                at = slice(i * share, (i + 1) * share)
                pltpu.make_async_copy(gdown.at[at], downs[i], store.at[9 + i]).wait()

        def inside():
            for g in range(slots // GROUP):
                for k in range(g * many, (g + 1) * many):
                    if k:
                        v_fars[k - 1].wait_recv()
                at = rows_at(flip(me // many, g) * GROUP, GROUP)
                for i in range(2):

                    @pl.loop(0, share // CHUNK + share % CHUNK // GROUP)
                    def _(c):
                        wide = share // (share // CHUNK + share % CHUNK // GROUP)
                        cols = pl.ds(pl.multiple_of(shares[i] * share + c * wide, 128), wide)
                        kept = pl.ds(pl.multiple_of(i * share + c * wide, 128), wide)
                        act_far[at, kept] = gelu(dot(v_far[at], win[:, cols])).astype(bf16)

            for one in gy_fars:
                one.wait_recv()
            down([0, 1], True)
            for one in gy_fars + v_fars:
                one.wait_send()
            taken([0, 1])

        down([2, 3] if ends else [0], False)
        if ends:
            pl.when(inner)(inside)

            @pl.when(outer)
            def _():
                for one in lines:
                    one.wait_send()

        taken([2, 3] if ends else [0])
        for one in gy_copies + v_copies:
            one.wait_send()
        for one in stores:
            one.wait()
        if ends:
            relay.landed(0)
            relay.sent(0)

    pl.run_scoped(
        experts,
        pltpu.VMEM((slots, hidden // 2) if ends else (16, 128), bf16),
        pltpu.VMEM((hidden, width), bf16), pltpu.VMEM((width, hidden), bf16),
        pltpu.VMEM((width, slots), bf16),
    )


def forward(groups, cap, ends, tokens, segs, experts, gates, g1, w_qkv, w_out, g2, w_in, w_down, cot):
    rows, width = tokens.shape
    hidden = w_in.shape[1]
    slots = groups * cap
    pairs = width // PAIR
    wide = 3 * BAND
    count = 4 if ends else 1
    parts = [(width // count, hidden)] * count + [(hidden // count, width)] * count
    parts += [(width // count, hidden)] * ends
    shapes = [
        ((rows, width), f32), ((rows, 3 * width), bf16), ((rows, width), bf16), ((rows, width), f32),
        ((pairs, 2 * rows, wide), bf16), ((slots, hidden), bf16), ((slots, hidden), bf16),
    ] + [(one, bf16) for one in parts]
    sems = pltpu.SemaphoreType.DMA
    lines = pltpu.VMEM((rows, width), bf16)
    block = pltpu.VMEM((slots, width), bf16)
    tiny = (16, 128)
    far = block if ends else pltpu.VMEM(tiny, bf16)
    far_line = lines if ends else pltpu.VMEM(tiny, bf16)
    return pl.pallas_call(
        functools.partial(forward_kernel, groups, cap, int(ends)),
        out_shape=[jax.ShapeDtypeStruct(*one) for one in shapes],
        in_specs=[ANY, VMEM, VMEM, VMEM, VMEM, ANY, ANY, VMEM, ANY, ANY, ANY],
        out_specs=[ANY] * len(shapes),
        scratch_shapes=[
            lines, lines, pltpu.VMEM(w_in.shape, bf16), pltpu.VMEM(w_down.shape, bf16), lines,
            pltpu.VMEM((rows, width), f32), pltpu.VMEM((slots, rows), bf16), block, block, block,
            block, lines, pltpu.VMEM((8, rows), f32), far_line, far_line, pltpu.VMEM((8, rows), f32),
            far, far, far, far,
            pltpu.VMEM((slots, hidden), bf16), pltpu.VMEM((slots, hidden), bf16),
            sems((6,)), sems((13,)), sems((slots // GROUP,)), sems((slots // GROUP,)),
        ]
        + [sems((groups,))] * 8
        + [sems((3,))] * 2
        + [sems((1,))] * 2,
        compiler_params=pltpu.CompilerParams(
            collective_id=0, has_side_effects=True, vmem_limit_bytes=60 * MIB
        ),
        cost_estimate=pl.CostEstimate(
            flops=200 * 10**9, bytes_accessed=40 * 10**6, transcendentals=10**7
        ),
        name="forward",
    )(tokens, segs, experts, gates, g1, w_qkv, w_out, g2, w_in, w_down, cot)


def backward_kernel(groups, cap, copies, ends, *refs):
    (
        act_hbm, gpre_hbm, win_hbm, wdown_hbm, te_ref, gate_ref, h1_hbm, cot_hbm, tok_hbm, g1_ref,
        g2_ref, att_hbm, inv_hbm, probs_hbm, qkv_hbm, wqkv_hbm, wout_hbm,
    ) = refs[:17]
    parts, refs = refs[17 : 17 + 9 * ends], refs[17 + 9 * ends :]
    block_out, gtok_out, whole_out, total_ref = refs[:4]
    landed, refs = refs[4 : 4 + 9 * ends], refs[4 + 9 * ends :]
    (
        gv_send, gvr, y_send, yr, dense, other, got, ring, ring_got, final, whole, gains_ref,
        gains_pair, gains_chip, gains_part, gains_ring, load, store, gv_ssem, gv_rsem, y_ssem, y_rsem,
        s_pair, r_pair, s_chip, r_chip, s_ring, r_ring, s_out, r_out, s_gain, r_gain, rel_s, rel_r,
        pool_sem, *pools,
    ) = refs
    dp, me = lax.axis_index("dp"), lax.axis_index("expert")
    slots, width = gvr.shape
    rows, hidden = tok_hbm.shape[0], win_hbm.shape[1]
    rounds = [lax.rem(dp + k, copies) for k in range(copies)]
    half = groups // 2
    per, wide = got.shape[1:]
    many = GROUP // cap
    mine = rows_at(me * cap, cap)

    def exchange(source, target, ssem, rsem):
        return [
            pltpu.make_async_remote_copy(
                src_ref=source.at[rows_at(flip(me, k) * cap, cap)],
                dst_ref=target.at[rows_at(me * cap, cap)],
                send_sem=ssem.at[k],
                recv_sem=rsem.at[k],
                device_id=(dp, flip(me, k)),
                device_id_type=MESH,
            )
            for k in range(1, groups)
        ]

    gv_copies = exchange(gv_send, gvr, gv_ssem, gv_rsem)
    y_copies = exchange(y_send, yr, y_ssem, y_rsem)
    relay = None
    if ends:
        up_far, up_near, up_out, up_own, up_far_in, down_far, down_near, down_out, down_own = parts
        relay = Relay(
            dp, me,
            [
                ("inward", up_near, landed[0]), ("inward", down_own, landed[1]),
                ("inward", up_own, landed[2]), ("across", down_far, landed[3]),
                ("across", pools[0], landed[4]), ("across", pools[1], landed[5]),
                ("across", down_near, landed[6]), ("outward", pools[2], landed[7]),
                ("outward", pools[3], landed[8]),
            ],
            rel_s, rel_r,
        )

    def first():
        if ends:
            relay.start(0, 3)
            relay.merged(up_far, up_far_in, pools[0], pools[4], pool_sem)
            relay.start(4)

    def second():
        if ends:
            relay.sent(0)
            relay.start(1)
            relay.landed(0)
            relay.merged(up_near, landed[0], pools[1], pools[4], pool_sem)
            relay.start(5)

    def third():
        if ends:
            relay.sent(1)
            relay.start(2, 6)
            relay.landed(3)
            relay.merged(down_out, landed[3], pools[2], pools[5], pool_sem)
            relay.landed(4)
            relay.merged(up_out, landed[4], pools[3], pools[4], pool_sem)
            relay.start(7, 8)

    def experts(act, gpre, win, wdown):
        loads = [
            pltpu.make_async_copy(src, dst, load.at[i])
            for i, (src, dst) in enumerate(
                ((win_hbm, win), (gpre_hbm, gpre), (wdown_hbm, wdown), (act_hbm, act))
            )
        ]
        for one in loads:
            one.start()
        greet(
            [(dp, flip(me, k)) for k in range(1, groups)] + [(one, me) for one in rounds[1:]]
        )
        first()
        for one in loads[:2]:
            one.wait()
        for g in range(slots // GROUP - 1, -1, -1):
            at = rows_at(flip(me // many, g) * GROUP, GROUP)

            @pl.loop(0, width // GROUP)
            def _(n):
                cols = rows_at(n * GROUP, GROUP)
                gv_send[at, cols] = dot_nt(gpre[at], win[cols]).astype(bf16)

            for k in range(g * many, (g + 1) * many):
                if k:
                    gv_copies[k - 1].start()
        gvr[mine] = gv_send[mine]
        for one in loads[2:]:
            one.wait()

        @pl.loop(0, width // GROUP)
        def _(n):
            cols = rows_at(n * GROUP, GROUP)
            y_send[:, cols] = dot(act[...], wdown[:, cols]).astype(bf16)

    pl.run_scoped(
        experts,
        pltpu.VMEM((slots, hidden), bf16), pltpu.VMEM((slots, hidden), bf16),
        pltpu.VMEM((width, hidden), bf16), pltpu.VMEM((hidden, width), bf16),
    )

    def dense_part(
        h1, cot, tok, att, inv, probs, qkv, wqkv, wout, place, gh1, low, gatt, inner_sum, gqkv,
        turned, gk, gvv, outv,
    ):
        loads = [
            pltpu.make_async_copy(src, dst, load.at[i])
            for i, (src, dst) in enumerate(
                (
                    (h1_hbm, h1), (cot_hbm, cot), (att_hbm, att), (wout_hbm, wout), (inv_hbm, inv),
                    (qkv_hbm, qkv), (probs_hbm, probs), (tok_hbm, tok), (wqkv_hbm, wqkv),
                )
            )
        ]
        for one in loads:
            one.start()
        spot = column_of(slot_row(te_ref[...], groups, cap))
        for r in range(rows // BAND):
            at = slice(r * BAND, (r + 1) * BAND)
            here = lax.broadcasted_iota(jnp.int32, (BAND, slots), 1).astype(f32)
            place[at] = jnp.where(here == spot[at], 1.0, 0.0).astype(bf16)
        gate = column_of(gate_ref[...])
        gains_ref[...] = jnp.zeros_like(gains_ref)
        for one in gv_copies:
            one.wait_recv()
        for one in y_copies:
            one.start()
        yr[mine] = y_send[mine]
        second()
        for i in range(2):
            loads[i].wait()
        for r in range(rows // BAND):
            at = slice(r * BAND, (r + 1) * BAND)
            back = dot(place[at], gvr[...])
            resid = h1[at]
            centre, inverse = centred(resid)
            unit = centre * inverse
            gains_ref[1:2] += jnp.sum(back * unit, axis=0, keepdims=True)
            slant = back * g2_ref[...].reshape(1, width)
            inner = slant - jnp.mean(slant, axis=-1, keepdims=True)
            inner = inner - unit * jnp.mean(slant * unit, axis=-1, keepdims=True)
            grad = cot[at].astype(f32) + inverse * inner
            gh1[at] = grad
            low[at] = grad.astype(bf16)
        for i in range(2, 5):
            loads[i].wait()

        @pl.loop(0, width // GROUP)
        def _(n):
            cols = rows_at(n * GROUP, GROUP)
            grad = dot_nt(low[...], wout[cols]) * inv[:, cols]
            gatt[:, cols] = grad.astype(bf16)
            inner_sum[:, cols] = grad * att[:, cols].astype(f32) * HEAD_DIM**-0.5

        turned[...] = att[...].T

        @pl.loop(0, width // GROUP)
        def _(n):
            cols = rows_at(n * GROUP, GROUP)
            dense[0:width, rows_at(3 * width + n * GROUP, GROUP)] = dot(
                turned[...], low[:, cols]
            ).astype(bf16)

        loads[5].wait()
        loads[6].wait()
        left = lax.broadcasted_iota(jnp.int32, (1, PAIR), 1) < HEAD_DIM
        none = jnp.zeros((), bf16)

        def halves(block):
            return jnp.concatenate([jnp.where(left, block, none), jnp.where(left, none, block)], axis=0)

        @pl.loop(0, width // PAIR)
        def _(h):
            at = rows_at(h * PAIR, PAIR)
            k_at = rows_at(width + h * PAIR, PAIR)
            v_at = rows_at(2 * width + h * PAIR, PAIR)
            gk[...] = jnp.zeros_like(gk)
            gvv[...] = jnp.zeros_like(gvv)
            for i in range(rows // BAND):
                first, wide = band(i)
                mine, seen = slice(i * BAND, (i + 1) * BAND), slice(first, first + wide)
                keys = qkv[seen, k_at]
                values = qkv[seen, v_at] * jnp.asarray(HEAD_DIM**-0.5, bf16)
                query, grad = halves(qkv[mine, at]), halves(gatt[mine, at])
                share = probs[h, 2 * i * BAND : 2 * (i + 1) * BAND, 0:wide]
                inner = inner_sum[mine, at]
                middle = jnp.concatenate(
                    [
                        jnp.sum(jnp.where(left, inner, 0.0), axis=-1, keepdims=True),
                        jnp.sum(jnp.where(left, 0.0, inner), axis=-1, keepdims=True),
                    ],
                    axis=0,
                )
                graw = (share.astype(f32) * (dot_nt(grad, values) - middle)).astype(bf16)
                gquery = dot(graw, keys)
                gqkv[mine, at] = jnp.where(left, gquery[0:BAND], gquery[BAND:]).astype(bf16)
                gk[seen] += dot_tn(graw, query)
                gvv[seen] += dot_tn(share, grad)
            gqkv[:, k_at] = gk[...].astype(bf16)
            gqkv[:, v_at] = gvv[...].astype(bf16)
        loads[7].wait()
        loads[8].wait()
        for r in range(rows // BAND):
            at = slice(r * BAND, (r + 1) * BAND)
            centre, inverse = centred(tok[at].astype(f32))
            low[at] = (centre * inverse * g1_ref[...].reshape(1, width)).astype(bf16)
        turned[...] = low[...].T

        @pl.loop(0, 3 * width // GROUP)
        def _(n):
            cols = rows_at(n * GROUP, GROUP)
            dense[0:width, cols] = dot(turned[...], gqkv[:, cols]).astype(bf16)

        def rest():
            for r in range(rows // BAND):
                at = slice(r * BAND, (r + 1) * BAND)
                back = dot_nt(gqkv[at], wqkv[...])
                centre, inverse = centred(tok[at].astype(f32))
                unit = centre * inverse
                gains_ref[0:1] += jnp.sum(back * unit, axis=0, keepdims=True)
                slant = back * g1_ref[...].reshape(1, width)
                inner = slant - jnp.mean(slant, axis=-1, keepdims=True)
                inner = inner - unit * jnp.mean(slant * unit, axis=-1, keepdims=True)
                outv[at] = (gh1[at] + inverse * inner).astype(bf16)
            out_three = pltpu.make_async_copy(outv, gtok_out, store.at[0])
            out_three.start()
            for one in y_copies:
                one.wait_recv()
            for r in range(rows // BAND):
                at = slice(r * BAND, (r + 1) * BAND)
                low[at] = (h1[at] + gate[at] * dot(place[at], yr[...])).astype(bf16)
            out_one = pltpu.make_async_copy(low, block_out, store.at[1])
            out_one.start()
            out_one.wait()
            out_three.wait()

        dense_sums(rest)

    def dense_sums(rest):
        chip, core = me // 2, me % 2
        there = flip(me, 1)
        chips = [flip(chip, k) for k in range(half)]
        def send(source, target, ssem, rsem, device):
            return pltpu.make_async_remote_copy(
                src_ref=source, dst_ref=target, send_sem=ssem, recv_sem=rsem, device_id=device,
                device_id_type=MESH,
            )

        started = []

        def go(copy):
            copy.start()
            started.append(copy)
            return copy

        pair = []
        for k in range(half - 1, -1, -1):
            block = chips[k]
            pair.append(
                go(
                    send(
                        dense.at[rows_at(((1 - core) * half + block) * per, per)],
                        other.at[rows_at(block * per, per)],
                        s_pair.at[k], r_pair.at[k], (dp, there),
                    )
                )
            )
        far = {}
        for i, k in enumerate(range(half - 1, -1, -1)):
            at = rows_at(chips[k] * per, per)
            pair[i].wait_recv()
            other[at] = add(dense[rows_at((core * half + chips[k]) * per, per)], other[at])
            if k:
                far[k] = go(
                    send(other.at[at], got.at[k], s_chip.at[k], r_chip.at[k], (dp, chips[k] * 2 + core))
                )
        rest()
        gain_pair = go(send(gains_ref, gains_pair, s_gain.at[0], r_gain.at[0], (dp, there)))
        third()
        gain_pair.wait_recv()
        gains_part[0] = gains_ref[...] + gains_pair[...]
        gain_far = [
            go(
                send(
                    gains_part.at[0], gains_chip.at[k], s_gain.at[k], r_gain.at[k],
                    (dp, chips[k] * 2 + core),
                )
            )
            for k in range(1, half)
        ]
        total = other[rows_at(chip * per, per)].astype(f32)
        for k in range(1, half):
            far[k].wait_recv()
            total = total + got[k].astype(f32)
        share = 3 * width // copies
        thin = width // copies
        for d in range(copies):
            ring[d] = jnp.concatenate(
                [
                    total[:, d * share : (d + 1) * share],
                    total[:, 3 * width + d * thin : 3 * width + (d + 1) * thin],
                ],
                axis=1,
            ).astype(bf16)
        around = [
            go(send(ring.at[rounds[k]], ring_got.at[k], s_ring.at[k], r_ring.at[k], (rounds[k], me)))
            for k in range(1, copies)
        ]
        gains = gains_part[0]
        for k in range(1, half):
            gain_far[k - 1].wait_recv()
            gains = gains + gains_chip[k]
        gains_part[1] = gains
        gain_around = [
            go(
                send(
                    gains_part.at[1], gains_ring.at[k], s_gain.at[half + k], r_gain.at[half + k],
                    (rounds[k], me),
                )
            )
            for k in range(1, copies)
        ]
        summed = ring[dp].astype(f32)
        for k in range(1, copies):
            around[k - 1].wait_recv()
            summed = summed + ring_got[k].astype(f32)
        place = rows_at((core * half + chip) * per, per)
        final[...] = summed.astype(bf16)
        whole[place] = final[...]
        spread = [
            go(send(final, whole.at[place], s_out.at[k], r_out.at[k], (dp, flip(me, k))))
            for k in range(groups - 1, 0, -1)
        ]
        for k in range(1, copies):
            gain_around[k - 1].wait_recv()
            gains = gains + gains_ring[k]
        total_ref[...] = gains
        for one in spread:
            one.wait_recv()
        last = pltpu.make_async_copy(whole, whole_out, store.at[2])
        last.start()
        last.wait()
        for one in started:
            one.wait_send()

    pl.run_scoped(
        dense_part,
        pltpu.VMEM((rows, width), f32), pltpu.VMEM((rows, width), bf16),
        pltpu.VMEM((rows, width), bf16), pltpu.VMEM((rows, width), bf16),
        pltpu.VMEM((rows, width), f32), pltpu.VMEM(probs_hbm.shape, bf16),
        pltpu.VMEM((rows, 3 * width), bf16), pltpu.VMEM((width, 3 * width), bf16),
        pltpu.VMEM((width, width), bf16), pltpu.VMEM((rows, slots), bf16),
        pltpu.VMEM((rows, width), f32), pltpu.VMEM((rows, width), bf16),
        pltpu.VMEM((rows, width), bf16), pltpu.VMEM((rows, width), f32),
        pltpu.VMEM((rows, 3 * width), bf16), pltpu.VMEM((width, rows), bf16),
        pltpu.VMEM((rows, PAIR), f32), pltpu.VMEM((rows, PAIR), f32),
        pltpu.VMEM((rows, width), bf16),
    )
    for one in gv_copies + y_copies:
        one.wait_send()
    if ends:
        for i in range(9):
            if i not in (0, 3, 4):
                relay.landed(i)
            if i > 1:
                relay.sent(i)


def backward(
    groups, cap, copies, ends, per, act, gpre, w_in, w_down, experts, gates, h1, cot, tok, g1, g2, att,
    inv, probs, qkv, w_qkv, w_out, parts,
):
    slots, hidden = act.shape
    rows, width = tok.shape
    wide = 4 * width
    half = groups // 2
    thin = wide // copies
    sems = pltpu.SemaphoreType.DMA
    block = pltpu.VMEM((slots, width), bf16)
    tile = (8, width)
    up = (width // 4, hidden)
    down = (hidden // 4, width)
    land = [up, down, up, down, up, up, down, down, up] if ends else []
    pools = [up, up, down, up] if ends else []
    return pl.pallas_call(
        functools.partial(backward_kernel, groups, cap, copies, ends),
        out_shape=[
            jax.ShapeDtypeStruct((rows, width), bf16), jax.ShapeDtypeStruct((rows, width), bf16),
            jax.ShapeDtypeStruct((groups * per, thin), bf16), jax.ShapeDtypeStruct(tile, f32),
        ]
        + [jax.ShapeDtypeStruct(one, bf16) for one in land],
        in_specs=[ANY] * 4 + [VMEM] * 2 + [ANY] * 3 + [VMEM] * 2 + [ANY] * (6 + len(parts)),
        out_specs=[ANY] * 3 + [VMEM] + [ANY] * len(land),
        scratch_shapes=[
            block, block, block, block,
            pltpu.VMEM((groups * per, wide), bf16), pltpu.VMEM((half * per, wide), bf16),
            pltpu.VMEM((half, per, wide), bf16), pltpu.VMEM((copies, per, thin), bf16),
            pltpu.VMEM((copies, per, thin), bf16), pltpu.VMEM((per, thin), bf16),
            pltpu.VMEM((groups * per, thin), bf16), pltpu.VMEM(tile, f32), pltpu.VMEM(tile, f32),
            pltpu.VMEM((half, *tile), f32), pltpu.VMEM((2, *tile), f32),
            pltpu.VMEM((copies, *tile), f32), sems((9,)), sems((3,)), sems((groups,)),
            sems((groups,)), sems((groups,)), sems((groups,)), sems((half,)), sems((half,)),
            sems((half,)), sems((half,)), sems((copies,)), sems((copies,)), sems((groups,)),
            sems((groups,)), sems((half + copies,)), sems((half + copies,)), sems((9,)), sems((9,)),
            sems((2,)),
        ]
        + [pltpu.VMEM(one, bf16) for one in pools]
        + [pltpu.VMEM(one, bf16) for one in (up, down) if ends],
        compiler_params=pltpu.CompilerParams(
            collective_id=1, has_side_effects=True, vmem_limit_bytes=60 * MIB
        ),
        cost_estimate=pl.CostEstimate(
            flops=200 * 10**9, bytes_accessed=40 * 10**6, transcendentals=0
        ),
        name="backward",
    )(
        act, gpre, w_in, w_down, experts, gates, h1, cot, tok, g1, g2, att, inv, probs, qkv, w_qkv,
        w_out, *parts,
    )


def finish_kernel(*refs):
    (
        up_own, up_in, up_across, up_out, up_outward, down_own, down_in, down_across, down_out,
        down_outward, block, gtok, whole_ref, gains_ref, up_ref, down_ref, qkv_hbm, out_hbm, one_ref,
        two_ref, block_ref, gtok_ref, a, b, c, d, e, f, up, down, qkv_ref, out_ref,
        block_line, gtok_line, load, store,
    ) = refs
    dp = lax.axis_index("dp")
    outer = (dp == 0) | (dp == 3)
    inner = jnp.logical_not(outer)
    hand_in = [
        pltpu.make_async_copy(block, block_line, load.at[6]),
        pltpu.make_async_copy(gtok, gtok_line, load.at[7]),
    ]
    handed = [
        pltpu.make_async_copy(block_line, block_ref, store.at[0]),
        pltpu.make_async_copy(gtok_line, gtok_ref, store.at[1]),
    ]

    def loads(sources, targets):
        return [
            pltpu.make_async_copy(src, dst, load.at[i])
            for i, (src, dst) in enumerate(zip(sources, targets))
        ]

    inside = loads((up_own, up_in, up_across, down_own, down_in, down_across), (a, b, c, d, e, f))
    outside = loads((up_out, up_outward, down_out, down_outward), (a, b, d, e))

    @pl.when(inner)
    def _():
        for one in inside:
            one.start()

    @pl.when(outer)
    def _():
        for one in outside:
            one.start()

    for one in hand_in:
        one.start()
    thin = qkv_ref.shape[0]
    turned = whole_ref[...].astype(f32).T
    qkv_ref[...] = turned[:thin]
    out_ref[...] = turned[thin:]
    handed += [
        pltpu.make_async_copy(qkv_ref, qkv_hbm, store.at[4]),
        pltpu.make_async_copy(out_ref, out_hbm, store.at[5]),
    ]
    for one in hand_in:
        one.wait()
    for one in handed:
        one.start()
    size = one_ref.shape[1]
    for row, target in ((0, one_ref), (1, two_ref)):
        line = jnp.zeros((1, size), f32)
        for plane in range(4):
            part = gains_ref[row : row + 1, plane * size : (plane + 1) * size]
            line = jnp.where(dp == plane, part, line)
        target[...] = line

    def summed(target, terms):
        lines = target.shape[0] // 12

        @pl.loop(0, 12)
        def _(r):
            at = rows_at(r * lines, lines)
            total = terms[0][at].astype(f32)
            for term in terms[1:]:
                total = total + term[at].astype(f32)
            target[at] = total

    up_store = pltpu.make_async_copy(up, up_ref, store.at[2])
    down_store = pltpu.make_async_copy(down, down_ref, store.at[3])

    @pl.when(inner)
    def _():
        for one in inside[:3]:
            one.wait()
        summed(up, (a, b, c))
        up_store.start()
        for one in inside[3:]:
            one.wait()
        summed(down, (d, e, f))

    @pl.when(outer)
    def _():
        for one in outside[:2]:
            one.wait()
        summed(up, (a, b))
        up_store.start()
        for one in outside[2:]:
            one.wait()
        summed(down, (d, e))

    down_store.start()
    for one in handed:
        one.wait()
    up_store.wait()
    down_store.wait()


def finish(ups, downs, block, gtok, whole, gains):
    up, down = ups[0].shape, downs[0].shape
    width = whole.shape[1]
    thin = width // 4
    sems = pltpu.SemaphoreType.DMA
    return pl.pallas_call(
        finish_kernel,
        out_shape=[
            jax.ShapeDtypeStruct(up, f32), jax.ShapeDtypeStruct(down, f32),
            jax.ShapeDtypeStruct((3 * thin, whole.shape[0]), f32),
            jax.ShapeDtypeStruct((thin, whole.shape[0]), f32),
            jax.ShapeDtypeStruct((1, thin), f32), jax.ShapeDtypeStruct((1, thin), f32),
            jax.ShapeDtypeStruct(block.shape, bf16), jax.ShapeDtypeStruct(gtok.shape, bf16),
        ],
        in_specs=[ANY] * 12 + [VMEM] * 2,
        out_specs=[ANY] * 4 + [VMEM] * 2 + [ANY] * 2,
        scratch_shapes=[pltpu.VMEM(up, bf16)] * 3
        + [pltpu.VMEM(down, bf16)] * 3
        + [
            pltpu.VMEM(up, f32), pltpu.VMEM(down, f32), pltpu.VMEM((3 * thin, whole.shape[0]), f32),
            pltpu.VMEM((thin, whole.shape[0]), f32), pltpu.VMEM(block.shape, bf16),
            pltpu.VMEM(gtok.shape, bf16), sems((8,)), sems((6,)),
        ],
        compiler_params=pltpu.CompilerParams(vmem_limit_bytes=60 * MIB),
        name="finish",
    )(*ups, *downs, block, gtok, whole, gains)


def shards(
    tokens, segment_ids, token_expert, gates, ln1_gain, w_qkv, w_out, ln2_gain, expert_in,
    expert_out, cotangent,
):
    rows, width = tokens.shape
    groups, copies = lax.axis_size("expert"), lax.axis_size("dp")
    cap = 2 * rows // groups
    per = -(-width // (16 * groups)) * 16
    w_in, w_down = expert_in[0], expert_out[0]
    experts, gate_row = token_expert.reshape(1, rows), gates.reshape(1, rows)
    ends = copies == 4
    h1, qkv, att, inv, probs, act, gpre, *parts = forward(
        groups, cap, ends, tokens, segment_ids, experts, gate_row, ln1_gain, w_qkv, w_out,
        ln2_gain, w_in, w_down, cotangent,
    )
    if ends:
        up_far, up_near, up_out, up_own, down_far, down_near, down_out, down_own, up_far_in = parts
        parts = [up_far, up_near, up_out, up_own, up_far_in, down_far, down_near, down_out, down_own]
    block_out, grad_tokens, whole, gains, *landed = backward(
        groups, cap, copies, ends, per, act, gpre, w_in, w_down, experts, gate_row, h1, cotangent,
        tokens, ln1_gain, ln2_gain, att, inv, probs, qkv, w_qkv, w_out, parts if ends else [],
    )
    if ends:
        _, down_own_in, up_own_in, _, _, up_across, down_across, down_outward, up_outward = landed
        up_share, down_share, share_qkv, share_out, share_one, share_two, block, gtok = finish(
            (up_own, up_own_in, up_across, up_out, up_outward),
            (down_own, down_own_in, down_across, down_out, down_outward),
            block_out, grad_tokens, whole[:width], gains,
        )
        return (
            block, gtok, share_one[0], share_qkv.T, share_out.T, share_two[0], up_share[None],
            down_share[None],
        )
    up_share, down_share = (
        lax.psum_scatter(one[None], "dp", scatter_dimension=1, tiled=True) for one in parts
    )
    whole = whole[:width].astype(f32)
    share = width // copies
    gains = lax.dynamic_slice_in_dim(gains, lax.axis_index("dp") * share, share, 1)
    return (
        block_out,
        grad_tokens,
        gains[0],
        whole[:, : 3 * share],
        whole[:, 3 * share :],
        gains[1],
        up_share.astype(f32),
        down_share.astype(f32),
    )


def solution(mesh):
    tokens, experts = P(("dp", "expert"), None), P("expert", None, None)
    return jax.shard_map(
        shards,
        mesh=mesh,
        in_specs=(
            tokens, tokens, tokens, P(("dp", "expert")), P(), P(), P(), P(), experts, experts,
            tokens,
        ),
        out_specs=(
            tokens, tokens, P("dp"), P(None, "dp"), P(None, "dp"), P("dp"),
            P("expert", "dp", None), P("expert", "dp", None),
        ),
        check_vma=False,
    )
```

```python
import functools

import jax
import jax.numpy as jnp
from jax import lax
from jax.experimental import pallas as pl
from jax.experimental.pallas import tpu as pltpu
from jax.sharding import PartitionSpec as P

HEAD_DIM = 64
EPSILON = 1e-05
NEG_LARGE = -1e30
BAND = 128
PAIR = 2 * HEAD_DIM
GROUP = 256
CHUNK = 512
MIB = 2**20
MESH = pl.DeviceIdType.MESH
ANY = pl.BlockSpec(memory_space=pl.ANY)
VMEM = pl.BlockSpec(memory_space=pltpu.VMEM)
f32, bf16 = jnp.float32, jnp.bfloat16


def dot(a, b):
    return jnp.dot(a, b, preferred_element_type=f32)


def dot_nt(a, b):
    return lax.dot_general(a, b, (((1,), (1,)), ((), ())), preferred_element_type=f32)


def dot_tn(a, b):
    return lax.dot_general(a, b, (((0,), (0,)), ((), ())), preferred_element_type=f32)


def flip(index, bits):
    place = 1
    while bits:
        if bits % 2:
            index = index + place * (1 - 2 * ((index // place) % 2))
        bits, place = bits // 2, place * 2
    return index


def add(a, b):
    return (a.astype(f32) + b.astype(f32)).astype(bf16)


def rows_at(start, size):
    return pl.ds(pl.multiple_of(start, size), size)


def greet(peers):
    barrier = pltpu.get_barrier_semaphore()
    for peer in peers:
        pl.semaphore_signal(barrier, inc=1, device_id=peer, device_id_type=MESH)
    pl.semaphore_wait(barrier, len(peers))


def sides(dp):
    side = dp // 2
    return flip(dp, 1), 3 - dp, [3 * (1 - side), 2 - side, 3 * side, 1 + side]


class Relay:
    def __init__(self, dp, me, moves, ssem, rsem):
        self.outer = (dp == 0) | (dp == 3)
        self.inner = jnp.logical_not(self.outer)
        beside, across, _ = sides(dp)
        self.moves = []
        for i, (kind, source, target) in enumerate(moves):
            plane = across if kind == "across" else beside
            copy = pltpu.make_async_remote_copy(
                src_ref=source, dst_ref=target, send_sem=ssem.at[i], recv_sem=rsem.at[i],
                device_id=(plane, me), device_id_type=MESH,
            )
            sender = self.outer if kind == "inward" else self.inner
            receiver = self.outer if kind == "outward" else self.inner
            self.moves.append((copy, sender, receiver))

    def start(self, *which):
        for i in which:
            copy, sender, _ = self.moves[i]
            pl.when(sender)(copy.start)

    def sent(self, i):
        pl.when(self.moves[i][1])(self.moves[i][0].wait_send)

    def landed(self, i):
        pl.when(self.moves[i][2])(self.moves[i][0].wait_recv)

    def merged(self, first, second, total, spare, sem):
        @pl.when(self.inner)
        def _():
            loads = [
                pltpu.make_async_copy(first, total, sem.at[0]),
                pltpu.make_async_copy(second, spare, sem.at[1]),
            ]
            for one in loads:
                one.start()
            for one in loads:
                one.wait()
            lines = total.shape[0] // 12

            @pl.loop(0, 12)
            def _(r):
                at = rows_at(r * lines, lines)
                total[at] = add(total[at], spare[at])


def band(index):
    first = max(0, index - 2) * BAND
    return first, (index + 1) * BAND - first


def column_of(row):
    size = row.shape[1]
    eye = lax.broadcasted_iota(jnp.int32, (size, size), 0) == lax.broadcasted_iota(
        jnp.int32, (size, size), 1
    )
    return jnp.sum(jnp.where(eye, row, 0.0), axis=1, keepdims=True)


def slot_row(experts, num_experts, capacity):
    rows = experts.shape[1]
    lines = max(16, num_experts)
    onehot = lax.broadcasted_iota(jnp.int32, (lines, rows), 0) == experts
    onehot = jnp.where(onehot, 1.0, 0.0)
    before = lax.broadcasted_iota(jnp.int32, (rows, rows), 0) < lax.broadcasted_iota(
        jnp.int32, (rows, rows), 1
    )
    earlier = dot(onehot.astype(bf16), jnp.where(before, 1.0, 0.0).astype(bf16))
    rank = jnp.sum(onehot * earlier, axis=0, keepdims=True)
    return experts.astype(f32) * float(capacity) + rank


def centred(hidden):
    centre = hidden - jnp.mean(hidden, axis=-1, keepdims=True)
    spread = jnp.mean(centre * centre, axis=-1, keepdims=True)
    return centre, lax.rsqrt(spread + EPSILON)


def gelu_pair(x):
    bell = jnp.exp2((-0.5 * 1.4426950408889634) * (x * x))
    phi = 0.5 + 0.5 * lax.erf(x * 0.7071067811865476)
    return x * phi, phi + x * (bell * 0.3989422804014327)


def gelu(x):
    return gelu_pair(x)[0]


def forward_kernel(groups, cap, ends, *refs):
    (
        tok_hbm, seg_ref, te_ref, gate_ref, g1_ref, wqkv_hbm, wout_hbm, g2_ref, win_hbm, wdown_hbm,
        cot_hbm, h1_out, qkv_out, att_out, inv_out, probs_out, act_out, gpre_out,
    ) = refs[:18]
    count = 4 if ends else 1
    ups, downs = refs[18 : 18 + count], refs[18 + count : 18 + 2 * count]
    up_land = refs[18 + 2 * count : 18 + 2 * count + ends]
    (
        tok, cot, win, wdown, low, h1, place, sent, gy_send, gy_got, v_got, gy_low, spot_own, gy_line,
        v_line, spot_far, place_far, gy_fsend, far_send, gy_far, v_far, act,
        gpre, load, store, act_store, gpre_store, gy_ssem, gy_rsem, v_ssem, v_rsem, gy_fssem,
        gy_frsem, v_fssem, v_frsem, line_ssem, line_rsem, rel_s, rel_r,
    ) = refs[18 + 2 * count + ends :]
    dp, me = lax.axis_index("dp"), lax.axis_index("expert")
    rows, width = tok.shape
    slots, hidden = act.shape
    pairs = width // PAIR
    outer = (dp == 0) | (dp == 3)
    inner = jnp.logical_not(outer)
    first_loads = [
        pltpu.make_async_copy(src, dst, load.at[i])
        for i, (src, dst) in enumerate(
            ((cot_hbm, cot), (tok_hbm, tok), (win_hbm, win), (wdown_hbm, wdown))
        )
    ]
    first_loads[0].start()
    first_loads[1].start()
    beside = [(flip(dp, 1), me)] if ends else []
    greet([(dp, flip(me, k)) for k in range(1, groups)] + beside)

    def exchange(source, target, send, receive, k):
        peer = flip(me, k)
        return pltpu.make_async_remote_copy(
            src_ref=source.at[rows_at(peer * cap, cap)],
            dst_ref=target.at[rows_at(me * cap, cap)],
            send_sem=send.at[k],
            recv_sem=receive.at[k],
            device_id=(dp, peer),
            device_id_type=MESH,
        )

    gy_copies = [exchange(gy_send, gy_got, gy_ssem, gy_rsem, k) for k in range(1, groups)]
    v_copies = [exchange(sent, v_got, v_ssem, v_rsem, k) for k in range(1, groups)]
    far_groups = groups if ends else 0
    gy_fars = [exchange(gy_fsend, gy_far, gy_fssem, gy_frsem, k) for k in range(1, far_groups)]
    v_fars = [exchange(far_send, v_far, v_fssem, v_frsem, k) for k in range(1, far_groups)]
    lines = ends and [
        pltpu.make_async_remote_copy(
            src_ref=source, dst_ref=target, send_sem=line_ssem.at[i], recv_sem=line_rsem.at[i],
            device_id=(flip(dp, 1), me), device_id_type=MESH,
        )
        for i, (source, target) in enumerate(
            ((spot_own, spot_far), (gy_low, gy_line), (low, v_line))
        )
    ]

    def when(condition, action):
        if ends:
            pl.when(condition)(action)

    def positions(spot, target):
        @pl.loop(0, slots // GROUP)
        def _(g):
            here = lax.broadcasted_iota(jnp.int32, (GROUP, rows), 0) + g * GROUP
            there = jnp.where(here.astype(f32) == spot, 1.0, 0.0)
            target[rows_at(g * GROUP, GROUP)] = there.astype(bf16)

    def placed(where, line, target):
        @pl.loop(0, width // GROUP)
        def _(n):
            cols = rows_at(n * GROUP, GROUP)
            target[:, cols] = dot(where[...], line[:, cols]).astype(bf16)

    def far_gy():
        lines[0].wait_recv()
        lines[1].wait_recv()
        positions(spot_far[0:1], place_far)
        placed(place_far, gy_line, gy_fsend)
        for one in gy_fars:
            one.start()
        gy_far[mine] = gy_fsend[mine]

    def far_v():
        lines[2].wait_recv()
        placed(place_far, v_line, far_send)
        for one in v_fars:
            one.start()
        v_far[mine] = far_send[mine]

    mine = rows_at(me * cap, cap)

    def attention(wqkv, wout, qkv, att, inv, probs, bias):
        loads = [
            pltpu.make_async_copy(wqkv_hbm, wqkv, load.at[4]),
            pltpu.make_async_copy(wout_hbm, wout, load.at[5]),
        ]
        for one in loads + first_loads[2:]:
            one.start()
        spot = slot_row(te_ref[...], groups, cap)

        positions(spot, place)
        first_loads[0].wait()
        gate = column_of(gate_ref[...])
        gy_low[...] = (gate * cot[...].astype(f32)).astype(bf16)
        if ends:
            spot_own[...] = jnp.broadcast_to(spot, spot_own.shape)

            @pl.when(outer)
            def _():
                lines[0].start()
                lines[1].start()

        placed(place, gy_low, gy_send)
        for one in gy_copies:
            one.start()
        gy_got[mine] = gy_send[mine]
        segs = seg_ref[...].astype(f32)
        seg_col = column_of(segs)
        for i in range(rows // BAND):
            first, wide = band(i)
            causal = (lax.broadcasted_iota(jnp.int32, (BAND, wide), 0) + i * BAND) >= (
                lax.broadcasted_iota(jnp.int32, (BAND, wide), 1) + first
            )
            same = seg_col[i * BAND : (i + 1) * BAND] == segs[:, first : first + wide]
            bias[i * BAND : (i + 1) * BAND, 0:wide] = jnp.where(causal & same, 0.0, NEG_LARGE)

        first_loads[1].wait()

        @pl.loop(0, rows // BAND)
        def _(r):
            at = rows_at(r * BAND, BAND)
            centre, inverse = centred(tok[at].astype(f32))
            low[at] = (centre * inverse * g1_ref[...].reshape(1, width)).astype(bf16)

        loads[0].wait()

        @pl.loop(0, 3 * width // GROUP)
        def _(c):
            at = rows_at(c * GROUP, GROUP)
            qkv[:, at] = dot(low[...], wqkv[:, at]).astype(bf16)

        left = lax.broadcasted_iota(jnp.int32, (1, PAIR), 1) < HEAD_DIM
        none, unit = jnp.zeros((), bf16), jnp.ones((), bf16)

        def attend(h):
            at = rows_at(h * PAIR, PAIR)
            k_at = rows_at(width + h * PAIR, PAIR)
            v_at = rows_at(2 * width + h * PAIR, PAIR)
            for i in range(rows // BAND):
                first, wide = band(i)
                here = slice(i * BAND, (i + 1) * BAND)
                keys = qkv[first : first + wide, k_at]
                values = qkv[first : first + wide, v_at]
                query = qkv[here, at] * jnp.asarray(HEAD_DIM**-0.5, bf16)
                query = jnp.concatenate(
                    [jnp.where(left, query, none), jnp.where(left, none, query)], axis=0
                )
                scores = dot_nt(query, keys).reshape(2, BAND, wide) + bias[here, 0:wide][None]
                weights = jnp.exp(scores - jnp.max(scores, axis=-1, keepdims=True)).astype(bf16)
                probs[h, 2 * i * BAND : 2 * (i + 1) * BAND, 0:wide] = weights.reshape(
                    2 * BAND, wide
                )
                one = dot(weights[0], jnp.where(left, values, unit))
                two = dot(weights[1], jnp.where(left, unit, values))
                scale = 1.0 / pltpu.roll(jnp.where(left, two, one), HEAD_DIM, 1)
                inv[here, at] = scale
                att[here, at] = (jnp.where(left, one, two) * scale).astype(bf16)

        pl.loop(0, pairs)(attend)
        when(inner, far_gy)
        stores = [
            pltpu.make_async_copy(src, dst, store.at[i])
            for i, (src, dst) in enumerate(
                ((qkv, qkv_out), (probs, probs_out), (att, att_out), (inv, inv_out))
            )
        ]
        for one in stores:
            one.start()
        loads[1].wait()

        @pl.loop(0, width // GROUP)
        def _(n):
            cols = rows_at(n * GROUP, GROUP)
            h1[:, cols] = dot(att[...], wout[:, cols])

        @pl.loop(0, rows // BAND)
        def _(r):
            at = rows_at(r * BAND, BAND)
            resid = tok[at].astype(f32) + h1[at]
            h1[at] = resid
            centre, inverse = centred(resid)
            low[at] = (centre * inverse * g2_ref[...].reshape(1, width)).astype(bf16)

        when(outer, lambda: lines[2].start())

        placed(place, low, sent)
        for one in v_copies:
            one.start()
        v_got[mine] = sent[mine]
        for one in stores:
            one.wait()

    pl.run_scoped(
        attention,
        pltpu.VMEM((width, 3 * width), bf16), pltpu.VMEM((width, width), bf16),
        pltpu.VMEM((rows, 3 * width), bf16), pltpu.VMEM((rows, width), bf16),
        pltpu.VMEM((rows, width), f32), pltpu.VMEM((pairs, 2 * rows, 3 * BAND), bf16),
        pltpu.VMEM((rows, 3 * BAND), f32),
    )

    def experts(act_far, gdown, gup, turned):
        stores = [pltpu.make_async_copy(h1, h1_out, store.at[4])]
        stores[0].start()
        for one in first_loads[2:]:
            one.wait()
        for one in gy_copies:
            one.wait_recv()

        @pl.loop(0, hidden // GROUP)
        def _(c):
            at = rows_at(c * GROUP, GROUP)
            gpre[:, at] = dot_nt(gy_got[...], wdown[at]).astype(bf16)

        many = GROUP // cap
        for g in range(slots // GROUP):
            for k in range(g * many, (g + 1) * many):
                if k:
                    v_copies[k - 1].wait_recv()
            at = rows_at(flip(me // many, g) * GROUP, GROUP)

            @pl.loop(0, hidden // CHUNK)
            def _(c):
                cols = rows_at(c * CHUNK, CHUNK)
                value, back = gelu_pair(dot(v_got[at], win[:, cols]))
                act[at, cols] = value.astype(bf16)
                gpre[at, cols] = (gpre[at, cols].astype(f32) * back).astype(bf16)

            for source, target, sem in ((act, act_out, act_store), (gpre, gpre_out, gpre_store)):
                stores.append(pltpu.make_async_copy(source.at[at], target.at[at], sem.at[g]))
                stores[-1].start()
            if g == 1:
                when(inner, far_v)

        turned[...] = v_got[...].T

        @pl.loop(0, hidden // GROUP)
        def _(c):
            cols = rows_at(c * GROUP, GROUP)
            gup[:, cols] = dot(turned[...], gpre[:, cols]).astype(bf16)

        shares = sides(dp)[2] if ends else [0]
        size, share = width // count, hidden // count
        for i, (one, part) in enumerate(zip(shares, ups)):
            source = gup.at[rows_at(one * size, size)]
            stores.append(pltpu.make_async_copy(source, part, store.at[5 + i]))
            stores[-1].start()
        if ends:
            relay = Relay(
                dp, me, [("inward", gup.at[rows_at(shares[0] * size, size)], up_land[0])],
                rel_s, rel_r,
            )
            relay.start(0)

        def down(kept, shared):
            for i in kept:

                @pl.loop(0, share // GROUP)
                def _(c):
                    cols = pl.ds(pl.multiple_of(shares[i] * share + c * GROUP, GROUP), GROUP)
                    at = pl.ds(pl.multiple_of(i * share + c * GROUP, GROUP), GROUP)
                    total = dot_tn(act[:, cols], gy_got[...])
                    if shared:
                        total = total + dot_tn(act_far[:, at], gy_far[...])
                    gdown[at] = total.astype(bf16)

            for i in kept:
                at = slice(i * share, (i + 1) * share)
                pltpu.make_async_copy(gdown.at[at], downs[i], store.at[9 + i]).start()

        def taken(kept):
            for i in kept:
                at = slice(i * share, (i + 1) * share)
                pltpu.make_async_copy(gdown.at[at], downs[i], store.at[9 + i]).wait()

        def inside():
            for g in range(slots // GROUP):
                for k in range(g * many, (g + 1) * many):
                    if k:
                        v_fars[k - 1].wait_recv()
                at = rows_at(flip(me // many, g) * GROUP, GROUP)
                for i in range(2):

                    @pl.loop(0, 2)
                    def _(c):
                        cols = pl.ds(pl.multiple_of(shares[i] * share + c * (share // 2), 128), share // 2)
                        kept = pl.ds(pl.multiple_of(i * share + c * (share // 2), 128), share // 2)
                        act_far[at, kept] = gelu(dot(v_far[at], win[:, cols])).astype(bf16)

            for one in gy_fars:
                one.wait_recv()
            down([0, 1], True)
            for one in gy_fars + v_fars:
                one.wait_send()
            taken([0, 1])

        down([2, 3] if ends else [0], False)
        if ends:
            pl.when(inner)(inside)

            @pl.when(outer)
            def _():
                for one in lines:
                    one.wait_send()

        taken([2, 3] if ends else [0])
        for one in gy_copies + v_copies:
            one.wait_send()
        for one in stores:
            one.wait()
        if ends:
            relay.landed(0)
            relay.sent(0)

    pl.run_scoped(
        experts,
        pltpu.VMEM((slots, hidden // 2) if ends else (16, 128), bf16),
        pltpu.VMEM((hidden, width), bf16), pltpu.VMEM((width, hidden), bf16),
        pltpu.VMEM((width, slots), bf16),
    )


def forward(groups, cap, ends, tokens, segs, experts, gates, g1, w_qkv, w_out, g2, w_in, w_down, cot):
    rows, width = tokens.shape
    hidden = w_in.shape[1]
    slots = groups * cap
    pairs = width // PAIR
    wide = 3 * BAND
    count = 4 if ends else 1
    parts = [(width // count, hidden)] * count + [(hidden // count, width)] * count
    parts += [(width // count, hidden)] * ends
    shapes = [
        ((rows, width), f32), ((rows, 3 * width), bf16), ((rows, width), bf16), ((rows, width), f32),
        ((pairs, 2 * rows, wide), bf16), ((slots, hidden), bf16), ((slots, hidden), bf16),
    ] + [(one, bf16) for one in parts]
    sems = pltpu.SemaphoreType.DMA
    lines = pltpu.VMEM((rows, width), bf16)
    block = pltpu.VMEM((slots, width), bf16)
    tiny = (16, 128)
    far = block if ends else pltpu.VMEM(tiny, bf16)
    far_line = lines if ends else pltpu.VMEM(tiny, bf16)
    return pl.pallas_call(
        functools.partial(forward_kernel, groups, cap, int(ends)),
        out_shape=[jax.ShapeDtypeStruct(*one) for one in shapes],
        in_specs=[ANY, VMEM, VMEM, VMEM, VMEM, ANY, ANY, VMEM, ANY, ANY, ANY],
        out_specs=[ANY] * len(shapes),
        scratch_shapes=[
            lines, lines, pltpu.VMEM(w_in.shape, bf16), pltpu.VMEM(w_down.shape, bf16), lines,
            pltpu.VMEM((rows, width), f32), pltpu.VMEM((slots, rows), bf16), block, block, block,
            block, lines, pltpu.VMEM((8, rows), f32), far_line, far_line, pltpu.VMEM((8, rows), f32),
            pltpu.VMEM((slots, rows) if ends else tiny, bf16), far, far, far, far,
            pltpu.VMEM((slots, hidden), bf16), pltpu.VMEM((slots, hidden), bf16),
            sems((6,)), sems((13,)), sems((slots // GROUP,)), sems((slots // GROUP,)),
        ]
        + [sems((groups,))] * 8
        + [sems((3,))] * 2
        + [sems((1,))] * 2,
        compiler_params=pltpu.CompilerParams(
            collective_id=0, has_side_effects=True, vmem_limit_bytes=60 * MIB
        ),
        cost_estimate=pl.CostEstimate(
            flops=200 * 10**9, bytes_accessed=40 * 10**6, transcendentals=10**7
        ),
        name="forward",
    )(tokens, segs, experts, gates, g1, w_qkv, w_out, g2, w_in, w_down, cot)


def backward_kernel(groups, cap, copies, ends, *refs):
    (
        act_hbm, gpre_hbm, win_hbm, wdown_hbm, te_ref, gate_ref, h1_hbm, cot_hbm, tok_hbm, g1_ref,
        g2_ref, att_hbm, inv_hbm, probs_hbm, qkv_hbm, wqkv_hbm, wout_hbm,
    ) = refs[:17]
    parts, refs = refs[17 : 17 + 9 * ends], refs[17 + 9 * ends :]
    block_out, gtok_out, whole_out, total_ref = refs[:4]
    landed, refs = refs[4 : 4 + 9 * ends], refs[4 + 9 * ends :]
    (
        gv_send, gvr, y_send, yr, dense, other, got, ring, ring_got, final, whole, gains_ref,
        gains_pair, gains_chip, gains_part, gains_ring, load, store, gv_ssem, gv_rsem, y_ssem, y_rsem,
        s_pair, r_pair, s_chip, r_chip, s_ring, r_ring, s_out, r_out, s_gain, r_gain, rel_s, rel_r,
        pool_sem, *pools,
    ) = refs
    dp, me = lax.axis_index("dp"), lax.axis_index("expert")
    slots, width = gvr.shape
    rows, hidden = tok_hbm.shape[0], win_hbm.shape[1]
    rounds = [lax.rem(dp + k, copies) for k in range(copies)]
    half = groups // 2
    per, wide = got.shape[1:]
    many = CHUNK // cap
    mine = rows_at(me * cap, cap)

    def exchange(source, target, ssem, rsem):
        return [
            pltpu.make_async_remote_copy(
                src_ref=source.at[rows_at(flip(me, k) * cap, cap)],
                dst_ref=target.at[rows_at(me * cap, cap)],
                send_sem=ssem.at[k],
                recv_sem=rsem.at[k],
                device_id=(dp, flip(me, k)),
                device_id_type=MESH,
            )
            for k in range(1, groups)
        ]

    gv_copies = exchange(gv_send, gvr, gv_ssem, gv_rsem)
    y_copies = exchange(y_send, yr, y_ssem, y_rsem)
    relay = None
    if ends:
        up_far, up_near, up_out, up_own, up_far_in, down_far, down_near, down_out, down_own = parts
        relay = Relay(
            dp, me,
            [
                ("inward", up_near, landed[0]), ("inward", down_own, landed[1]),
                ("inward", up_own, landed[2]), ("across", down_far, landed[3]),
                ("across", pools[0], landed[4]), ("across", pools[1], landed[5]),
                ("across", down_near, landed[6]), ("outward", pools[2], landed[7]),
                ("outward", pools[3], landed[8]),
            ],
            rel_s, rel_r,
        )

    chip, core = me // 2, me % 2
    there = flip(me, 1)
    chips = [flip(chip, k) for k in range(half)]
    started = []
    sets = [(0, width), (width, 3 * width // 2), (5 * width // 2, 3 * width // 2)]
    pair, far = {}, {}

    def send(source, target, ssem, rsem, device):
        return pltpu.make_async_remote_copy(
            src_ref=source, dst_ref=target, send_sem=ssem, recv_sem=rsem, device_id=device,
            device_id_type=MESH,
        )

    def go(copy):
        copy.start()
        started.append(copy)
        return copy

    def pair_send(i):
        cols = slice(sets[i][0], sum(sets[i]))
        pair[i] = go(
            send(
                dense.at[rows_at((1 - core) * (half * per), half * per), cols], other.at[:, cols],
                s_pair.at[i], r_pair.at[i], (dp, there),
            )
        )

    def combine(i):
        cols = slice(sets[i][0], sum(sets[i]))
        pair[i].wait_recv()
        for k in range(half - 1, -1, -1):
            at = rows_at(chips[k] * per, per)
            own = rows_at((core * half + chips[k]) * per, per)
            other[at, cols] = add(dense[own, cols], other[at, cols])
            if k:
                far[i, k] = go(
                    send(
                        other.at[at, cols], got.at[k, :, cols], s_chip.at[3 * k + i],
                        r_chip.at[3 * k + i], (dp, chips[k] * 2 + core),
                    )
                )

    def first():
        if ends:
            relay.start(0, 3)

    def between():
        if ends:
            relay.merged(up_far, up_far_in, pools[0], pools[4], pool_sem)
            relay.start(4)

    def second():
        if ends:
            relay.sent(0)
            relay.start(1)
            relay.landed(0)
            relay.merged(up_near, landed[0], pools[1], pools[4], pool_sem)
            relay.start(5)
            relay.landed(3)
            relay.merged(down_out, landed[3], pools[2], pools[5], pool_sem)
            relay.start(7)

    def third():
        if ends:
            relay.sent(1)
            relay.start(2)
            relay.landed(4)
            relay.merged(up_out, landed[4], pools[3], pools[4], pool_sem)
            relay.start(8)

    def fourth():
        if ends:
            relay.start(6)

    def experts(act, gpre, win, wdown):
        loads = [
            pltpu.make_async_copy(src, dst, load.at[i])
            for i, (src, dst) in enumerate(
                ((win_hbm, win), (gpre_hbm, gpre), (wdown_hbm, wdown), (act_hbm, act))
            )
        ]
        for one in loads:
            one.start()
        greet(
            [(dp, flip(me, k)) for k in range(1, groups)] + [(one, me) for one in rounds[1:]]
        )
        first()
        for one in loads[:2]:
            one.wait()
        for g in range(slots // CHUNK - 1, -1, -1):
            at = rows_at(flip(me // many, g) * CHUNK, CHUNK)

            @pl.loop(0, width // GROUP)
            def _(n):
                cols = rows_at(n * GROUP, GROUP)
                gv_send[at, cols] = dot_nt(gpre[at], win[cols]).astype(bf16)

            for k in range(g * many, (g + 1) * many):
                if k:
                    gv_copies[k - 1].start()
        gvr[mine] = gv_send[mine]
        for one in loads[2:]:
            one.wait()

        @pl.loop(0, width // GROUP)
        def _(n):
            cols = rows_at(n * GROUP, GROUP)
            y_send[:, cols] = dot(act[...], wdown[:, cols]).astype(bf16)

        between()

    pl.run_scoped(
        experts,
        pltpu.VMEM((slots, hidden), bf16), pltpu.VMEM((slots, hidden), bf16),
        pltpu.VMEM((width, hidden), bf16), pltpu.VMEM((hidden, width), bf16),
    )

    def dense_part(
        h1, cot, tok, att, inv, probs, qkv, wqkv, wout, place, gh1, low, gatt, inner_sum, gqkv,
        turned, gk, gvv, outv,
    ):
        loads = [
            pltpu.make_async_copy(src, dst, load.at[i])
            for i, (src, dst) in enumerate(
                (
                    (h1_hbm, h1), (cot_hbm, cot), (att_hbm, att), (wout_hbm, wout), (inv_hbm, inv),
                    (qkv_hbm, qkv), (probs_hbm, probs), (tok_hbm, tok), (wqkv_hbm, wqkv),
                )
            )
        ]
        for one in loads:
            one.start()
        spot = column_of(slot_row(te_ref[...], groups, cap))
        for r in range(rows // BAND):
            at = slice(r * BAND, (r + 1) * BAND)
            here = lax.broadcasted_iota(jnp.int32, (BAND, slots), 1).astype(f32)
            place[at] = jnp.where(here == spot[at], 1.0, 0.0).astype(bf16)
        gate = column_of(gate_ref[...])
        gains_ref[...] = jnp.zeros_like(gains_ref)
        for one in gv_copies:
            one.wait_recv()
        for one in y_copies:
            one.start()
        yr[mine] = y_send[mine]
        for i in range(2):
            loads[i].wait()

        @pl.loop(0, width // GROUP)
        def _(n):
            cols = rows_at(n * GROUP, GROUP)
            gh1[:, cols] = dot(place[...], gvr[:, cols])

        for r in range(rows // BAND):
            at = slice(r * BAND, (r + 1) * BAND)
            back = gh1[at]
            resid = h1[at]
            centre, inverse = centred(resid)
            unit = centre * inverse
            gains_ref[1:2] += jnp.sum(back * unit, axis=0, keepdims=True)
            slant = back * g2_ref[...].reshape(1, width)
            inner = slant - jnp.mean(slant, axis=-1, keepdims=True)
            inner = inner - unit * jnp.mean(slant * unit, axis=-1, keepdims=True)
            grad = cot[at].astype(f32) + inverse * inner
            gh1[at] = grad
            low[at] = grad.astype(bf16)
        for i in range(2, 5):
            loads[i].wait()

        @pl.loop(0, width // GROUP)
        def _(n):
            cols = rows_at(n * GROUP, GROUP)
            grad = dot_nt(low[...], wout[cols]) * inv[:, cols]
            gatt[:, cols] = grad.astype(bf16)
            inner_sum[:, cols] = grad * att[:, cols].astype(f32) * HEAD_DIM**-0.5

        turned[...] = att[...].T

        @pl.loop(0, width // GROUP)
        def _(n):
            cols = rows_at(n * GROUP, GROUP)
            dense[0:width, cols] = dot(turned[...], low[:, cols]).astype(bf16)

        pair_send(0)
        loads[7].wait()
        for r in range(rows // BAND):
            at = slice(r * BAND, (r + 1) * BAND)
            centre, inverse = centred(tok[at].astype(f32))
            low[at] = (centre * inverse * g1_ref[...].reshape(1, width)).astype(bf16)
        turned[...] = low[...].T
        second()
        loads[5].wait()
        loads[6].wait()
        left = lax.broadcasted_iota(jnp.int32, (1, PAIR), 1) < HEAD_DIM
        none = jnp.zeros((), bf16)

        def halves(block):
            return jnp.concatenate([jnp.where(left, block, none), jnp.where(left, none, block)], axis=0)

        def attend(h):
            at = rows_at(h * PAIR, PAIR)
            k_at = rows_at(width + h * PAIR, PAIR)
            v_at = rows_at(2 * width + h * PAIR, PAIR)
            gk[...] = jnp.zeros_like(gk)
            gvv[...] = jnp.zeros_like(gvv)
            for i in range(rows // BAND):
                first, wide = band(i)
                mine, seen = slice(i * BAND, (i + 1) * BAND), slice(first, first + wide)
                keys = qkv[seen, k_at]
                values = qkv[seen, v_at] * jnp.asarray(HEAD_DIM**-0.5, bf16)
                query, grad = halves(qkv[mine, at]), halves(gatt[mine, at])
                share = probs[h, 2 * i * BAND : 2 * (i + 1) * BAND, 0:wide]
                inner = inner_sum[mine, at]
                middle = jnp.concatenate(
                    [
                        jnp.sum(jnp.where(left, inner, 0.0), axis=-1, keepdims=True),
                        jnp.sum(jnp.where(left, 0.0, inner), axis=-1, keepdims=True),
                    ],
                    axis=0,
                )
                graw = (share.astype(f32) * (dot_nt(grad, values) - middle)).astype(bf16)
                gquery = dot(graw, keys)
                gqkv[mine, at] = jnp.where(left, gquery[0:BAND], gquery[BAND:]).astype(bf16)
                gk[seen] += dot_tn(graw, query)
                gvv[seen] += dot_tn(share, grad)
            gqkv[:, k_at] = gk[...].astype(bf16)
            gqkv[:, v_at] = gvv[...].astype(bf16)
        heads = width // PAIR // 2
        for part in range(2):
            pl.loop(part * heads, (part + 1) * heads)(attend)
            for i in range(3):
                source = i * width + part * heads * PAIR
                target = width + (3 * part + i) * heads * PAIR
                dense[0:width, target : target + heads * PAIR] = dot(
                    turned[...], gqkv[:, source : source + heads * PAIR]
                ).astype(bf16)
            pair_send(part + 1)
            combine(part)
        loads[8].wait()

        def rest():
            @pl.loop(0, width // GROUP)
            def _(n):
                cols = rows_at(n * GROUP, GROUP)
                inner_sum[:, cols] = dot_nt(gqkv[...], wqkv[cols])

            for r in range(rows // BAND):
                at = slice(r * BAND, (r + 1) * BAND)
                back = inner_sum[at]
                centre, inverse = centred(tok[at].astype(f32))
                unit = centre * inverse
                gains_ref[0:1] += jnp.sum(back * unit, axis=0, keepdims=True)
                slant = back * g1_ref[...].reshape(1, width)
                inner = slant - jnp.mean(slant, axis=-1, keepdims=True)
                inner = inner - unit * jnp.mean(slant * unit, axis=-1, keepdims=True)
                outv[at] = (gh1[at] + inverse * inner).astype(bf16)
            out_three = pltpu.make_async_copy(outv, gtok_out, store.at[0])
            out_three.start()
            for one in y_copies:
                one.wait_recv()

            @pl.loop(0, width // GROUP)
            def _(n):
                cols = rows_at(n * GROUP, GROUP)
                low[:, cols] = (h1[:, cols] + gate * dot(place[...], yr[:, cols])).astype(bf16)

            out_one = pltpu.make_async_copy(low, block_out, store.at[1])
            out_one.start()
            out_one.wait()
            out_three.wait()

        combine(2)
        rest()
        dense_sums()

    def dense_sums():
        gain_pair = go(send(gains_ref, gains_pair, s_gain.at[0], r_gain.at[0], (dp, there)))
        third()
        gain_pair.wait_recv()
        gains_part[0] = gains_ref[...] + gains_pair[...]
        gain_far = [
            go(
                send(
                    gains_part.at[0], gains_chip.at[k], s_gain.at[k], r_gain.at[k],
                    (dp, chips[k] * 2 + core),
                )
            )
            for k in range(1, half)
        ]
        total = other[rows_at(chip * per, per)].astype(f32)
        for k in range(1, half):
            for i in range(3):
                far[i, k].wait_recv()
            total = total + got[k].astype(f32)
        share = 3 * width // copies
        thin = width // copies
        part = width // 2
        thirds = jnp.concatenate(
            [
                total[:, width + (3 * j + i) * part : width + (3 * j + i + 1) * part]
                for i in range(3)
                for j in range(2)
            ],
            axis=1,
        )
        for d in range(copies):
            ring[d] = jnp.concatenate(
                [thirds[:, d * share : (d + 1) * share], total[:, d * thin : (d + 1) * thin]],
                axis=1,
            ).astype(bf16)
        around = [
            go(send(ring.at[rounds[k]], ring_got.at[k], s_ring.at[k], r_ring.at[k], (rounds[k], me)))
            for k in range(1, copies)
        ]
        fourth()
        gains = gains_part[0]
        for k in range(1, half):
            gain_far[k - 1].wait_recv()
            gains = gains + gains_chip[k]
        gains_part[1] = gains
        gain_around = [
            go(
                send(
                    gains_part.at[1], gains_ring.at[k], s_gain.at[half + k], r_gain.at[half + k],
                    (rounds[k], me),
                )
            )
            for k in range(1, copies)
        ]
        summed = ring[dp].astype(f32)
        for k in range(1, copies):
            around[k - 1].wait_recv()
            summed = summed + ring_got[k].astype(f32)
        place = rows_at((core * half + chip) * per, per)
        final[...] = summed.astype(bf16)
        whole[place] = final[...]
        spread = [
            go(send(final, whole.at[place], s_out.at[k], r_out.at[k], (dp, flip(me, k))))
            for k in range(groups - 1, 0, -1)
        ]
        for k in range(1, copies):
            gain_around[k - 1].wait_recv()
            gains = gains + gains_ring[k]
        total_ref[...] = gains
        for one in spread:
            one.wait_recv()
        last = pltpu.make_async_copy(whole, whole_out, store.at[2])
        last.start()
        last.wait()
        for one in started:
            one.wait_send()

    pl.run_scoped(
        dense_part,
        pltpu.VMEM((rows, width), f32), pltpu.VMEM((rows, width), bf16),
        pltpu.VMEM((rows, width), bf16), pltpu.VMEM((rows, width), bf16),
        pltpu.VMEM((rows, width), f32), pltpu.VMEM(probs_hbm.shape, bf16),
        pltpu.VMEM((rows, 3 * width), bf16), pltpu.VMEM((width, 3 * width), bf16),
        pltpu.VMEM((width, width), bf16), pltpu.VMEM((rows, slots), bf16),
        pltpu.VMEM((rows, width), f32), pltpu.VMEM((rows, width), bf16),
        pltpu.VMEM((rows, width), bf16), pltpu.VMEM((rows, width), f32),
        pltpu.VMEM((rows, 3 * width), bf16), pltpu.VMEM((width, rows), bf16),
        pltpu.VMEM((rows, PAIR), f32), pltpu.VMEM((rows, PAIR), f32),
        pltpu.VMEM((rows, width), bf16),
    )
    for one in gv_copies + y_copies:
        one.wait_send()
    if ends:
        for i in range(9):
            if i not in (0, 3, 4):
                relay.landed(i)
            if i > 1:
                relay.sent(i)


def backward(
    groups, cap, copies, ends, per, act, gpre, w_in, w_down, experts, gates, h1, cot, tok, g1, g2, att,
    inv, probs, qkv, w_qkv, w_out, parts,
):
    slots, hidden = act.shape
    rows, width = tok.shape
    wide = 4 * width
    half = groups // 2
    thin = wide // copies
    sems = pltpu.SemaphoreType.DMA
    block = pltpu.VMEM((slots, width), bf16)
    tile = (8, width)
    up = (width // 4, hidden)
    down = (hidden // 4, width)
    land = [up, down, up, down, up, up, down, down, up] if ends else []
    pools = [up, up, down, up] if ends else []
    return pl.pallas_call(
        functools.partial(backward_kernel, groups, cap, copies, ends),
        out_shape=[
            jax.ShapeDtypeStruct((rows, width), bf16), jax.ShapeDtypeStruct((rows, width), bf16),
            jax.ShapeDtypeStruct((groups * per, thin), bf16), jax.ShapeDtypeStruct(tile, f32),
        ]
        + [jax.ShapeDtypeStruct(one, bf16) for one in land],
        in_specs=[ANY] * 4 + [VMEM] * 2 + [ANY] * 3 + [VMEM] * 2 + [ANY] * (6 + len(parts)),
        out_specs=[ANY] * 3 + [VMEM] + [ANY] * len(land),
        scratch_shapes=[
            block, block, block, block,
            pltpu.VMEM((groups * per, wide), bf16), pltpu.VMEM((half * per, wide), bf16),
            pltpu.VMEM((half, per, wide), bf16), pltpu.VMEM((copies, per, thin), bf16),
            pltpu.VMEM((copies, per, thin), bf16), pltpu.VMEM((per, thin), bf16),
            pltpu.VMEM((groups * per, thin), bf16), pltpu.VMEM(tile, f32), pltpu.VMEM(tile, f32),
            pltpu.VMEM((half, *tile), f32), pltpu.VMEM((2, *tile), f32),
            pltpu.VMEM((copies, *tile), f32), sems((9,)), sems((3,)), sems((groups,)),
            sems((groups,)), sems((groups,)), sems((groups,)), sems((3,)), sems((3,)),
            sems((3 * half,)), sems((3 * half,)), sems((copies,)), sems((copies,)), sems((groups,)),
            sems((groups,)), sems((half + copies,)), sems((half + copies,)), sems((9,)), sems((9,)),
            sems((2,)),
        ]
        + [pltpu.VMEM(one, bf16) for one in pools]
        + [pltpu.VMEM(one, bf16) for one in (up, down) if ends],
        compiler_params=pltpu.CompilerParams(
            collective_id=1, has_side_effects=True, vmem_limit_bytes=60 * MIB
        ),
        cost_estimate=pl.CostEstimate(
            flops=200 * 10**9, bytes_accessed=40 * 10**6, transcendentals=0
        ),
        name="backward",
    )(
        act, gpre, w_in, w_down, experts, gates, h1, cot, tok, g1, g2, att, inv, probs, qkv, w_qkv,
        w_out, *parts,
    )


def finish_kernel(*refs):
    (
        up_own, up_in, up_across, up_out, up_outward, down_own, down_in, down_across, down_out,
        down_outward, block, gtok, whole_ref, gains_ref, up_ref, down_ref, qkv_hbm, out_hbm, one_ref,
        two_ref, block_ref, gtok_ref, a, b, c, d, e, f, up, down, qkv_ref, out_ref,
        block_line, gtok_line, load, store,
    ) = refs
    dp = lax.axis_index("dp")
    outer = (dp == 0) | (dp == 3)
    inner = jnp.logical_not(outer)
    hand_in = [
        pltpu.make_async_copy(block, block_line, load.at[6]),
        pltpu.make_async_copy(gtok, gtok_line, load.at[7]),
    ]
    handed = [
        pltpu.make_async_copy(block_line, block_ref, store.at[0]),
        pltpu.make_async_copy(gtok_line, gtok_ref, store.at[1]),
    ]

    def loads(sources, targets):
        return [
            pltpu.make_async_copy(src, dst, load.at[i])
            for i, (src, dst) in enumerate(zip(sources, targets))
        ]

    inside = loads((up_own, up_in, up_across, down_own, down_in, down_across), (a, b, c, d, e, f))
    outside = loads((up_out, up_outward, down_out, down_outward), (a, b, d, e))

    @pl.when(inner)
    def _():
        for one in inside:
            one.start()

    @pl.when(outer)
    def _():
        for one in outside:
            one.start()

    for one in hand_in:
        one.start()
    thin = qkv_ref.shape[0]
    turned = whole_ref[...].astype(f32).T
    qkv_ref[...] = turned[:thin]
    out_ref[...] = turned[thin:]
    handed += [
        pltpu.make_async_copy(qkv_ref, qkv_hbm, store.at[4]),
        pltpu.make_async_copy(out_ref, out_hbm, store.at[5]),
    ]
    for one in hand_in:
        one.wait()
    for one in handed:
        one.start()
    size = one_ref.shape[1]
    for row, target in ((0, one_ref), (1, two_ref)):
        line = jnp.zeros((1, size), f32)
        for plane in range(4):
            part = gains_ref[row : row + 1, plane * size : (plane + 1) * size]
            line = jnp.where(dp == plane, part, line)
        target[...] = line

    def summed(target, terms):
        lines = target.shape[0] // 12

        @pl.loop(0, 12)
        def _(r):
            at = rows_at(r * lines, lines)
            total = terms[0][at].astype(f32)
            for term in terms[1:]:
                total = total + term[at].astype(f32)
            target[at] = total

    up_store = pltpu.make_async_copy(up, up_ref, store.at[2])
    down_store = pltpu.make_async_copy(down, down_ref, store.at[3])

    @pl.when(inner)
    def _():
        for one in inside[:3]:
            one.wait()
        summed(up, (a, b, c))
        up_store.start()
        for one in inside[3:]:
            one.wait()
        summed(down, (d, e, f))

    @pl.when(outer)
    def _():
        for one in outside[:2]:
            one.wait()
        summed(up, (a, b))
        up_store.start()
        for one in outside[2:]:
            one.wait()
        summed(down, (d, e))

    down_store.start()
    for one in handed:
        one.wait()
    up_store.wait()
    down_store.wait()


def finish(ups, downs, block, gtok, whole, gains):
    up, down = ups[0].shape, downs[0].shape
    width = whole.shape[1]
    thin = width // 4
    sems = pltpu.SemaphoreType.DMA
    return pl.pallas_call(
        finish_kernel,
        out_shape=[
            jax.ShapeDtypeStruct(up, f32), jax.ShapeDtypeStruct(down, f32),
            jax.ShapeDtypeStruct((3 * thin, whole.shape[0]), f32),
            jax.ShapeDtypeStruct((thin, whole.shape[0]), f32),
            jax.ShapeDtypeStruct((1, thin), f32), jax.ShapeDtypeStruct((1, thin), f32),
            jax.ShapeDtypeStruct(block.shape, bf16), jax.ShapeDtypeStruct(gtok.shape, bf16),
        ],
        in_specs=[ANY] * 12 + [VMEM] * 2,
        out_specs=[ANY] * 4 + [VMEM] * 2 + [ANY] * 2,
        scratch_shapes=[pltpu.VMEM(up, bf16)] * 3
        + [pltpu.VMEM(down, bf16)] * 3
        + [
            pltpu.VMEM(up, f32), pltpu.VMEM(down, f32), pltpu.VMEM((3 * thin, whole.shape[0]), f32),
            pltpu.VMEM((thin, whole.shape[0]), f32), pltpu.VMEM(block.shape, bf16),
            pltpu.VMEM(gtok.shape, bf16), sems((8,)), sems((6,)),
        ],
        compiler_params=pltpu.CompilerParams(vmem_limit_bytes=60 * MIB),
        name="finish",
    )(*ups, *downs, block, gtok, whole, gains)


def shards(
    tokens, segment_ids, token_expert, gates, ln1_gain, w_qkv, w_out, ln2_gain, expert_in,
    expert_out, cotangent,
):
    rows, width = tokens.shape
    groups, copies = lax.axis_size("expert"), lax.axis_size("dp")
    cap = 2 * rows // groups
    per = -(-width // (16 * groups)) * 16
    w_in, w_down = expert_in[0], expert_out[0]
    experts, gate_row = token_expert.reshape(1, rows), gates.reshape(1, rows)
    ends = copies == 4
    h1, qkv, att, inv, probs, act, gpre, *parts = forward(
        groups, cap, ends, tokens, segment_ids, experts, gate_row, ln1_gain, w_qkv, w_out,
        ln2_gain, w_in, w_down, cotangent,
    )
    if ends:
        up_far, up_near, up_out, up_own, down_far, down_near, down_out, down_own, up_far_in = parts
        parts = [up_far, up_near, up_out, up_own, up_far_in, down_far, down_near, down_out, down_own]
    block_out, grad_tokens, whole, gains, *landed = backward(
        groups, cap, copies, ends, per, act, gpre, w_in, w_down, experts, gate_row, h1, cotangent,
        tokens, ln1_gain, ln2_gain, att, inv, probs, qkv, w_qkv, w_out, parts if ends else [],
    )
    if ends:
        _, down_own_in, up_own_in, _, _, up_across, down_across, down_outward, up_outward = landed
        up_share, down_share, share_qkv, share_out, share_one, share_two, block, gtok = finish(
            (up_own, up_own_in, up_across, up_out, up_outward),
            (down_own, down_own_in, down_across, down_out, down_outward),
            block_out, grad_tokens, whole[:width], gains,
        )
        return (
            block, gtok, share_one[0], share_qkv.T, share_out.T, share_two[0], up_share[None],
            down_share[None],
        )
    up_share, down_share = (
        lax.psum_scatter(one[None], "dp", scatter_dimension=1, tiled=True) for one in parts
    )
    whole = whole[:width].astype(f32)
    share = width // copies
    gains = lax.dynamic_slice_in_dim(gains, lax.axis_index("dp") * share, share, 1)
    return (
        block_out,
        grad_tokens,
        gains[0],
        whole[:, : 3 * share],
        whole[:, 3 * share :],
        gains[1],
        up_share.astype(f32),
        down_share.astype(f32),
    )


def solution(mesh):
    tokens, experts = P(("dp", "expert"), None), P("expert", None, None)
    return jax.shard_map(
        shards,
        mesh=mesh,
        in_specs=(
            tokens, tokens, tokens, P(("dp", "expert")), P(), P(), P(), P(), experts, experts,
            tokens,
        ),
        out_specs=(
            tokens, tokens, P("dp"), P(None, "dp"), P(None, "dp"), P("dp"),
            P("expert", "dp", None), P("expert", "dp", None),
        ),
        check_vma=False,
    )
```

```python
import functools

import jax
import jax.numpy as jnp
from jax import lax
from jax.experimental import pallas as pl
from jax.experimental.pallas import tpu as pltpu
from jax.sharding import PartitionSpec as P

HEAD_DIM = 64
EPSILON = 1e-05
NEG_LARGE = -1e30
BAND = 128
PAIR = 2 * HEAD_DIM
GROUP = 256
CHUNK = 512
MIB = 2**20
MESH = pl.DeviceIdType.MESH
ANY = pl.BlockSpec(memory_space=pl.ANY)
VMEM = pl.BlockSpec(memory_space=pltpu.VMEM)
f32, bf16 = jnp.float32, jnp.bfloat16


def dot(a, b):
    return jnp.dot(a, b, preferred_element_type=f32)


def dot_nt(a, b):
    return lax.dot_general(a, b, (((1,), (1,)), ((), ())), preferred_element_type=f32)


def dot_tn(a, b):
    return lax.dot_general(a, b, (((0,), (0,)), ((), ())), preferred_element_type=f32)


def flip(index, bits):
    place = 1
    while bits:
        if bits % 2:
            index = index + place * (1 - 2 * ((index // place) % 2))
        bits, place = bits // 2, place * 2
    return index


def add(a, b):
    return (a.astype(f32) + b.astype(f32)).astype(bf16)


def rows_at(start, size):
    return pl.ds(pl.multiple_of(start, size), size)


def greet(peers):
    barrier = pltpu.get_barrier_semaphore()
    for peer in peers:
        pl.semaphore_signal(barrier, inc=1, device_id=peer, device_id_type=MESH)
    pl.semaphore_wait(barrier, len(peers))


def sides(dp):
    side = dp // 2
    return flip(dp, 1), 3 - dp, [3 * (1 - side), 2 - side, 3 * side, 1 + side]


class Relay:
    def __init__(self, dp, me, moves, ssem, rsem):
        self.outer = (dp == 0) | (dp == 3)
        self.inner = jnp.logical_not(self.outer)
        beside, across, _ = sides(dp)
        self.moves = []
        for i, (kind, source, target) in enumerate(moves):
            plane = across if kind == "across" else beside
            copy = pltpu.make_async_remote_copy(
                src_ref=source, dst_ref=target, send_sem=ssem.at[i], recv_sem=rsem.at[i],
                device_id=(plane, me), device_id_type=MESH,
            )
            sender = self.outer if kind == "inward" else self.inner
            receiver = self.outer if kind == "outward" else self.inner
            self.moves.append((copy, sender, receiver))

    def start(self, *which):
        for i in which:
            copy, sender, _ = self.moves[i]
            pl.when(sender)(copy.start)

    def sent(self, i):
        pl.when(self.moves[i][1])(self.moves[i][0].wait_send)

    def landed(self, i):
        pl.when(self.moves[i][2])(self.moves[i][0].wait_recv)

    def merged(self, first, second, total, spare, sem):
        @pl.when(self.inner)
        def _():
            loads = [
                pltpu.make_async_copy(first, total, sem.at[0]),
                pltpu.make_async_copy(second, spare, sem.at[1]),
            ]
            for one in loads:
                one.start()
            for one in loads:
                one.wait()
            lines = total.shape[0] // 12

            @pl.loop(0, 12)
            def _(r):
                at = rows_at(r * lines, lines)
                total[at] = add(total[at], spare[at])


def band(index):
    first = max(0, index - 2) * BAND
    return first, (index + 1) * BAND - first


def column_of(row):
    size = row.shape[1]
    eye = lax.broadcasted_iota(jnp.int32, (size, size), 0) == lax.broadcasted_iota(
        jnp.int32, (size, size), 1
    )
    return jnp.sum(jnp.where(eye, row, 0.0), axis=1, keepdims=True)


def slot_row(experts, num_experts, capacity):
    rows = experts.shape[1]
    lines = max(16, num_experts)
    onehot = lax.broadcasted_iota(jnp.int32, (lines, rows), 0) == experts
    onehot = jnp.where(onehot, 1.0, 0.0)
    before = lax.broadcasted_iota(jnp.int32, (rows, rows), 0) < lax.broadcasted_iota(
        jnp.int32, (rows, rows), 1
    )
    earlier = dot(onehot.astype(bf16), jnp.where(before, 1.0, 0.0).astype(bf16))
    rank = jnp.sum(onehot * earlier, axis=0, keepdims=True)
    return experts.astype(f32) * float(capacity) + rank


def centred(hidden):
    centre = hidden - jnp.mean(hidden, axis=-1, keepdims=True)
    spread = jnp.mean(centre * centre, axis=-1, keepdims=True)
    return centre, lax.rsqrt(spread + EPSILON)


def gelu_pair(x):
    bell = jnp.exp2((-0.5 * 1.4426950408889634) * (x * x))
    phi = 0.5 + 0.5 * lax.erf(x * 0.7071067811865476)
    return x * phi, phi + x * (bell * 0.3989422804014327)


def gelu(x):
    return gelu_pair(x)[0]


def forward_kernel(groups, cap, ends, *refs):
    (
        tok_hbm, seg_ref, te_ref, gate_ref, g1_ref, wqkv_hbm, wout_hbm, g2_ref, win_hbm, wdown_hbm,
        cot_hbm, h1_out, qkv_out, att_out, inv_out, probs_out, act_out, gpre_out,
    ) = refs[:18]
    count = 4 if ends else 1
    ups, downs = refs[18 : 18 + count], refs[18 + count : 18 + 2 * count]
    up_land = refs[18 + 2 * count : 18 + 2 * count + ends]
    (
        tok, cot, win, wdown, low, h1, place, sent, gy_send, gy_got, v_got, gy_low, spot_own, gy_line,
        v_line, spot_far, place_far, gy_fsend, far_send, gy_far, v_far, act,
        gpre, load, store, act_store, gpre_store, gy_ssem, gy_rsem, v_ssem, v_rsem, gy_fssem,
        gy_frsem, v_fssem, v_frsem, line_ssem, line_rsem, rel_s, rel_r,
    ) = refs[18 + 2 * count + ends :]
    dp, me = lax.axis_index("dp"), lax.axis_index("expert")
    rows, width = tok.shape
    slots, hidden = act.shape
    pairs = width // PAIR
    outer = (dp == 0) | (dp == 3)
    inner = jnp.logical_not(outer)
    first_loads = [
        pltpu.make_async_copy(src, dst, load.at[i])
        for i, (src, dst) in enumerate(
            ((cot_hbm, cot), (tok_hbm, tok), (win_hbm, win), (wdown_hbm, wdown))
        )
    ]
    first_loads[0].start()
    first_loads[1].start()
    beside = [(flip(dp, 1), me)] if ends else []
    greet([(dp, flip(me, k)) for k in range(1, groups)] + beside)

    def exchange(source, target, send, receive, k):
        peer = flip(me, k)
        return pltpu.make_async_remote_copy(
            src_ref=source.at[rows_at(peer * cap, cap)],
            dst_ref=target.at[rows_at(me * cap, cap)],
            send_sem=send.at[k],
            recv_sem=receive.at[k],
            device_id=(dp, peer),
            device_id_type=MESH,
        )

    gy_copies = [exchange(gy_send, gy_got, gy_ssem, gy_rsem, k) for k in range(1, groups)]
    v_copies = [exchange(sent, v_got, v_ssem, v_rsem, k) for k in range(1, groups)]
    far_groups = groups if ends else 0
    gy_fars = [exchange(gy_fsend, gy_far, gy_fssem, gy_frsem, k) for k in range(1, far_groups)]
    v_fars = [exchange(far_send, v_far, v_fssem, v_frsem, k) for k in range(1, far_groups)]
    lines = ends and [
        pltpu.make_async_remote_copy(
            src_ref=source, dst_ref=target, send_sem=line_ssem.at[i], recv_sem=line_rsem.at[i],
            device_id=(flip(dp, 1), me), device_id_type=MESH,
        )
        for i, (source, target) in enumerate(
            ((spot_own, spot_far), (gy_low, gy_line), (low, v_line))
        )
    ]

    def when(condition, action):
        if ends:
            pl.when(condition)(action)

    def positions(spot, target):
        @pl.loop(0, slots // GROUP)
        def _(g):
            here = lax.broadcasted_iota(jnp.int32, (GROUP, rows), 0) + g * GROUP
            there = jnp.where(here.astype(f32) == spot, 1.0, 0.0)
            target[rows_at(g * GROUP, GROUP)] = there.astype(bf16)

    def placed(where, line, target):
        @pl.loop(0, width // GROUP)
        def _(n):
            cols = rows_at(n * GROUP, GROUP)
            target[:, cols] = dot(where[...], line[:, cols]).astype(bf16)

    def far_gy():
        lines[0].wait_recv()
        lines[1].wait_recv()
        positions(spot_far[0:1], place_far)
        placed(place_far, gy_line, gy_fsend)
        for one in gy_fars:
            one.start()
        gy_far[mine] = gy_fsend[mine]

    def far_v():
        lines[2].wait_recv()
        placed(place_far, v_line, far_send)
        for one in v_fars:
            one.start()
        v_far[mine] = far_send[mine]

    mine = rows_at(me * cap, cap)

    def attention(wqkv, wout, qkv, att, inv, probs, bias):
        loads = [
            pltpu.make_async_copy(wqkv_hbm, wqkv, load.at[4]),
            pltpu.make_async_copy(wout_hbm, wout, load.at[5]),
        ]
        for one in loads + first_loads[2:]:
            one.start()
        spot = slot_row(te_ref[...], groups, cap)

        positions(spot, place)
        first_loads[0].wait()
        gate = column_of(gate_ref[...])
        gy_low[...] = (gate * cot[...].astype(f32)).astype(bf16)
        if ends:
            spot_own[...] = jnp.broadcast_to(spot, spot_own.shape)

            @pl.when(outer)
            def _():
                lines[0].start()
                lines[1].start()

        placed(place, gy_low, gy_send)
        for one in gy_copies:
            one.start()
        gy_got[mine] = gy_send[mine]
        segs = seg_ref[...].astype(f32)
        seg_col = column_of(segs)
        for i in range(rows // BAND):
            first, wide = band(i)
            causal = (lax.broadcasted_iota(jnp.int32, (BAND, wide), 0) + i * BAND) >= (
                lax.broadcasted_iota(jnp.int32, (BAND, wide), 1) + first
            )
            same = seg_col[i * BAND : (i + 1) * BAND] == segs[:, first : first + wide]
            bias[i * BAND : (i + 1) * BAND, 0:wide] = jnp.where(causal & same, 0.0, NEG_LARGE)

        first_loads[1].wait()

        @pl.loop(0, rows // BAND)
        def _(r):
            at = rows_at(r * BAND, BAND)
            centre, inverse = centred(tok[at].astype(f32))
            low[at] = (centre * inverse * g1_ref[...].reshape(1, width)).astype(bf16)

        loads[0].wait()

        @pl.loop(0, 3 * width // GROUP)
        def _(c):
            at = rows_at(c * GROUP, GROUP)
            qkv[:, at] = dot(low[...], wqkv[:, at]).astype(bf16)

        left = lax.broadcasted_iota(jnp.int32, (1, PAIR), 1) < HEAD_DIM
        none, unit = jnp.zeros((), bf16), jnp.ones((), bf16)

        def attend(h):
            at = rows_at(h * PAIR, PAIR)
            k_at = rows_at(width + h * PAIR, PAIR)
            v_at = rows_at(2 * width + h * PAIR, PAIR)
            for i in range(rows // BAND):
                first, wide = band(i)
                here = slice(i * BAND, (i + 1) * BAND)
                keys = qkv[first : first + wide, k_at]
                values = qkv[first : first + wide, v_at]
                query = qkv[here, at] * jnp.asarray(HEAD_DIM**-0.5, bf16)
                query = jnp.concatenate(
                    [jnp.where(left, query, none), jnp.where(left, none, query)], axis=0
                )
                scores = dot_nt(query, keys).reshape(2, BAND, wide) + bias[here, 0:wide][None]
                weights = jnp.exp(scores - jnp.max(scores, axis=-1, keepdims=True)).astype(bf16)
                probs[h, 2 * i * BAND : 2 * (i + 1) * BAND, 0:wide] = weights.reshape(
                    2 * BAND, wide
                )
                one = dot(weights[0], jnp.where(left, values, unit))
                two = dot(weights[1], jnp.where(left, unit, values))
                scale = 1.0 / pltpu.roll(jnp.where(left, two, one), HEAD_DIM, 1)
                inv[here, at] = scale
                att[here, at] = (jnp.where(left, one, two) * scale).astype(bf16)

        pl.loop(0, pairs)(attend)
        stores = [
            pltpu.make_async_copy(src, dst, store.at[i])
            for i, (src, dst) in enumerate(
                ((qkv, qkv_out), (probs, probs_out), (att, att_out), (inv, inv_out))
            )
        ]
        for one in stores:
            one.start()
        loads[1].wait()

        @pl.loop(0, width // GROUP)
        def _(n):
            cols = rows_at(n * GROUP, GROUP)
            h1[:, cols] = dot(att[...], wout[:, cols])

        @pl.loop(0, rows // BAND)
        def _(r):
            at = rows_at(r * BAND, BAND)
            resid = tok[at].astype(f32) + h1[at]
            h1[at] = resid
            centre, inverse = centred(resid)
            low[at] = (centre * inverse * g2_ref[...].reshape(1, width)).astype(bf16)

        when(outer, lambda: lines[2].start())

        placed(place, low, sent)
        for one in v_copies:
            one.start()
        v_got[mine] = sent[mine]
        when(inner, far_gy)
        for one in stores:
            one.wait()

    pl.run_scoped(
        attention,
        pltpu.VMEM((width, 3 * width), bf16), pltpu.VMEM((width, width), bf16),
        pltpu.VMEM((rows, 3 * width), bf16), pltpu.VMEM((rows, width), bf16),
        pltpu.VMEM((rows, width), f32), pltpu.VMEM((pairs, 2 * rows, 3 * BAND), bf16),
        pltpu.VMEM((rows, 3 * BAND), f32),
    )

    def experts(act_far, gdown, gup, turned):
        stores = [pltpu.make_async_copy(h1, h1_out, store.at[4])]
        stores[0].start()
        for one in first_loads[2:]:
            one.wait()
        for one in gy_copies:
            one.wait_recv()

        @pl.loop(0, hidden // GROUP)
        def _(c):
            at = rows_at(c * GROUP, GROUP)
            gpre[:, at] = dot_nt(gy_got[...], wdown[at]).astype(bf16)

        many = GROUP // cap
        for g in range(slots // GROUP):
            for k in range(g * many, (g + 1) * many):
                if k:
                    v_copies[k - 1].wait_recv()
            at = rows_at(flip(me // many, g) * GROUP, GROUP)

            @pl.loop(0, hidden // CHUNK)
            def _(c):
                cols = rows_at(c * CHUNK, CHUNK)
                value, back = gelu_pair(dot(v_got[at], win[:, cols]))
                act[at, cols] = value.astype(bf16)
                gpre[at, cols] = (gpre[at, cols].astype(f32) * back).astype(bf16)

            for source, target, sem in ((act, act_out, act_store), (gpre, gpre_out, gpre_store)):
                stores.append(pltpu.make_async_copy(source.at[at], target.at[at], sem.at[g]))
                stores[-1].start()
            if g == 1:
                when(inner, far_v)

        turned[...] = v_got[...].T

        @pl.loop(0, hidden // GROUP)
        def _(c):
            cols = rows_at(c * GROUP, GROUP)
            gup[:, cols] = dot(turned[...], gpre[:, cols]).astype(bf16)

        shares = sides(dp)[2] if ends else [0]
        size, share = width // count, hidden // count
        for i, (one, part) in enumerate(zip(shares, ups)):
            source = gup.at[rows_at(one * size, size)]
            stores.append(pltpu.make_async_copy(source, part, store.at[5 + i]))
            stores[-1].start()
        if ends:
            relay = Relay(
                dp, me, [("inward", gup.at[rows_at(shares[0] * size, size)], up_land[0])],
                rel_s, rel_r,
            )
            relay.start(0)

        def down(kept, shared):
            for i in kept:

                @pl.loop(0, share // GROUP)
                def _(c):
                    cols = pl.ds(pl.multiple_of(shares[i] * share + c * GROUP, GROUP), GROUP)
                    at = pl.ds(pl.multiple_of(i * share + c * GROUP, GROUP), GROUP)
                    total = dot_tn(act[:, cols], gy_got[...])
                    if shared:
                        total = total + dot_tn(act_far[:, at], gy_far[...])
                    gdown[at] = total.astype(bf16)

            for i in kept:
                at = slice(i * share, (i + 1) * share)
                pltpu.make_async_copy(gdown.at[at], downs[i], store.at[9 + i]).start()

        def taken(kept):
            for i in kept:
                at = slice(i * share, (i + 1) * share)
                pltpu.make_async_copy(gdown.at[at], downs[i], store.at[9 + i]).wait()

        def inside():
            for g in range(slots // GROUP):
                for k in range(g * many, (g + 1) * many):
                    if k:
                        v_fars[k - 1].wait_recv()
                at = rows_at(flip(me // many, g) * GROUP, GROUP)
                for i in range(2):

                    @pl.loop(0, 2)
                    def _(c):
                        cols = pl.ds(pl.multiple_of(shares[i] * share + c * (share // 2), 128), share // 2)
                        kept = pl.ds(pl.multiple_of(i * share + c * (share // 2), 128), share // 2)
                        act_far[at, kept] = gelu(dot(v_far[at], win[:, cols])).astype(bf16)

            for one in gy_fars:
                one.wait_recv()
            down([0, 1], True)
            for one in gy_fars + v_fars:
                one.wait_send()
            taken([0, 1])

        down([2, 3] if ends else [0], False)
        if ends:
            pl.when(inner)(inside)

            @pl.when(outer)
            def _():
                for one in lines:
                    one.wait_send()

        taken([2, 3] if ends else [0])
        for one in gy_copies + v_copies:
            one.wait_send()
        for one in stores:
            one.wait()
        if ends:
            relay.landed(0)
            relay.sent(0)

    pl.run_scoped(
        experts,
        pltpu.VMEM((slots, hidden // 2) if ends else (16, 128), bf16),
        pltpu.VMEM((hidden, width), bf16), pltpu.VMEM((width, hidden), bf16),
        pltpu.VMEM((width, slots), bf16),
    )


def forward(groups, cap, ends, tokens, segs, experts, gates, g1, w_qkv, w_out, g2, w_in, w_down, cot):
    rows, width = tokens.shape
    hidden = w_in.shape[1]
    slots = groups * cap
    pairs = width // PAIR
    wide = 3 * BAND
    count = 4 if ends else 1
    parts = [(width // count, hidden)] * count + [(hidden // count, width)] * count
    parts += [(width // count, hidden)] * ends
    shapes = [
        ((rows, width), f32), ((rows, 3 * width), bf16), ((rows, width), bf16), ((rows, width), f32),
        ((pairs, 2 * rows, wide), bf16), ((slots, hidden), bf16), ((slots, hidden), bf16),
    ] + [(one, bf16) for one in parts]
    sems = pltpu.SemaphoreType.DMA
    lines = pltpu.VMEM((rows, width), bf16)
    block = pltpu.VMEM((slots, width), bf16)
    tiny = (16, 128)
    far = block if ends else pltpu.VMEM(tiny, bf16)
    far_line = lines if ends else pltpu.VMEM(tiny, bf16)
    return pl.pallas_call(
        functools.partial(forward_kernel, groups, cap, int(ends)),
        out_shape=[jax.ShapeDtypeStruct(*one) for one in shapes],
        in_specs=[ANY, VMEM, VMEM, VMEM, VMEM, ANY, ANY, VMEM, ANY, ANY, ANY],
        out_specs=[ANY] * len(shapes),
        scratch_shapes=[
            lines, lines, pltpu.VMEM(w_in.shape, bf16), pltpu.VMEM(w_down.shape, bf16), lines,
            pltpu.VMEM((rows, width), f32), pltpu.VMEM((slots, rows), bf16), block, block, block,
            block, lines, pltpu.VMEM((8, rows), f32), far_line, far_line, pltpu.VMEM((8, rows), f32),
            pltpu.VMEM((slots, rows) if ends else tiny, bf16), far, far, far, far,
            pltpu.VMEM((slots, hidden), bf16), pltpu.VMEM((slots, hidden), bf16),
            sems((6,)), sems((13,)), sems((slots // GROUP,)), sems((slots // GROUP,)),
        ]
        + [sems((groups,))] * 8
        + [sems((3,))] * 2
        + [sems((1,))] * 2,
        compiler_params=pltpu.CompilerParams(
            collective_id=0, has_side_effects=True, vmem_limit_bytes=60 * MIB
        ),
        cost_estimate=pl.CostEstimate(
            flops=200 * 10**9, bytes_accessed=40 * 10**6, transcendentals=10**7
        ),
        name="forward",
    )(tokens, segs, experts, gates, g1, w_qkv, w_out, g2, w_in, w_down, cot)


def backward_kernel(groups, cap, copies, ends, *refs):
    (
        act_hbm, gpre_hbm, win_hbm, wdown_hbm, te_ref, gate_ref, h1_hbm, cot_hbm, tok_hbm, g1_ref,
        g2_ref, att_hbm, inv_hbm, probs_hbm, qkv_hbm, wqkv_hbm, wout_hbm,
    ) = refs[:17]
    parts, refs = refs[17 : 17 + 9 * ends], refs[17 + 9 * ends :]
    block_out, gtok_out, whole_out, total_ref = refs[:4]
    landed, refs = refs[4 : 4 + 9 * ends], refs[4 + 9 * ends :]
    (
        gv_send, gvr, y_send, yr, dense, other, got, ring, ring_got, final, whole, gains_ref,
        gains_pair, gains_chip, gains_part, gains_ring, load, store, gv_ssem, gv_rsem, y_ssem, y_rsem,
        s_pair, r_pair, s_chip, r_chip, s_ring, r_ring, s_out, r_out, s_gain, r_gain, rel_s, rel_r,
        pool_sem, *pools,
    ) = refs
    dp, me = lax.axis_index("dp"), lax.axis_index("expert")
    slots, width = gvr.shape
    rows, hidden = tok_hbm.shape[0], win_hbm.shape[1]
    rounds = [lax.rem(dp + k, copies) for k in range(copies)]
    half = groups // 2
    per, wide = got.shape[1:]
    many = CHUNK // cap
    mine = rows_at(me * cap, cap)

    def exchange(source, target, ssem, rsem):
        return [
            pltpu.make_async_remote_copy(
                src_ref=source.at[rows_at(flip(me, k) * cap, cap)],
                dst_ref=target.at[rows_at(me * cap, cap)],
                send_sem=ssem.at[k],
                recv_sem=rsem.at[k],
                device_id=(dp, flip(me, k)),
                device_id_type=MESH,
            )
            for k in range(1, groups)
        ]

    gv_copies = exchange(gv_send, gvr, gv_ssem, gv_rsem)
    y_copies = exchange(y_send, yr, y_ssem, y_rsem)
    relay = None
    if ends:
        up_far, up_near, up_out, up_own, up_far_in, down_far, down_near, down_out, down_own = parts
        relay = Relay(
            dp, me,
            [
                ("inward", up_near, landed[0]), ("inward", down_own, landed[1]),
                ("inward", up_own, landed[2]), ("across", down_far, landed[3]),
                ("across", pools[0], landed[4]), ("across", pools[1], landed[5]),
                ("across", down_near, landed[6]), ("outward", pools[2], landed[7]),
                ("outward", pools[3], landed[8]),
            ],
            rel_s, rel_r,
        )

    chip, core = me // 2, me % 2
    there = flip(me, 1)
    chips = [flip(chip, k) for k in range(half)]
    started = []
    sets = [(0, width), (width, 3 * width // 2), (5 * width // 2, 3 * width // 2)]
    pair, far = {}, {}

    def send(source, target, ssem, rsem, device):
        return pltpu.make_async_remote_copy(
            src_ref=source, dst_ref=target, send_sem=ssem, recv_sem=rsem, device_id=device,
            device_id_type=MESH,
        )

    def go(copy):
        copy.start()
        started.append(copy)
        return copy

    def pair_send(i):
        cols = slice(sets[i][0], sum(sets[i]))
        pair[i] = go(
            send(
                dense.at[rows_at((1 - core) * (half * per), half * per), cols], other.at[:, cols],
                s_pair.at[i], r_pair.at[i], (dp, there),
            )
        )

    def combine(i):
        cols = slice(sets[i][0], sum(sets[i]))
        pair[i].wait_recv()
        for k in range(half - 1, -1, -1):
            at = rows_at(chips[k] * per, per)
            own = rows_at((core * half + chips[k]) * per, per)
            other[at, cols] = add(dense[own, cols], other[at, cols])
            if k:
                far[i, k] = go(
                    send(
                        other.at[at, cols], got.at[k, :, cols], s_chip.at[3 * k + i],
                        r_chip.at[3 * k + i], (dp, chips[k] * 2 + core),
                    )
                )

    def first():
        if ends:
            relay.start(0, 3)

    def between():
        if ends:
            relay.merged(up_far, up_far_in, pools[0], pools[4], pool_sem)
            relay.start(4)

    def second():
        if ends:
            relay.sent(0)
            relay.start(1)
            relay.landed(0)
            relay.merged(up_near, landed[0], pools[1], pools[4], pool_sem)
            relay.start(5)
            relay.landed(3)
            relay.merged(down_out, landed[3], pools[2], pools[5], pool_sem)
            relay.start(7)

    def third():
        if ends:
            relay.sent(1)
            relay.start(2)

    def outward():
        if ends:
            relay.landed(4)
            relay.merged(up_out, landed[4], pools[3], pools[4], pool_sem)
            relay.start(8)

    def fourth():
        if ends:
            relay.start(6)

    def experts(act, gpre, win, wdown):
        loads = [
            pltpu.make_async_copy(src, dst, load.at[i])
            for i, (src, dst) in enumerate(
                ((win_hbm, win), (gpre_hbm, gpre), (wdown_hbm, wdown), (act_hbm, act))
            )
        ]
        for one in loads:
            one.start()
        greet(
            [(dp, flip(me, k)) for k in range(1, groups)] + [(one, me) for one in rounds[1:]]
        )
        first()
        for one in loads[:2]:
            one.wait()
        for g in range(slots // CHUNK - 1, -1, -1):
            at = rows_at(flip(me // many, g) * CHUNK, CHUNK)

            @pl.loop(0, width // GROUP)
            def _(n):
                cols = rows_at(n * GROUP, GROUP)
                gv_send[at, cols] = dot_nt(gpre[at], win[cols]).astype(bf16)

            for k in range(g * many, (g + 1) * many):
                if k:
                    gv_copies[k - 1].start()
        gvr[mine] = gv_send[mine]
        for one in loads[2:]:
            one.wait()

        @pl.loop(0, width // GROUP)
        def _(n):
            cols = rows_at(n * GROUP, GROUP)
            y_send[:, cols] = dot(act[...], wdown[:, cols]).astype(bf16)

        between()

    pl.run_scoped(
        experts,
        pltpu.VMEM((slots, hidden), bf16), pltpu.VMEM((slots, hidden), bf16),
        pltpu.VMEM((width, hidden), bf16), pltpu.VMEM((hidden, width), bf16),
    )

    def dense_part(
        h1, cot, tok, att, inv, probs, qkv, wqkv, wout, place, gh1, low, gatt, inner_sum, gqkv,
        turned, gk, gvv, outv,
    ):
        loads = [
            pltpu.make_async_copy(src, dst, load.at[i])
            for i, (src, dst) in enumerate(
                (
                    (h1_hbm, h1), (cot_hbm, cot), (att_hbm, att), (wout_hbm, wout), (inv_hbm, inv),
                    (qkv_hbm, qkv), (probs_hbm, probs), (tok_hbm, tok), (wqkv_hbm, wqkv),
                )
            )
        ]
        for one in loads:
            one.start()
        spot = column_of(slot_row(te_ref[...], groups, cap))
        for r in range(rows // BAND):
            at = slice(r * BAND, (r + 1) * BAND)
            here = lax.broadcasted_iota(jnp.int32, (BAND, slots), 1).astype(f32)
            place[at] = jnp.where(here == spot[at], 1.0, 0.0).astype(bf16)
        gate = column_of(gate_ref[...])
        gains_ref[...] = jnp.zeros_like(gains_ref)
        for one in gv_copies:
            one.wait_recv()
        for i in range(2):
            loads[i].wait()

        @pl.loop(0, width // GROUP)
        def _(n):
            cols = rows_at(n * GROUP, GROUP)
            gh1[:, cols] = dot(place[...], gvr[:, cols])

        for r in range(rows // BAND):
            at = slice(r * BAND, (r + 1) * BAND)
            back = gh1[at]
            resid = h1[at]
            centre, inverse = centred(resid)
            unit = centre * inverse
            gains_ref[1:2] += jnp.sum(back * unit, axis=0, keepdims=True)
            slant = back * g2_ref[...].reshape(1, width)
            inner = slant - jnp.mean(slant, axis=-1, keepdims=True)
            inner = inner - unit * jnp.mean(slant * unit, axis=-1, keepdims=True)
            grad = cot[at].astype(f32) + inverse * inner
            gh1[at] = grad
            low[at] = grad.astype(bf16)
        for i in range(2, 5):
            loads[i].wait()

        @pl.loop(0, width // GROUP)
        def _(n):
            cols = rows_at(n * GROUP, GROUP)
            grad = dot_nt(low[...], wout[cols]) * inv[:, cols]
            gatt[:, cols] = grad.astype(bf16)
            inner_sum[:, cols] = grad * att[:, cols].astype(f32) * HEAD_DIM**-0.5

        turned[...] = att[...].T

        @pl.loop(0, width // GROUP)
        def _(n):
            cols = rows_at(n * GROUP, GROUP)
            dense[0:width, cols] = dot(turned[...], low[:, cols]).astype(bf16)

        pair_send(0)
        loads[7].wait()
        for r in range(rows // BAND):
            at = slice(r * BAND, (r + 1) * BAND)
            centre, inverse = centred(tok[at].astype(f32))
            low[at] = (centre * inverse * g1_ref[...].reshape(1, width)).astype(bf16)
        turned[...] = low[...].T
        second()
        loads[5].wait()
        loads[6].wait()
        left = lax.broadcasted_iota(jnp.int32, (1, PAIR), 1) < HEAD_DIM
        none = jnp.zeros((), bf16)

        def halves(block):
            return jnp.concatenate([jnp.where(left, block, none), jnp.where(left, none, block)], axis=0)

        def attend(h):
            at = rows_at(h * PAIR, PAIR)
            k_at = rows_at(width + h * PAIR, PAIR)
            v_at = rows_at(2 * width + h * PAIR, PAIR)
            gk[...] = jnp.zeros_like(gk)
            gvv[...] = jnp.zeros_like(gvv)
            for i in range(rows // BAND):
                first, wide = band(i)
                mine, seen = slice(i * BAND, (i + 1) * BAND), slice(first, first + wide)
                keys = qkv[seen, k_at]
                values = qkv[seen, v_at] * jnp.asarray(HEAD_DIM**-0.5, bf16)
                query, grad = halves(qkv[mine, at]), halves(gatt[mine, at])
                share = probs[h, 2 * i * BAND : 2 * (i + 1) * BAND, 0:wide]
                inner = inner_sum[mine, at]
                middle = jnp.concatenate(
                    [
                        jnp.sum(jnp.where(left, inner, 0.0), axis=-1, keepdims=True),
                        jnp.sum(jnp.where(left, 0.0, inner), axis=-1, keepdims=True),
                    ],
                    axis=0,
                )
                graw = (share.astype(f32) * (dot_nt(grad, values) - middle)).astype(bf16)
                gquery = dot(graw, keys)
                gqkv[mine, at] = jnp.where(left, gquery[0:BAND], gquery[BAND:]).astype(bf16)
                gk[seen] += dot_tn(graw, query)
                gvv[seen] += dot_tn(share, grad)
            gqkv[:, k_at] = gk[...].astype(bf16)
            gqkv[:, v_at] = gvv[...].astype(bf16)
        heads = width // PAIR // 2
        for part in range(2):
            pl.loop(part * heads, (part + 1) * heads)(attend)
            for i in range(3):
                source = i * width + part * heads * PAIR
                target = width + (3 * part + i) * heads * PAIR
                dense[0:width, target : target + heads * PAIR] = dot(
                    turned[...], gqkv[:, source : source + heads * PAIR]
                ).astype(bf16)
            pair_send(part + 1)
            combine(part)
        loads[8].wait()

        def rest():
            @pl.loop(0, width // GROUP)
            def _(n):
                cols = rows_at(n * GROUP, GROUP)
                inner_sum[:, cols] = dot_nt(gqkv[...], wqkv[cols])

            for r in range(rows // BAND):
                at = slice(r * BAND, (r + 1) * BAND)
                back = inner_sum[at]
                centre, inverse = centred(tok[at].astype(f32))
                unit = centre * inverse
                gains_ref[0:1] += jnp.sum(back * unit, axis=0, keepdims=True)
                slant = back * g1_ref[...].reshape(1, width)
                inner = slant - jnp.mean(slant, axis=-1, keepdims=True)
                inner = inner - unit * jnp.mean(slant * unit, axis=-1, keepdims=True)
                outv[at] = (gh1[at] + inverse * inner).astype(bf16)
            pltpu.make_async_copy(outv, gtok_out, store.at[0]).start()

        def y_part():
            for one in y_copies:
                one.wait_recv()

            @pl.loop(0, width // GROUP)
            def _(n):
                cols = rows_at(n * GROUP, GROUP)
                low[:, cols] = (h1[:, cols] + gate * dot(place[...], yr[:, cols])).astype(bf16)

            out_one = pltpu.make_async_copy(low, block_out, store.at[1])
            out_one.start()
            out_one.wait()
            pltpu.make_async_copy(outv, gtok_out, store.at[0]).wait()

        combine(2)
        rest()
        dense_sums(y_part)

    def dense_sums(y_part):
        gain_pair = go(send(gains_ref, gains_pair, s_gain.at[0], r_gain.at[0], (dp, there)))
        third()
        gain_pair.wait_recv()
        gains_part[0] = gains_ref[...] + gains_pair[...]
        gain_far = [
            go(
                send(
                    gains_part.at[0], gains_chip.at[k], s_gain.at[k], r_gain.at[k],
                    (dp, chips[k] * 2 + core),
                )
            )
            for k in range(1, half)
        ]
        total = other[rows_at(chip * per, per)].astype(f32)
        for k in range(1, half):
            for i in range(3):
                far[i, k].wait_recv()
            total = total + got[k].astype(f32)
        share = 3 * width // copies
        thin = width // copies
        part = width // 2
        thirds = jnp.concatenate(
            [
                total[:, width + (3 * j + i) * part : width + (3 * j + i + 1) * part]
                for i in range(3)
                for j in range(2)
            ],
            axis=1,
        )
        for d in range(copies):
            ring[d] = jnp.concatenate(
                [thirds[:, d * share : (d + 1) * share], total[:, d * thin : (d + 1) * thin]],
                axis=1,
            ).astype(bf16)
        around = [
            go(send(ring.at[rounds[k]], ring_got.at[k], s_ring.at[k], r_ring.at[k], (rounds[k], me)))
            for k in range(1, copies)
        ]
        outward()
        for one in y_copies:
            one.start()
        yr[mine] = y_send[mine]
        gains = gains_part[0]
        for k in range(1, half):
            gain_far[k - 1].wait_recv()
            gains = gains + gains_chip[k]
        gains_part[1] = gains
        gain_around = [
            go(
                send(
                    gains_part.at[1], gains_ring.at[k], s_gain.at[half + k], r_gain.at[half + k],
                    (rounds[k], me),
                )
            )
            for k in range(1, copies)
        ]
        summed = ring[dp].astype(f32)
        for k in range(1, copies):
            around[k - 1].wait_recv()
            summed = summed + ring_got[k].astype(f32)
        fourth()
        place = rows_at((core * half + chip) * per, per)
        final[...] = summed.astype(bf16)
        whole[place] = final[...]
        spread = [
            go(
                send(
                    final, whole.at[place], s_out.at[k], r_out.at[k], (dp, chips[k] * 2 + core)
                )
            )
            for k in range(half - 1, 0, -1)
        ]
        y_part()
        for k in range(1, copies):
            gain_around[k - 1].wait_recv()
            gains = gains + gains_ring[k]
        total_ref[...] = gains
        for one in spread:
            one.wait_recv()
        ours = whole.at[rows_at(core * (half * per), half * per)]
        go(send(ours, ours, s_out.at[0], r_out.at[0], (dp, there))).wait_recv()
        last = pltpu.make_async_copy(whole, whole_out, store.at[2])
        last.start()
        last.wait()
        for one in started:
            one.wait_send()

    pl.run_scoped(
        dense_part,
        pltpu.VMEM((rows, width), f32), pltpu.VMEM((rows, width), bf16),
        pltpu.VMEM((rows, width), bf16), pltpu.VMEM((rows, width), bf16),
        pltpu.VMEM((rows, width), f32), pltpu.VMEM(probs_hbm.shape, bf16),
        pltpu.VMEM((rows, 3 * width), bf16), pltpu.VMEM((width, 3 * width), bf16),
        pltpu.VMEM((width, width), bf16), pltpu.VMEM((rows, slots), bf16),
        pltpu.VMEM((rows, width), f32), pltpu.VMEM((rows, width), bf16),
        pltpu.VMEM((rows, width), bf16), pltpu.VMEM((rows, width), f32),
        pltpu.VMEM((rows, 3 * width), bf16), pltpu.VMEM((width, rows), bf16),
        pltpu.VMEM((rows, PAIR), f32), pltpu.VMEM((rows, PAIR), f32),
        pltpu.VMEM((rows, width), bf16),
    )
    for one in gv_copies + y_copies:
        one.wait_send()
    if ends:
        for i in range(9):
            if i not in (0, 3, 4):
                relay.landed(i)
            if i > 1:
                relay.sent(i)


def backward(
    groups, cap, copies, ends, per, act, gpre, w_in, w_down, experts, gates, h1, cot, tok, g1, g2, att,
    inv, probs, qkv, w_qkv, w_out, parts,
):
    slots, hidden = act.shape
    rows, width = tok.shape
    wide = 4 * width
    half = groups // 2
    thin = wide // copies
    sems = pltpu.SemaphoreType.DMA
    block = pltpu.VMEM((slots, width), bf16)
    tile = (8, width)
    up = (width // 4, hidden)
    down = (hidden // 4, width)
    land = [up, down, up, down, up, up, down, down, up] if ends else []
    pools = [up, up, down, up] if ends else []
    return pl.pallas_call(
        functools.partial(backward_kernel, groups, cap, copies, ends),
        out_shape=[
            jax.ShapeDtypeStruct((rows, width), bf16), jax.ShapeDtypeStruct((rows, width), bf16),
            jax.ShapeDtypeStruct((groups * per, thin), bf16), jax.ShapeDtypeStruct(tile, f32),
        ]
        + [jax.ShapeDtypeStruct(one, bf16) for one in land],
        in_specs=[ANY] * 4 + [VMEM] * 2 + [ANY] * 3 + [VMEM] * 2 + [ANY] * (6 + len(parts)),
        out_specs=[ANY] * 3 + [VMEM] + [ANY] * len(land),
        scratch_shapes=[
            block, block, block, block,
            pltpu.VMEM((groups * per, wide), bf16), pltpu.VMEM((half * per, wide), bf16),
            pltpu.VMEM((half, per, wide), bf16), pltpu.VMEM((copies, per, thin), bf16),
            pltpu.VMEM((copies, per, thin), bf16), pltpu.VMEM((per, thin), bf16),
            pltpu.VMEM((groups * per, thin), bf16), pltpu.VMEM(tile, f32), pltpu.VMEM(tile, f32),
            pltpu.VMEM((half, *tile), f32), pltpu.VMEM((2, *tile), f32),
            pltpu.VMEM((copies, *tile), f32), sems((9,)), sems((3,)), sems((groups,)),
            sems((groups,)), sems((groups,)), sems((groups,)), sems((3,)), sems((3,)),
            sems((3 * half,)), sems((3 * half,)), sems((copies,)), sems((copies,)), sems((groups,)),
            sems((groups,)), sems((half + copies,)), sems((half + copies,)), sems((9,)), sems((9,)),
            sems((2,)),
        ]
        + [pltpu.VMEM(one, bf16) for one in pools]
        + [pltpu.VMEM(one, bf16) for one in (up, down) if ends],
        compiler_params=pltpu.CompilerParams(
            collective_id=1, has_side_effects=True, vmem_limit_bytes=60 * MIB
        ),
        cost_estimate=pl.CostEstimate(
            flops=200 * 10**9, bytes_accessed=40 * 10**6, transcendentals=0
        ),
        name="backward",
    )(
        act, gpre, w_in, w_down, experts, gates, h1, cot, tok, g1, g2, att, inv, probs, qkv, w_qkv,
        w_out, *parts,
    )


def finish_kernel(*refs):
    (
        up_own, up_in, up_across, up_out, up_outward, down_own, down_in, down_across, down_out,
        down_outward, block, gtok, whole_ref, gains_ref, up_ref, down_ref, qkv_hbm, out_hbm, one_ref,
        two_ref, block_ref, gtok_ref, a, b, c, d, e, f, up, down, qkv_ref, out_ref,
        block_line, gtok_line, load, store,
    ) = refs
    dp = lax.axis_index("dp")
    outer = (dp == 0) | (dp == 3)
    inner = jnp.logical_not(outer)
    hand_in = [
        pltpu.make_async_copy(block, block_line, load.at[6]),
        pltpu.make_async_copy(gtok, gtok_line, load.at[7]),
    ]
    handed = [
        pltpu.make_async_copy(block_line, block_ref, store.at[0]),
        pltpu.make_async_copy(gtok_line, gtok_ref, store.at[1]),
    ]

    def loads(sources, targets):
        return [
            pltpu.make_async_copy(src, dst, load.at[i])
            for i, (src, dst) in enumerate(zip(sources, targets))
        ]

    inside = loads((up_own, up_in, up_across, down_own, down_in, down_across), (a, b, c, d, e, f))
    outside = loads((up_out, up_outward, down_out, down_outward), (a, b, d, e))

    @pl.when(inner)
    def _():
        for one in inside:
            one.start()

    @pl.when(outer)
    def _():
        for one in outside:
            one.start()

    for one in hand_in:
        one.start()
    thin = qkv_ref.shape[0]
    turned = whole_ref[...].astype(f32).T
    qkv_ref[...] = turned[:thin]
    out_ref[...] = turned[thin:]
    handed += [
        pltpu.make_async_copy(qkv_ref, qkv_hbm, store.at[4]),
        pltpu.make_async_copy(out_ref, out_hbm, store.at[5]),
    ]
    for one in hand_in:
        one.wait()
    for one in handed:
        one.start()
    size = one_ref.shape[1]
    for row, target in ((0, one_ref), (1, two_ref)):
        line = jnp.zeros((1, size), f32)
        for plane in range(4):
            part = gains_ref[row : row + 1, plane * size : (plane + 1) * size]
            line = jnp.where(dp == plane, part, line)
        target[...] = line

    def summed(target, terms):
        lines = target.shape[0] // 12

        @pl.loop(0, 12)
        def _(r):
            at = rows_at(r * lines, lines)
            total = terms[0][at].astype(f32)
            for term in terms[1:]:
                total = total + term[at].astype(f32)
            target[at] = total

    up_store = pltpu.make_async_copy(up, up_ref, store.at[2])
    down_store = pltpu.make_async_copy(down, down_ref, store.at[3])

    @pl.when(inner)
    def _():
        for one in inside[:3]:
            one.wait()
        summed(up, (a, b, c))
        up_store.start()
        for one in inside[3:]:
            one.wait()
        summed(down, (d, e, f))

    @pl.when(outer)
    def _():
        for one in outside[:2]:
            one.wait()
        summed(up, (a, b))
        up_store.start()
        for one in outside[2:]:
            one.wait()
        summed(down, (d, e))

    down_store.start()
    for one in handed:
        one.wait()
    up_store.wait()
    down_store.wait()


def finish(ups, downs, block, gtok, whole, gains):
    up, down = ups[0].shape, downs[0].shape
    width = whole.shape[1]
    thin = width // 4
    sems = pltpu.SemaphoreType.DMA
    return pl.pallas_call(
        finish_kernel,
        out_shape=[
            jax.ShapeDtypeStruct(up, f32), jax.ShapeDtypeStruct(down, f32),
            jax.ShapeDtypeStruct((3 * thin, whole.shape[0]), f32),
            jax.ShapeDtypeStruct((thin, whole.shape[0]), f32),
            jax.ShapeDtypeStruct((1, thin), f32), jax.ShapeDtypeStruct((1, thin), f32),
            jax.ShapeDtypeStruct(block.shape, bf16), jax.ShapeDtypeStruct(gtok.shape, bf16),
        ],
        in_specs=[ANY] * 12 + [VMEM] * 2,
        out_specs=[ANY] * 4 + [VMEM] * 2 + [ANY] * 2,
        scratch_shapes=[pltpu.VMEM(up, bf16)] * 3
        + [pltpu.VMEM(down, bf16)] * 3
        + [
            pltpu.VMEM(up, f32), pltpu.VMEM(down, f32), pltpu.VMEM((3 * thin, whole.shape[0]), f32),
            pltpu.VMEM((thin, whole.shape[0]), f32), pltpu.VMEM(block.shape, bf16),
            pltpu.VMEM(gtok.shape, bf16), sems((8,)), sems((6,)),
        ],
        compiler_params=pltpu.CompilerParams(vmem_limit_bytes=60 * MIB),
        name="finish",
    )(*ups, *downs, block, gtok, whole, gains)


def shards(
    tokens, segment_ids, token_expert, gates, ln1_gain, w_qkv, w_out, ln2_gain, expert_in,
    expert_out, cotangent,
):
    rows, width = tokens.shape
    groups, copies = lax.axis_size("expert"), lax.axis_size("dp")
    cap = 2 * rows // groups
    per = -(-width // (16 * groups)) * 16
    w_in, w_down = expert_in[0], expert_out[0]
    experts, gate_row = token_expert.reshape(1, rows), gates.reshape(1, rows)
    ends = copies == 4
    h1, qkv, att, inv, probs, act, gpre, *parts = forward(
        groups, cap, ends, tokens, segment_ids, experts, gate_row, ln1_gain, w_qkv, w_out,
        ln2_gain, w_in, w_down, cotangent,
    )
    if ends:
        up_far, up_near, up_out, up_own, down_far, down_near, down_out, down_own, up_far_in = parts
        parts = [up_far, up_near, up_out, up_own, up_far_in, down_far, down_near, down_out, down_own]
    block_out, grad_tokens, whole, gains, *landed = backward(
        groups, cap, copies, ends, per, act, gpre, w_in, w_down, experts, gate_row, h1, cotangent,
        tokens, ln1_gain, ln2_gain, att, inv, probs, qkv, w_qkv, w_out, parts if ends else [],
    )
    if ends:
        _, down_own_in, up_own_in, _, _, up_across, down_across, down_outward, up_outward = landed
        up_share, down_share, share_qkv, share_out, share_one, share_two, block, gtok = finish(
            (up_own, up_own_in, up_across, up_out, up_outward),
            (down_own, down_own_in, down_across, down_out, down_outward),
            block_out, grad_tokens, whole[:width], gains,
        )
        return (
            block, gtok, share_one[0], share_qkv.T, share_out.T, share_two[0], up_share[None],
            down_share[None],
        )
    up_share, down_share = (
        lax.psum_scatter(one[None], "dp", scatter_dimension=1, tiled=True) for one in parts
    )
    whole = whole[:width].astype(f32)
    share = width // copies
    gains = lax.dynamic_slice_in_dim(gains, lax.axis_index("dp") * share, share, 1)
    return (
        block_out,
        grad_tokens,
        gains[0],
        whole[:, : 3 * share],
        whole[:, 3 * share :],
        gains[1],
        up_share.astype(f32),
        down_share.astype(f32),
    )


def solution(mesh):
    tokens, experts = P(("dp", "expert"), None), P("expert", None, None)
    return jax.shard_map(
        shards,
        mesh=mesh,
        in_specs=(
            tokens, tokens, tokens, P(("dp", "expert")), P(), P(), P(), P(), experts, experts,
            tokens,
        ),
        out_specs=(
            tokens, tokens, P("dp"), P(None, "dp"), P(None, "dp"), P("dp"),
            P("expert", "dp", None), P("expert", "dp", None),
        ),
        check_vma=False,
    )
```

```python
import functools

import jax
import jax.numpy as jnp
from jax import lax
from jax.experimental import pallas as pl
from jax.experimental.pallas import tpu as pltpu
from jax.sharding import PartitionSpec as P

HEAD_DIM = 64
EPSILON = 1e-05
NEG_LARGE = -1e30
BAND = 128
PAIR = 2 * HEAD_DIM
GROUP = 256
CHUNK = 512
MIB = 2**20
MESH = pl.DeviceIdType.MESH
ANY = pl.BlockSpec(memory_space=pl.ANY)
VMEM = pl.BlockSpec(memory_space=pltpu.VMEM)
f32, bf16 = jnp.float32, jnp.bfloat16


def dot(a, b):
    return jnp.dot(a, b, preferred_element_type=f32)


def dot_nt(a, b):
    return lax.dot_general(a, b, (((1,), (1,)), ((), ())), preferred_element_type=f32)


def dot_tn(a, b):
    return lax.dot_general(a, b, (((0,), (0,)), ((), ())), preferred_element_type=f32)


def flip(index, bits):
    place = 1
    while bits:
        if bits % 2:
            index = index + place * (1 - 2 * ((index // place) % 2))
        bits, place = bits // 2, place * 2
    return index


def add(a, b):
    return (a.astype(f32) + b.astype(f32)).astype(bf16)


def rows_at(start, size):
    return pl.ds(pl.multiple_of(start, size), size)


def greet(peers):
    barrier = pltpu.get_barrier_semaphore()
    for peer in peers:
        pl.semaphore_signal(barrier, inc=1, device_id=peer, device_id_type=MESH)
    pl.semaphore_wait(barrier, len(peers))


def sides(dp):
    side = dp // 2
    return flip(dp, 1), 3 - dp, [3 * (1 - side), 2 - side, 3 * side, 1 + side]


class Relay:
    def __init__(self, dp, me, moves, ssem, rsem):
        self.outer = (dp == 0) | (dp == 3)
        self.inner = jnp.logical_not(self.outer)
        beside, across, _ = sides(dp)
        self.moves = []
        for i, (kind, source, target) in enumerate(moves):
            plane = across if kind == "across" else beside
            copy = pltpu.make_async_remote_copy(
                src_ref=source, dst_ref=target, send_sem=ssem.at[i], recv_sem=rsem.at[i],
                device_id=(plane, me), device_id_type=MESH,
            )
            sender = self.outer if kind == "inward" else self.inner
            receiver = self.outer if kind == "outward" else self.inner
            self.moves.append((copy, sender, receiver))

    def start(self, *which):
        for i in which:
            copy, sender, _ = self.moves[i]
            pl.when(sender)(copy.start)

    def sent(self, i):
        pl.when(self.moves[i][1])(self.moves[i][0].wait_send)

    def landed(self, i):
        pl.when(self.moves[i][2])(self.moves[i][0].wait_recv)

    def merged(self, first, second, total, spare, sem):
        @pl.when(self.inner)
        def _():
            loads = [
                pltpu.make_async_copy(first, total, sem.at[0]),
                pltpu.make_async_copy(second, spare, sem.at[1]),
            ]
            for one in loads:
                one.start()
            for one in loads:
                one.wait()
            lines = total.shape[0] // 12

            @pl.loop(0, 12)
            def _(r):
                at = rows_at(r * lines, lines)
                total[at] = add(total[at], spare[at])


def band(index):
    first = max(0, index - 2) * BAND
    return first, (index + 1) * BAND - first


def column_of(row):
    size = row.shape[1]
    eye = lax.broadcasted_iota(jnp.int32, (size, size), 0) == lax.broadcasted_iota(
        jnp.int32, (size, size), 1
    )
    return jnp.sum(jnp.where(eye, row, 0.0), axis=1, keepdims=True)


def slot_row(experts, num_experts, capacity):
    rows = experts.shape[1]
    lines = max(16, num_experts)
    onehot = lax.broadcasted_iota(jnp.int32, (lines, rows), 0) == experts
    onehot = jnp.where(onehot, 1.0, 0.0)
    before = lax.broadcasted_iota(jnp.int32, (rows, rows), 0) < lax.broadcasted_iota(
        jnp.int32, (rows, rows), 1
    )
    earlier = dot(onehot.astype(bf16), jnp.where(before, 1.0, 0.0).astype(bf16))
    rank = jnp.sum(onehot * earlier, axis=0, keepdims=True)
    return experts.astype(f32) * float(capacity) + rank


def centred(hidden):
    centre = hidden - jnp.mean(hidden, axis=-1, keepdims=True)
    spread = jnp.mean(centre * centre, axis=-1, keepdims=True)
    return centre, lax.rsqrt(spread + EPSILON)


def gelu_pair(x):
    bell = jnp.exp2((-0.5 * 1.4426950408889634) * (x * x))
    phi = 0.5 + 0.5 * lax.erf(x * 0.7071067811865476)
    return x * phi, phi + x * (bell * 0.3989422804014327)


def gelu(x):
    return gelu_pair(x)[0]


def forward_kernel(groups, cap, ends, *refs):
    (
        tok_hbm, seg_ref, te_ref, gate_ref, g1_ref, wqkv_hbm, wout_hbm, g2_ref, win_hbm, wdown_hbm,
        cot_hbm, h1_out, qkv_out, att_out, inv_out, probs_out, act_out, gpre_out,
    ) = refs[:18]
    count = 4 if ends else 1
    ups, downs = refs[18 : 18 + count], refs[18 + count : 18 + 2 * count]
    up_land = refs[18 + 2 * count : 18 + 2 * count + ends]
    (
        tok, cot, win, wdown, low, h1, place, sent, gy_send, gy_got, v_got, gy_low, spot_own, gy_line,
        v_line, spot_far, place_far, gy_fsend, far_send, gy_far, v_far, act,
        gpre, load, store, act_store, gpre_store, gy_ssem, gy_rsem, v_ssem, v_rsem, gy_fssem,
        gy_frsem, v_fssem, v_frsem, line_ssem, line_rsem, rel_s, rel_r,
    ) = refs[18 + 2 * count + ends :]
    dp, me = lax.axis_index("dp"), lax.axis_index("expert")
    rows, width = tok.shape
    slots, hidden = act.shape
    pairs = width // PAIR
    outer = (dp == 0) | (dp == 3)
    inner = jnp.logical_not(outer)
    first_loads = [
        pltpu.make_async_copy(src, dst, load.at[i])
        for i, (src, dst) in enumerate(
            ((cot_hbm, cot), (tok_hbm, tok), (win_hbm, win), (wdown_hbm, wdown))
        )
    ]
    first_loads[0].start()
    first_loads[1].start()
    beside = [(flip(dp, 1), me)] if ends else []
    greet([(dp, flip(me, k)) for k in range(1, groups)] + beside)

    def exchange(source, target, send, receive, k):
        peer = flip(me, k)
        return pltpu.make_async_remote_copy(
            src_ref=source.at[rows_at(peer * cap, cap)],
            dst_ref=target.at[rows_at(me * cap, cap)],
            send_sem=send.at[k],
            recv_sem=receive.at[k],
            device_id=(dp, peer),
            device_id_type=MESH,
        )

    gy_copies = [exchange(gy_send, gy_got, gy_ssem, gy_rsem, k) for k in range(1, groups)]
    v_copies = [exchange(sent, v_got, v_ssem, v_rsem, k) for k in range(1, groups)]
    far_groups = groups if ends else 0
    gy_fars = [exchange(gy_fsend, gy_far, gy_fssem, gy_frsem, k) for k in range(1, far_groups)]
    v_fars = [exchange(far_send, v_far, v_fssem, v_frsem, k) for k in range(1, far_groups)]
    lines = ends and [
        pltpu.make_async_remote_copy(
            src_ref=source, dst_ref=target, send_sem=line_ssem.at[i], recv_sem=line_rsem.at[i],
            device_id=(flip(dp, 1), me), device_id_type=MESH,
        )
        for i, (source, target) in enumerate(
            ((spot_own, spot_far), (gy_low, gy_line), (low, v_line))
        )
    ]

    def when(condition, action):
        if ends:
            pl.when(condition)(action)

    def positions(spot, target):
        @pl.loop(0, slots // GROUP)
        def _(g):
            here = lax.broadcasted_iota(jnp.int32, (GROUP, rows), 0) + g * GROUP
            there = jnp.where(here.astype(f32) == spot, 1.0, 0.0)
            target[rows_at(g * GROUP, GROUP)] = there.astype(bf16)

    def placed(where, line, target):
        @pl.loop(0, width // GROUP)
        def _(n):
            cols = rows_at(n * GROUP, GROUP)
            target[:, cols] = dot(where[...], line[:, cols]).astype(bf16)

    def far_gy():
        lines[0].wait_recv()
        lines[1].wait_recv()
        positions(spot_far[0:1], place_far)
        placed(place_far, gy_line, gy_fsend)
        for one in gy_fars:
            one.start()
        gy_far[mine] = gy_fsend[mine]

    def far_v():
        lines[2].wait_recv()
        placed(place_far, v_line, far_send)
        for one in v_fars:
            one.start()
        v_far[mine] = far_send[mine]

    mine = rows_at(me * cap, cap)

    def attention(wqkv, wout, qkv, att, inv, probs, bias):
        loads = [
            pltpu.make_async_copy(wqkv_hbm, wqkv, load.at[4]),
            pltpu.make_async_copy(wout_hbm, wout, load.at[5]),
        ]
        for one in loads + first_loads[2:]:
            one.start()
        spot = slot_row(te_ref[...], groups, cap)

        positions(spot, place)
        first_loads[0].wait()
        gate = column_of(gate_ref[...])
        gy_low[...] = (gate * cot[...].astype(f32)).astype(bf16)
        if ends:
            spot_own[...] = jnp.broadcast_to(spot, spot_own.shape)

            @pl.when(outer)
            def _():
                lines[0].start()
                lines[1].start()

        placed(place, gy_low, gy_send)
        for one in gy_copies:
            one.start()
        gy_got[mine] = gy_send[mine]
        segs = seg_ref[...].astype(f32)
        seg_col = column_of(segs)
        for i in range(rows // BAND):
            first, wide = band(i)
            causal = (lax.broadcasted_iota(jnp.int32, (BAND, wide), 0) + i * BAND) >= (
                lax.broadcasted_iota(jnp.int32, (BAND, wide), 1) + first
            )
            same = seg_col[i * BAND : (i + 1) * BAND] == segs[:, first : first + wide]
            bias[i * BAND : (i + 1) * BAND, 0:wide] = jnp.where(causal & same, 0.0, NEG_LARGE)

        first_loads[1].wait()

        @pl.loop(0, rows // BAND)
        def _(r):
            at = rows_at(r * BAND, BAND)
            centre, inverse = centred(tok[at].astype(f32))
            low[at] = (centre * inverse * g1_ref[...].reshape(1, width)).astype(bf16)

        loads[0].wait()

        @pl.loop(0, 3 * width // GROUP)
        def _(c):
            at = rows_at(c * GROUP, GROUP)
            qkv[:, at] = dot(low[...], wqkv[:, at]).astype(bf16)

        left = lax.broadcasted_iota(jnp.int32, (1, PAIR), 1) < HEAD_DIM
        none, unit = jnp.zeros((), bf16), jnp.ones((), bf16)

        def attend(h):
            at = rows_at(h * PAIR, PAIR)
            k_at = rows_at(width + h * PAIR, PAIR)
            v_at = rows_at(2 * width + h * PAIR, PAIR)
            for i in range(rows // BAND):
                first, wide = band(i)
                here = slice(i * BAND, (i + 1) * BAND)
                keys = qkv[first : first + wide, k_at]
                values = qkv[first : first + wide, v_at]
                query = qkv[here, at] * jnp.asarray(HEAD_DIM**-0.5, bf16)
                query = jnp.concatenate(
                    [jnp.where(left, query, none), jnp.where(left, none, query)], axis=0
                )
                scores = dot_nt(query, keys).reshape(2, BAND, wide) + bias[here, 0:wide][None]
                weights = jnp.exp(scores - jnp.max(scores, axis=-1, keepdims=True)).astype(bf16)
                probs[h, 2 * i * BAND : 2 * (i + 1) * BAND, 0:wide] = weights.reshape(
                    2 * BAND, wide
                )
                one = dot(weights[0], jnp.where(left, values, unit))
                two = dot(weights[1], jnp.where(left, unit, values))
                scale = 1.0 / pltpu.roll(jnp.where(left, two, one), HEAD_DIM, 1)
                inv[here, at] = scale
                att[here, at] = (jnp.where(left, one, two) * scale).astype(bf16)

        pl.loop(0, pairs)(attend)
        stores = [
            pltpu.make_async_copy(src, dst, store.at[i])
            for i, (src, dst) in enumerate(
                ((qkv, qkv_out), (probs, probs_out), (att, att_out), (inv, inv_out))
            )
        ]
        for one in stores:
            one.start()
        loads[1].wait()

        @pl.loop(0, width // GROUP)
        def _(n):
            cols = rows_at(n * GROUP, GROUP)
            h1[:, cols] = dot(att[...], wout[:, cols])

        @pl.loop(0, rows // BAND)
        def _(r):
            at = rows_at(r * BAND, BAND)
            resid = tok[at].astype(f32) + h1[at]
            h1[at] = resid
            centre, inverse = centred(resid)
            low[at] = (centre * inverse * g2_ref[...].reshape(1, width)).astype(bf16)

        when(outer, lambda: lines[2].start())

        placed(place, low, sent)
        for one in v_copies:
            one.start()
        v_got[mine] = sent[mine]
        when(inner, far_gy)
        for one in stores:
            one.wait()

    pl.run_scoped(
        attention,
        pltpu.VMEM((width, 3 * width), bf16), pltpu.VMEM((width, width), bf16),
        pltpu.VMEM((rows, 3 * width), bf16), pltpu.VMEM((rows, width), bf16),
        pltpu.VMEM((rows, width), f32), pltpu.VMEM((pairs, 2 * rows, 3 * BAND), bf16),
        pltpu.VMEM((rows, 3 * BAND), f32),
    )

    def experts(act_far, gdown, gup, turned):
        stores = [pltpu.make_async_copy(h1, h1_out, store.at[4])]
        stores[0].start()
        for one in first_loads[2:]:
            one.wait()
        for one in gy_copies:
            one.wait_recv()

        @pl.loop(0, hidden // GROUP)
        def _(c):
            at = rows_at(c * GROUP, GROUP)
            gpre[:, at] = dot_nt(gy_got[...], wdown[at]).astype(bf16)

        many = GROUP // cap
        for g in range(slots // GROUP):
            for k in range(g * many, (g + 1) * many):
                if k:
                    v_copies[k - 1].wait_recv()
            at = rows_at(flip(me // many, g) * GROUP, GROUP)

            @pl.loop(0, hidden // CHUNK)
            def _(c):
                cols = rows_at(c * CHUNK, CHUNK)
                value, back = gelu_pair(dot(v_got[at], win[:, cols]))
                act[at, cols] = value.astype(bf16)
                gpre[at, cols] = (gpre[at, cols].astype(f32) * back).astype(bf16)

            for source, target, sem in ((act, act_out, act_store), (gpre, gpre_out, gpre_store)):
                stores.append(pltpu.make_async_copy(source.at[at], target.at[at], sem.at[g]))
                stores[-1].start()
            if g == 1:
                when(inner, far_v)

        turned[...] = v_got[...].T

        @pl.loop(0, hidden // GROUP)
        def _(c):
            cols = rows_at(c * GROUP, GROUP)
            gup[:, cols] = dot(turned[...], gpre[:, cols]).astype(bf16)

        shares = sides(dp)[2] if ends else [0]
        size, share = width // count, hidden // count
        for i, (one, part) in enumerate(zip(shares, ups)):
            source = gup.at[rows_at(one * size, size)]
            stores.append(pltpu.make_async_copy(source, part, store.at[5 + i]))
            stores[-1].start()
        if ends:
            relay = Relay(
                dp, me, [("inward", gup.at[rows_at(shares[0] * size, size)], up_land[0])],
                rel_s, rel_r,
            )
            relay.start(0)

        def down(kept, shared):
            for i in kept:

                @pl.loop(0, share // GROUP)
                def _(c):
                    cols = pl.ds(pl.multiple_of(shares[i] * share + c * GROUP, GROUP), GROUP)
                    at = pl.ds(pl.multiple_of(i * share + c * GROUP, GROUP), GROUP)
                    if shared:
                        total = gdown[at].astype(f32) + dot_tn(act_far[:, at], gy_far[...])
                    else:
                        total = dot_tn(act[:, cols], gy_got[...])
                    gdown[at] = total.astype(bf16)

        def leave(kept):
            for i in kept:
                at = slice(i * share, (i + 1) * share)
                pltpu.make_async_copy(gdown.at[at], downs[i], store.at[9 + i]).start()

        def taken(kept):
            for i in kept:
                at = slice(i * share, (i + 1) * share)
                pltpu.make_async_copy(gdown.at[at], downs[i], store.at[9 + i]).wait()

        def inside():
            down([0, 1], False)
            for g in range(slots // GROUP):
                for k in range(g * many, (g + 1) * many):
                    if k:
                        v_fars[k - 1].wait_recv()
                at = rows_at(flip(me // many, g) * GROUP, GROUP)
                for i in range(2):

                    @pl.loop(0, 2)
                    def _(c):
                        cols = pl.ds(pl.multiple_of(shares[i] * share + c * (share // 2), 128), share // 2)
                        kept = pl.ds(pl.multiple_of(i * share + c * (share // 2), 128), share // 2)
                        act_far[at, kept] = gelu(dot(v_far[at], win[:, cols])).astype(bf16)

            for one in gy_fars:
                one.wait_recv()
            down([0, 1], True)
            leave([0, 1])
            for one in gy_fars + v_fars:
                one.wait_send()
            taken([0, 1])

        down([2, 3] if ends else [0], False)
        leave([2, 3] if ends else [0])
        if ends:
            pl.when(inner)(inside)

            @pl.when(outer)
            def _():
                for one in lines:
                    one.wait_send()

        taken([2, 3] if ends else [0])
        for one in gy_copies + v_copies:
            one.wait_send()
        for one in stores:
            one.wait()
        if ends:
            relay.landed(0)
            relay.sent(0)

    pl.run_scoped(
        experts,
        pltpu.VMEM((slots, hidden // 2) if ends else (16, 128), bf16),
        pltpu.VMEM((hidden, width), bf16), pltpu.VMEM((width, hidden), bf16),
        pltpu.VMEM((width, slots), bf16),
    )


def forward(groups, cap, ends, tokens, segs, experts, gates, g1, w_qkv, w_out, g2, w_in, w_down, cot):
    rows, width = tokens.shape
    hidden = w_in.shape[1]
    slots = groups * cap
    pairs = width // PAIR
    wide = 3 * BAND
    count = 4 if ends else 1
    parts = [(width // count, hidden)] * count + [(hidden // count, width)] * count
    parts += [(width // count, hidden)] * ends
    shapes = [
        ((rows, width), f32), ((rows, 3 * width), bf16), ((rows, width), bf16), ((rows, width), f32),
        ((pairs, 2 * rows, wide), bf16), ((slots, hidden), bf16), ((slots, hidden), bf16),
    ] + [(one, bf16) for one in parts]
    sems = pltpu.SemaphoreType.DMA
    lines = pltpu.VMEM((rows, width), bf16)
    block = pltpu.VMEM((slots, width), bf16)
    tiny = (16, 128)
    far = block if ends else pltpu.VMEM(tiny, bf16)
    far_line = lines if ends else pltpu.VMEM(tiny, bf16)
    return pl.pallas_call(
        functools.partial(forward_kernel, groups, cap, int(ends)),
        out_shape=[jax.ShapeDtypeStruct(*one) for one in shapes],
        in_specs=[ANY, VMEM, VMEM, VMEM, VMEM, ANY, ANY, VMEM, ANY, ANY, ANY],
        out_specs=[ANY] * len(shapes),
        scratch_shapes=[
            lines, lines, pltpu.VMEM(w_in.shape, bf16), pltpu.VMEM(w_down.shape, bf16), lines,
            pltpu.VMEM((rows, width), f32), pltpu.VMEM((slots, rows), bf16), block, block, block,
            block, lines, pltpu.VMEM((8, rows), f32), far_line, far_line, pltpu.VMEM((8, rows), f32),
            pltpu.VMEM((slots, rows) if ends else tiny, bf16), far, far, far, far,
            pltpu.VMEM((slots, hidden), bf16), pltpu.VMEM((slots, hidden), bf16),
            sems((6,)), sems((13,)), sems((slots // GROUP,)), sems((slots // GROUP,)),
        ]
        + [sems((groups,))] * 8
        + [sems((3,))] * 2
        + [sems((1,))] * 2,
        compiler_params=pltpu.CompilerParams(
            collective_id=0, has_side_effects=True, vmem_limit_bytes=60 * MIB
        ),
        cost_estimate=pl.CostEstimate(
            flops=200 * 10**9, bytes_accessed=40 * 10**6, transcendentals=10**7
        ),
        name="forward",
    )(tokens, segs, experts, gates, g1, w_qkv, w_out, g2, w_in, w_down, cot)


def backward_kernel(groups, cap, copies, ends, *refs):
    (
        act_hbm, gpre_hbm, win_hbm, wdown_hbm, te_ref, gate_ref, h1_hbm, cot_hbm, tok_hbm, g1_ref,
        g2_ref, att_hbm, inv_hbm, probs_hbm, qkv_hbm, wqkv_hbm, wout_hbm,
    ) = refs[:17]
    parts, refs = refs[17 : 17 + 9 * ends], refs[17 + 9 * ends :]
    block_out, gtok_out, whole_out, total_ref = refs[:4]
    landed, refs = refs[4 : 4 + 9 * ends], refs[4 + 9 * ends :]
    (
        gv_send, gvr, y_send, yr, dense, other, got, ring, ring_got, final, whole, gains_ref,
        gains_pair, gains_chip, gains_part, gains_ring, load, store, gv_ssem, gv_rsem, y_ssem, y_rsem,
        s_pair, r_pair, s_chip, r_chip, s_ring, r_ring, s_out, r_out, s_gain, r_gain, rel_s, rel_r,
        pool_sem, *pools,
    ) = refs
    dp, me = lax.axis_index("dp"), lax.axis_index("expert")
    slots, width = gvr.shape
    rows, hidden = tok_hbm.shape[0], win_hbm.shape[1]
    rounds = [lax.rem(dp + k, copies) for k in range(copies)]
    half = groups // 2
    per, wide = got.shape[1:]
    many = CHUNK // cap
    mine = rows_at(me * cap, cap)

    def exchange(source, target, ssem, rsem):
        return [
            pltpu.make_async_remote_copy(
                src_ref=source.at[rows_at(flip(me, k) * cap, cap)],
                dst_ref=target.at[rows_at(me * cap, cap)],
                send_sem=ssem.at[k],
                recv_sem=rsem.at[k],
                device_id=(dp, flip(me, k)),
                device_id_type=MESH,
            )
            for k in range(1, groups)
        ]

    gv_copies = exchange(gv_send, gvr, gv_ssem, gv_rsem)
    y_copies = exchange(y_send, yr, y_ssem, y_rsem)
    relay = None
    if ends:
        up_far, up_near, up_out, up_own, up_far_in, down_far, down_near, down_out, down_own = parts
        relay = Relay(
            dp, me,
            [
                ("inward", up_near, landed[0]), ("inward", down_own, landed[1]),
                ("inward", up_own, landed[2]), ("across", down_far, landed[3]),
                ("across", pools[0], landed[4]), ("across", pools[1], landed[5]),
                ("across", down_near, landed[6]), ("outward", pools[2], landed[7]),
                ("outward", pools[3], landed[8]),
            ],
            rel_s, rel_r,
        )

    chip, core = me // 2, me % 2
    there = flip(me, 1)
    chips = [flip(chip, k) for k in range(half)]
    started = []
    sets = [(0, width), (width, 3 * width // 2), (5 * width // 2, 3 * width // 2)]
    pair, far = {}, {}

    def send(source, target, ssem, rsem, device):
        return pltpu.make_async_remote_copy(
            src_ref=source, dst_ref=target, send_sem=ssem, recv_sem=rsem, device_id=device,
            device_id_type=MESH,
        )

    def go(copy):
        copy.start()
        started.append(copy)
        return copy

    def pair_send(i):
        cols = slice(sets[i][0], sum(sets[i]))
        pair[i] = go(
            send(
                dense.at[rows_at((1 - core) * (half * per), half * per), cols], other.at[:, cols],
                s_pair.at[i], r_pair.at[i], (dp, there),
            )
        )

    def combine(i):
        cols = slice(sets[i][0], sum(sets[i]))
        pair[i].wait_recv()
        for k in range(half - 1, -1, -1):
            at = rows_at(chips[k] * per, per)
            own = rows_at((core * half + chips[k]) * per, per)
            other[at, cols] = add(dense[own, cols], other[at, cols])
            if k:
                far[i, k] = go(
                    send(
                        other.at[at, cols], got.at[k, :, cols], s_chip.at[3 * k + i],
                        r_chip.at[3 * k + i], (dp, chips[k] * 2 + core),
                    )
                )

    def first():
        if ends:
            relay.start(0, 3)

    def between():
        if ends:
            relay.merged(up_far, up_far_in, pools[0], pools[4], pool_sem)
            relay.start(4)

    def second():
        if ends:
            relay.sent(0)
            relay.start(1)
            relay.landed(0)
            relay.merged(up_near, landed[0], pools[1], pools[4], pool_sem)
            relay.start(5)
            relay.landed(3)
            relay.merged(down_out, landed[3], pools[2], pools[5], pool_sem)
            relay.start(7)

    def third():
        if ends:
            relay.sent(1)
            relay.start(2)

    def outward():
        if ends:
            relay.landed(4)
            relay.merged(up_out, landed[4], pools[3], pools[4], pool_sem)
            relay.start(8)

    def fourth():
        if ends:
            relay.start(6)

    def experts(act, gpre, win, wdown):
        loads = [
            pltpu.make_async_copy(src, dst, load.at[i])
            for i, (src, dst) in enumerate(
                ((win_hbm, win), (gpre_hbm, gpre), (wdown_hbm, wdown), (act_hbm, act))
            )
        ]
        for one in loads:
            one.start()
        greet(
            [(dp, flip(me, k)) for k in range(1, groups)] + [(one, me) for one in rounds[1:]]
        )
        first()
        for one in loads[:2]:
            one.wait()
        for g in range(slots // CHUNK - 1, -1, -1):
            at = rows_at(flip(me // many, g) * CHUNK, CHUNK)

            @pl.loop(0, width // GROUP)
            def _(n):
                cols = rows_at(n * GROUP, GROUP)
                gv_send[at, cols] = dot_nt(gpre[at], win[cols]).astype(bf16)

            for k in range(g * many, (g + 1) * many):
                if k:
                    gv_copies[k - 1].start()
        gvr[mine] = gv_send[mine]
        for one in loads[2:]:
            one.wait()

        @pl.loop(0, width // GROUP)
        def _(n):
            cols = rows_at(n * GROUP, GROUP)
            y_send[:, cols] = dot(act[...], wdown[:, cols]).astype(bf16)

        between()

    pl.run_scoped(
        experts,
        pltpu.VMEM((slots, hidden), bf16), pltpu.VMEM((slots, hidden), bf16),
        pltpu.VMEM((width, hidden), bf16), pltpu.VMEM((hidden, width), bf16),
    )

    def dense_part(
        h1, cot, tok, att, inv, probs, qkv, wqkv, wout, place, gh1, low, gatt, inner_sum, gqkv,
        turned, gk, gvv, outv, lines,
    ):
        loads = [
            pltpu.make_async_copy(src, dst, load.at[i])
            for i, (src, dst) in enumerate(
                (
                    (h1_hbm, h1), (cot_hbm, cot), (att_hbm, att), (wout_hbm, wout), (inv_hbm, inv),
                    (qkv_hbm, qkv), (probs_hbm, probs), (tok_hbm, tok), (wqkv_hbm, wqkv),
                )
            )
        ]
        loads[7].start()
        for i in (0, 1, 2, 3, 4, 5, 6, 8):
            loads[i].start()
        spot = column_of(slot_row(te_ref[...], groups, cap))
        for r in range(rows // BAND):
            at = slice(r * BAND, (r + 1) * BAND)
            here = lax.broadcasted_iota(jnp.int32, (BAND, slots), 1).astype(f32)
            place[at] = jnp.where(here == spot[at], 1.0, 0.0).astype(bf16)
        gate = column_of(gate_ref[...])
        gains_ref[...] = jnp.zeros_like(gains_ref)
        loads[7].wait()
        for r in range(rows // BAND):
            at = slice(r * BAND, (r + 1) * BAND)
            centre, inverse = centred(tok[at].astype(f32))
            outv[at] = (centre * inverse * g1_ref[...].reshape(1, width)).astype(bf16)
        lines[...] = outv[...].T
        for one in gv_copies:
            one.wait_recv()
        for i in range(2):
            loads[i].wait()

        @pl.loop(0, width // GROUP)
        def _(n):
            cols = rows_at(n * GROUP, GROUP)
            gh1[:, cols] = dot(place[...], gvr[:, cols])

        for r in range(rows // BAND):
            at = slice(r * BAND, (r + 1) * BAND)
            back = gh1[at]
            resid = h1[at]
            centre, inverse = centred(resid)
            unit = centre * inverse
            gains_ref[1:2] += jnp.sum(back * unit, axis=0, keepdims=True)
            slant = back * g2_ref[...].reshape(1, width)
            inner = slant - jnp.mean(slant, axis=-1, keepdims=True)
            inner = inner - unit * jnp.mean(slant * unit, axis=-1, keepdims=True)
            grad = cot[at].astype(f32) + inverse * inner
            gh1[at] = grad
            low[at] = grad.astype(bf16)
        for i in range(2, 5):
            loads[i].wait()

        @pl.loop(0, width // GROUP)
        def _(n):
            cols = rows_at(n * GROUP, GROUP)
            grad = dot_nt(low[...], wout[cols]) * inv[:, cols]
            gatt[:, cols] = grad.astype(bf16)
            inner_sum[:, cols] = grad * att[:, cols].astype(f32) * HEAD_DIM**-0.5

        turned[...] = att[...].T

        @pl.loop(0, width // GROUP)
        def _(n):
            cols = rows_at(n * GROUP, GROUP)
            dense[0:width, cols] = dot(turned[...], low[:, cols]).astype(bf16)

        pair_send(0)
        second()
        loads[5].wait()
        loads[6].wait()
        left = lax.broadcasted_iota(jnp.int32, (1, PAIR), 1) < HEAD_DIM
        none = jnp.zeros((), bf16)

        def halves(block):
            return jnp.concatenate([jnp.where(left, block, none), jnp.where(left, none, block)], axis=0)

        def attend(h):
            at = rows_at(h * PAIR, PAIR)
            k_at = rows_at(width + h * PAIR, PAIR)
            v_at = rows_at(2 * width + h * PAIR, PAIR)
            gk[...] = jnp.zeros_like(gk)
            gvv[...] = jnp.zeros_like(gvv)
            for i in range(rows // BAND):
                first, wide = band(i)
                mine, seen = slice(i * BAND, (i + 1) * BAND), slice(first, first + wide)
                keys = qkv[seen, k_at]
                values = qkv[seen, v_at] * jnp.asarray(HEAD_DIM**-0.5, bf16)
                query, grad = halves(qkv[mine, at]), halves(gatt[mine, at])
                share = probs[h, 2 * i * BAND : 2 * (i + 1) * BAND, 0:wide]
                inner = inner_sum[mine, at]
                middle = jnp.concatenate(
                    [
                        jnp.sum(jnp.where(left, inner, 0.0), axis=-1, keepdims=True),
                        jnp.sum(jnp.where(left, 0.0, inner), axis=-1, keepdims=True),
                    ],
                    axis=0,
                )
                graw = (share.astype(f32) * (dot_nt(grad, values) - middle)).astype(bf16)
                gquery = dot(graw, keys)
                gqkv[mine, at] = jnp.where(left, gquery[0:BAND], gquery[BAND:]).astype(bf16)
                gk[seen] += dot_tn(graw, query)
                gvv[seen] += dot_tn(share, grad)
            gqkv[:, k_at] = gk[...].astype(bf16)
            gqkv[:, v_at] = gvv[...].astype(bf16)
        heads = width // PAIR // 2
        for part in range(2):
            pl.loop(part * heads, (part + 1) * heads)(attend)
            for i in range(3):
                source = i * width + part * heads * PAIR
                target = width + (3 * part + i) * heads * PAIR
                dense[0:width, target : target + heads * PAIR] = dot(
                    lines[...], gqkv[:, source : source + heads * PAIR]
                ).astype(bf16)
            pair_send(part + 1)
            combine(part)
        loads[8].wait()

        def rest():
            @pl.loop(0, width // GROUP)
            def _(n):
                cols = rows_at(n * GROUP, GROUP)
                inner_sum[:, cols] = dot_nt(gqkv[...], wqkv[cols])

            for r in range(rows // BAND):
                at = slice(r * BAND, (r + 1) * BAND)
                back = inner_sum[at]
                centre, inverse = centred(tok[at].astype(f32))
                unit = centre * inverse
                gains_ref[0:1] += jnp.sum(back * unit, axis=0, keepdims=True)
                slant = back * g1_ref[...].reshape(1, width)
                inner = slant - jnp.mean(slant, axis=-1, keepdims=True)
                inner = inner - unit * jnp.mean(slant * unit, axis=-1, keepdims=True)
                outv[at] = (gh1[at] + inverse * inner).astype(bf16)
            pltpu.make_async_copy(outv, gtok_out, store.at[0]).start()

        def y_part():
            for one in y_copies:
                one.wait_recv()

            @pl.loop(0, width // GROUP)
            def _(n):
                cols = rows_at(n * GROUP, GROUP)
                low[:, cols] = (h1[:, cols] + gate * dot(place[...], yr[:, cols])).astype(bf16)

            out_one = pltpu.make_async_copy(low, block_out, store.at[1])
            out_one.start()
            out_one.wait()
            pltpu.make_async_copy(outv, gtok_out, store.at[0]).wait()

        combine(2)
        rest()
        dense_sums(y_part)

    def dense_sums(y_part):
        gain_pair = go(send(gains_ref, gains_pair, s_gain.at[0], r_gain.at[0], (dp, there)))
        third()
        gain_pair.wait_recv()
        gains_part[0] = gains_ref[...] + gains_pair[...]
        gain_far = [
            go(
                send(
                    gains_part.at[0], gains_chip.at[k], s_gain.at[k], r_gain.at[k],
                    (dp, chips[k] * 2 + core),
                )
            )
            for k in range(1, half)
        ]
        total = other[rows_at(chip * per, per)].astype(f32)
        for k in range(1, half):
            for i in range(3):
                far[i, k].wait_recv()
            total = total + got[k].astype(f32)
        share = 3 * width // copies
        thin = width // copies
        part = width // 2
        thirds = jnp.concatenate(
            [
                total[:, width + (3 * j + i) * part : width + (3 * j + i + 1) * part]
                for i in range(3)
                for j in range(2)
            ],
            axis=1,
        )
        for d in range(copies):
            ring[d] = jnp.concatenate(
                [thirds[:, d * share : (d + 1) * share], total[:, d * thin : (d + 1) * thin]],
                axis=1,
            ).astype(bf16)
        around = [
            go(send(ring.at[rounds[k]], ring_got.at[k], s_ring.at[k], r_ring.at[k], (rounds[k], me)))
            for k in range(1, copies)
        ]
        outward()
        for one in y_copies:
            one.start()
        yr[mine] = y_send[mine]
        gains = gains_part[0]
        for k in range(1, half):
            gain_far[k - 1].wait_recv()
            gains = gains + gains_chip[k]
        gains_part[1] = gains
        gain_around = [
            go(
                send(
                    gains_part.at[1], gains_ring.at[k], s_gain.at[half + k], r_gain.at[half + k],
                    (rounds[k], me),
                )
            )
            for k in range(1, copies)
        ]
        summed = ring[dp].astype(f32)
        for k in range(1, copies):
            around[k - 1].wait_recv()
            summed = summed + ring_got[k].astype(f32)
        fourth()
        place = rows_at((core * half + chip) * per, per)
        final[...] = summed.astype(bf16)
        whole[place] = final[...]
        spread = [
            go(
                send(
                    final, whole.at[place], s_out.at[k], r_out.at[k], (dp, chips[k] * 2 + core)
                )
            )
            for k in range(half - 1, 0, -1)
        ]
        y_part()
        for k in range(1, copies):
            gain_around[k - 1].wait_recv()
            gains = gains + gains_ring[k]
        total_ref[...] = gains
        for one in spread:
            one.wait_recv()
        ours = whole.at[rows_at(core * (half * per), half * per)]
        go(send(ours, ours, s_out.at[0], r_out.at[0], (dp, there))).wait_recv()
        last = pltpu.make_async_copy(whole, whole_out, store.at[2])
        last.start()
        last.wait()
        for one in started:
            one.wait_send()

    pl.run_scoped(
        dense_part,
        pltpu.VMEM((rows, width), f32), pltpu.VMEM((rows, width), bf16),
        pltpu.VMEM((rows, width), bf16), pltpu.VMEM((rows, width), bf16),
        pltpu.VMEM((rows, width), f32), pltpu.VMEM(probs_hbm.shape, bf16),
        pltpu.VMEM((rows, 3 * width), bf16), pltpu.VMEM((width, 3 * width), bf16),
        pltpu.VMEM((width, width), bf16), pltpu.VMEM((rows, slots), bf16),
        pltpu.VMEM((rows, width), f32), pltpu.VMEM((rows, width), bf16),
        pltpu.VMEM((rows, width), bf16), pltpu.VMEM((rows, width), f32),
        pltpu.VMEM((rows, 3 * width), bf16), pltpu.VMEM((width, rows), bf16),
        pltpu.VMEM((rows, PAIR), f32), pltpu.VMEM((rows, PAIR), f32),
        pltpu.VMEM((rows, width), bf16), pltpu.VMEM((width, rows), bf16),
    )
    for one in gv_copies + y_copies:
        one.wait_send()
    if ends:
        for i in range(9):
            if i not in (0, 3, 4):
                relay.landed(i)
            if i > 1:
                relay.sent(i)


def backward(
    groups, cap, copies, ends, per, act, gpre, w_in, w_down, experts, gates, h1, cot, tok, g1, g2, att,
    inv, probs, qkv, w_qkv, w_out, parts,
):
    slots, hidden = act.shape
    rows, width = tok.shape
    wide = 4 * width
    half = groups // 2
    thin = wide // copies
    sems = pltpu.SemaphoreType.DMA
    block = pltpu.VMEM((slots, width), bf16)
    tile = (8, width)
    up = (width // 4, hidden)
    down = (hidden // 4, width)
    land = [up, down, up, down, up, up, down, down, up] if ends else []
    pools = [up, up, down, up] if ends else []
    return pl.pallas_call(
        functools.partial(backward_kernel, groups, cap, copies, ends),
        out_shape=[
            jax.ShapeDtypeStruct((rows, width), bf16), jax.ShapeDtypeStruct((rows, width), bf16),
            jax.ShapeDtypeStruct((groups * per, thin), bf16), jax.ShapeDtypeStruct(tile, f32),
        ]
        + [jax.ShapeDtypeStruct(one, bf16) for one in land],
        in_specs=[ANY] * 4 + [VMEM] * 2 + [ANY] * 3 + [VMEM] * 2 + [ANY] * (6 + len(parts)),
        out_specs=[ANY] * 3 + [VMEM] + [ANY] * len(land),
        scratch_shapes=[
            block, block, block, block,
            pltpu.VMEM((groups * per, wide), bf16), pltpu.VMEM((half * per, wide), bf16),
            pltpu.VMEM((half, per, wide), bf16), pltpu.VMEM((copies, per, thin), bf16),
            pltpu.VMEM((copies, per, thin), bf16), pltpu.VMEM((per, thin), bf16),
            pltpu.VMEM((groups * per, thin), bf16), pltpu.VMEM(tile, f32), pltpu.VMEM(tile, f32),
            pltpu.VMEM((half, *tile), f32), pltpu.VMEM((2, *tile), f32),
            pltpu.VMEM((copies, *tile), f32), sems((9,)), sems((3,)), sems((groups,)),
            sems((groups,)), sems((groups,)), sems((groups,)), sems((3,)), sems((3,)),
            sems((3 * half,)), sems((3 * half,)), sems((copies,)), sems((copies,)), sems((groups,)),
            sems((groups,)), sems((half + copies,)), sems((half + copies,)), sems((9,)), sems((9,)),
            sems((2,)),
        ]
        + [pltpu.VMEM(one, bf16) for one in pools]
        + [pltpu.VMEM(one, bf16) for one in (up, down) if ends],
        compiler_params=pltpu.CompilerParams(
            collective_id=1, has_side_effects=True, vmem_limit_bytes=60 * MIB
        ),
        cost_estimate=pl.CostEstimate(
            flops=200 * 10**9, bytes_accessed=40 * 10**6, transcendentals=0
        ),
        name="backward",
    )(
        act, gpre, w_in, w_down, experts, gates, h1, cot, tok, g1, g2, att, inv, probs, qkv, w_qkv,
        w_out, *parts,
    )


def finish_kernel(*refs):
    (
        up_own, up_in, up_across, up_out, up_outward, down_own, down_in, down_across, down_out,
        down_outward, block, gtok, whole_ref, gains_ref, up_ref, down_ref, qkv_hbm, out_hbm, one_ref,
        two_ref, block_ref, gtok_ref, a, b, c, d, e, f, up, down, qkv_ref, out_ref,
        block_line, gtok_line, load, store,
    ) = refs
    dp = lax.axis_index("dp")
    outer = (dp == 0) | (dp == 3)
    inner = jnp.logical_not(outer)
    hand_in = [
        pltpu.make_async_copy(block, block_line, load.at[6]),
        pltpu.make_async_copy(gtok, gtok_line, load.at[7]),
    ]
    handed = [
        pltpu.make_async_copy(block_line, block_ref, store.at[0]),
        pltpu.make_async_copy(gtok_line, gtok_ref, store.at[1]),
    ]

    def loads(sources, targets):
        return [
            pltpu.make_async_copy(src, dst, load.at[i])
            for i, (src, dst) in enumerate(zip(sources, targets))
        ]

    inside = loads((up_own, up_in, up_across, down_own, down_in, down_across), (a, b, c, d, e, f))
    outside = loads((up_out, up_outward, down_out, down_outward), (a, b, d, e))

    @pl.when(inner)
    def _():
        for one in inside:
            one.start()

    @pl.when(outer)
    def _():
        for one in outside:
            one.start()

    for one in hand_in:
        one.start()

    def summed(target, goal, terms, first):
        part = target.shape[0] // 3
        lines = part // 4
        for piece in range(3):

            @pl.loop(0, 4)
            def _(r):
                at = rows_at(piece * part + r * lines, lines)
                total = terms[0][at].astype(f32)
                for term in terms[1:]:
                    total = total + term[at].astype(f32)
                target[at] = total

            out(target, goal, first, piece).start()

    def out(target, goal, first, piece):
        part = target.shape[0] // 3
        at = slice(piece * part, (piece + 1) * part)
        return pltpu.make_async_copy(target.at[at], goal.at[at], store.at[first + piece])

    @pl.when(inner)
    def _():
        for one in inside[:3]:
            one.wait()
        summed(up, up_ref, (a, b, c), 6)
        for one in inside[3:]:
            one.wait()
        summed(down, down_ref, (d, e, f), 9)

    @pl.when(outer)
    def _():
        for one in outside[:2]:
            one.wait()
        summed(up, up_ref, (a, b), 6)
        for one in outside[2:]:
            one.wait()
        summed(down, down_ref, (d, e), 9)

    thin = qkv_ref.shape[0]
    turned = whole_ref[...].astype(f32).T
    qkv_ref[...] = turned[:thin]
    out_ref[...] = turned[thin:]
    handed += [
        pltpu.make_async_copy(qkv_ref, qkv_hbm, store.at[4]),
        pltpu.make_async_copy(out_ref, out_hbm, store.at[5]),
    ]
    for one in hand_in:
        one.wait()
    for one in handed:
        one.start()
    size = one_ref.shape[1]
    for row, target in ((0, one_ref), (1, two_ref)):
        line = jnp.zeros((1, size), f32)
        for plane in range(4):
            part = gains_ref[row : row + 1, plane * size : (plane + 1) * size]
            line = jnp.where(dp == plane, part, line)
        target[...] = line
    for one in handed:
        one.wait()
    for piece in range(3):
        out(up, up_ref, 6, piece).wait()
        out(down, down_ref, 9, piece).wait()


def finish(ups, downs, block, gtok, whole, gains):
    up, down = ups[0].shape, downs[0].shape
    width = whole.shape[1]
    thin = width // 4
    sems = pltpu.SemaphoreType.DMA
    return pl.pallas_call(
        finish_kernel,
        out_shape=[
            jax.ShapeDtypeStruct(up, f32), jax.ShapeDtypeStruct(down, f32),
            jax.ShapeDtypeStruct((3 * thin, whole.shape[0]), f32),
            jax.ShapeDtypeStruct((thin, whole.shape[0]), f32),
            jax.ShapeDtypeStruct((1, thin), f32), jax.ShapeDtypeStruct((1, thin), f32),
            jax.ShapeDtypeStruct(block.shape, bf16), jax.ShapeDtypeStruct(gtok.shape, bf16),
        ],
        in_specs=[ANY] * 12 + [VMEM] * 2,
        out_specs=[ANY] * 4 + [VMEM] * 2 + [ANY] * 2,
        scratch_shapes=[pltpu.VMEM(up, bf16)] * 3
        + [pltpu.VMEM(down, bf16)] * 3
        + [
            pltpu.VMEM(up, f32), pltpu.VMEM(down, f32), pltpu.VMEM((3 * thin, whole.shape[0]), f32),
            pltpu.VMEM((thin, whole.shape[0]), f32), pltpu.VMEM(block.shape, bf16),
            pltpu.VMEM(gtok.shape, bf16), sems((8,)), sems((12,)),
        ],
        compiler_params=pltpu.CompilerParams(vmem_limit_bytes=60 * MIB),
        name="finish",
    )(*ups, *downs, block, gtok, whole, gains)


def shards(
    tokens, segment_ids, token_expert, gates, ln1_gain, w_qkv, w_out, ln2_gain, expert_in,
    expert_out, cotangent,
):
    rows, width = tokens.shape
    groups, copies = lax.axis_size("expert"), lax.axis_size("dp")
    cap = 2 * rows // groups
    per = -(-width // (16 * groups)) * 16
    w_in, w_down = expert_in[0], expert_out[0]
    experts, gate_row = token_expert.reshape(1, rows), gates.reshape(1, rows)
    ends = copies == 4
    h1, qkv, att, inv, probs, act, gpre, *parts = forward(
        groups, cap, ends, tokens, segment_ids, experts, gate_row, ln1_gain, w_qkv, w_out,
        ln2_gain, w_in, w_down, cotangent,
    )
    if ends:
        up_far, up_near, up_out, up_own, down_far, down_near, down_out, down_own, up_far_in = parts
        parts = [up_far, up_near, up_out, up_own, up_far_in, down_far, down_near, down_out, down_own]
    block_out, grad_tokens, whole, gains, *landed = backward(
        groups, cap, copies, ends, per, act, gpre, w_in, w_down, experts, gate_row, h1, cotangent,
        tokens, ln1_gain, ln2_gain, att, inv, probs, qkv, w_qkv, w_out, parts if ends else [],
    )
    if ends:
        _, down_own_in, up_own_in, _, _, up_across, down_across, down_outward, up_outward = landed
        up_share, down_share, share_qkv, share_out, share_one, share_two, block, gtok = finish(
            (up_own, up_own_in, up_across, up_out, up_outward),
            (down_own, down_own_in, down_across, down_out, down_outward),
            block_out, grad_tokens, whole[:width], gains,
        )
        return (
            block, gtok, share_one[0], share_qkv.T, share_out.T, share_two[0], up_share[None],
            down_share[None],
        )
    up_share, down_share = (
        lax.psum_scatter(one[None], "dp", scatter_dimension=1, tiled=True) for one in parts
    )
    whole = whole[:width].astype(f32)
    share = width // copies
    gains = lax.dynamic_slice_in_dim(gains, lax.axis_index("dp") * share, share, 1)
    return (
        block_out,
        grad_tokens,
        gains[0],
        whole[:, : 3 * share],
        whole[:, 3 * share :],
        gains[1],
        up_share.astype(f32),
        down_share.astype(f32),
    )


def solution(mesh):
    tokens, experts = P(("dp", "expert"), None), P("expert", None, None)
    return jax.shard_map(
        shards,
        mesh=mesh,
        in_specs=(
            tokens, tokens, tokens, P(("dp", "expert")), P(), P(), P(), P(), experts, experts,
            tokens,
        ),
        out_specs=(
            tokens, tokens, P("dp"), P(None, "dp"), P(None, "dp"), P("dp"),
            P("expert", "dp", None), P("expert", "dp", None),
        ),
        check_vma=False,
    )
```

```python
import functools

import jax
import jax.numpy as jnp
from jax import lax
from jax.experimental import pallas as pl
from jax.experimental.pallas import tpu as pltpu
from jax.sharding import PartitionSpec as P

HEAD_DIM = 64
EPSILON = 1e-05
NEG_LARGE = -1e30
BAND = 128
PAIR = 2 * HEAD_DIM
GROUP = 256
CHUNK = 512
MIB = 2**20
MESH = pl.DeviceIdType.MESH
ANY = pl.BlockSpec(memory_space=pl.ANY)
VMEM = pl.BlockSpec(memory_space=pltpu.VMEM)
f32, bf16 = jnp.float32, jnp.bfloat16


def dot(a, b):
    return jnp.dot(a, b, preferred_element_type=f32)


def dot_nt(a, b):
    return lax.dot_general(a, b, (((1,), (1,)), ((), ())), preferred_element_type=f32)


def dot_tn(a, b):
    return lax.dot_general(a, b, (((0,), (0,)), ((), ())), preferred_element_type=f32)


def flip(index, bits):
    place = 1
    while bits:
        if bits % 2:
            index = index + place * (1 - 2 * ((index // place) % 2))
        bits, place = bits // 2, place * 2
    return index


def add(a, b):
    return (a.astype(f32) + b.astype(f32)).astype(bf16)


def rows_at(start, size):
    return pl.ds(pl.multiple_of(start, size), size)


def greet(peers):
    barrier = pltpu.get_barrier_semaphore()
    for peer in peers:
        pl.semaphore_signal(barrier, inc=1, device_id=peer, device_id_type=MESH)
    pl.semaphore_wait(barrier, len(peers))


def sides(dp):
    side = dp // 2
    return flip(dp, 1), 3 - dp, [3 * (1 - side), 2 - side, 3 * side, 1 + side]


class Relay:
    def __init__(self, dp, me, moves, ssem, rsem):
        self.outer = (dp == 0) | (dp == 3)
        self.inner = jnp.logical_not(self.outer)
        beside, across, _ = sides(dp)
        self.moves = []
        for i, (kind, source, target) in enumerate(moves):
            plane = across if kind == "across" else beside
            copy = pltpu.make_async_remote_copy(
                src_ref=source, dst_ref=target, send_sem=ssem.at[i], recv_sem=rsem.at[i],
                device_id=(plane, me), device_id_type=MESH,
            )
            sender = self.outer if kind == "inward" else self.inner
            receiver = self.outer if kind == "outward" else self.inner
            self.moves.append((copy, sender, receiver))

    def start(self, *which):
        for i in which:
            copy, sender, _ = self.moves[i]
            pl.when(sender)(copy.start)

    def sent(self, i):
        pl.when(self.moves[i][1])(self.moves[i][0].wait_send)

    def landed(self, i):
        pl.when(self.moves[i][2])(self.moves[i][0].wait_recv)

    def merged(self, first, second, total, spare, sem):
        @pl.when(self.inner)
        def _():
            loads = [
                pltpu.make_async_copy(first, total, sem.at[0]),
                pltpu.make_async_copy(second, spare, sem.at[1]),
            ]
            for one in loads:
                one.start()
            for one in loads:
                one.wait()
            lines = total.shape[0] // 12

            @pl.loop(0, 12)
            def _(r):
                at = rows_at(r * lines, lines)
                total[at] = add(total[at], spare[at])


def band(index):
    first = max(0, index - 2) * BAND
    return first, (index + 1) * BAND - first


def column_of(row):
    size = row.shape[1]
    eye = lax.broadcasted_iota(jnp.int32, (size, size), 0) == lax.broadcasted_iota(
        jnp.int32, (size, size), 1
    )
    return jnp.sum(jnp.where(eye, row, 0.0), axis=1, keepdims=True)


def slot_row(experts, num_experts, capacity):
    rows = experts.shape[1]
    lines = max(16, num_experts)
    onehot = lax.broadcasted_iota(jnp.int32, (lines, rows), 0) == experts
    onehot = jnp.where(onehot, 1.0, 0.0)
    before = lax.broadcasted_iota(jnp.int32, (rows, rows), 0) < lax.broadcasted_iota(
        jnp.int32, (rows, rows), 1
    )
    earlier = dot(onehot.astype(bf16), jnp.where(before, 1.0, 0.0).astype(bf16))
    rank = jnp.sum(onehot * earlier, axis=0, keepdims=True)
    return experts.astype(f32) * float(capacity) + rank


def centred(hidden):
    centre = hidden - jnp.mean(hidden, axis=-1, keepdims=True)
    spread = jnp.mean(centre * centre, axis=-1, keepdims=True)
    return centre, lax.rsqrt(spread + EPSILON)


def gelu_pair(x):
    bell = jnp.exp2((-0.5 * 1.4426950408889634) * (x * x))
    phi = 0.5 + 0.5 * lax.erf(x * 0.7071067811865476)
    return x * phi, phi + x * (bell * 0.3989422804014327)


def gelu(x):
    return gelu_pair(x)[0]


def forward_kernel(groups, cap, ends, *refs):
    (
        tok_hbm, seg_ref, te_ref, gate_ref, g1_ref, wqkv_hbm, wout_hbm, g2_ref, win_hbm, wdown_hbm,
        cot_hbm, h1_out, qkv_out, att_out, inv_out, probs_out, act_out, gpre_out,
    ) = refs[:18]
    count = 4 if ends else 1
    ups, downs = refs[18 : 18 + count], refs[18 + count : 18 + 2 * count]
    up_land = refs[18 + 2 * count : 18 + 2 * count + ends]
    (
        tok, cot, win, wdown, low, h1, place, sent, gy_send, gy_got, v_got, gy_low, spot_own, gy_line,
        v_line, spot_far, place_far, gy_fsend, far_send, gy_far, v_far, act,
        gpre, load, store, act_store, gpre_store, gy_ssem, gy_rsem, v_ssem, v_rsem, gy_fssem,
        gy_frsem, v_fssem, v_frsem, line_ssem, line_rsem, rel_s, rel_r,
    ) = refs[18 + 2 * count + ends :]
    dp, me = lax.axis_index("dp"), lax.axis_index("expert")
    rows, width = tok.shape
    slots, hidden = act.shape
    pairs = width // PAIR
    outer = (dp == 0) | (dp == 3)
    inner = jnp.logical_not(outer)
    first_loads = [
        pltpu.make_async_copy(src, dst, load.at[i])
        for i, (src, dst) in enumerate(
            ((cot_hbm, cot), (tok_hbm, tok), (win_hbm, win), (wdown_hbm, wdown))
        )
    ]
    first_loads[0].start()
    first_loads[1].start()
    beside = [(flip(dp, 1), me)] if ends else []
    greet([(dp, flip(me, k)) for k in range(1, groups)] + beside)

    def exchange(source, target, send, receive, k):
        peer = flip(me, k)
        return pltpu.make_async_remote_copy(
            src_ref=source.at[rows_at(peer * cap, cap)],
            dst_ref=target.at[rows_at(me * cap, cap)],
            send_sem=send.at[k],
            recv_sem=receive.at[k],
            device_id=(dp, peer),
            device_id_type=MESH,
        )

    gy_copies = [exchange(gy_send, gy_got, gy_ssem, gy_rsem, k) for k in range(1, groups)]
    v_copies = [exchange(sent, v_got, v_ssem, v_rsem, k) for k in range(1, groups)]
    far_groups = groups if ends else 0
    gy_fars = [exchange(gy_fsend, gy_far, gy_fssem, gy_frsem, k) for k in range(1, far_groups)]
    v_fars = [exchange(far_send, v_far, v_fssem, v_frsem, k) for k in range(1, far_groups)]
    lines = ends and [
        pltpu.make_async_remote_copy(
            src_ref=source, dst_ref=target, send_sem=line_ssem.at[i], recv_sem=line_rsem.at[i],
            device_id=(flip(dp, 1), me), device_id_type=MESH,
        )
        for i, (source, target) in enumerate(
            ((spot_own, spot_far), (gy_low, gy_line), (low, v_line))
        )
    ]

    def when(condition, action):
        if ends:
            pl.when(condition)(action)

    def positions(spot, target):
        @pl.loop(0, slots // GROUP)
        def _(g):
            here = lax.broadcasted_iota(jnp.int32, (GROUP, rows), 0) + g * GROUP
            there = jnp.where(here.astype(f32) == spot, 1.0, 0.0)
            target[rows_at(g * GROUP, GROUP)] = there.astype(bf16)

    def placed(where, line, target):
        @pl.loop(0, width // GROUP)
        def _(n):
            cols = rows_at(n * GROUP, GROUP)
            target[:, cols] = dot(where[...], line[:, cols]).astype(bf16)

    def far_gy():
        lines[0].wait_recv()
        lines[1].wait_recv()
        positions(spot_far[0:1], place_far)
        placed(place_far, gy_line, gy_fsend)
        for one in gy_fars:
            one.start()
        gy_far[mine] = gy_fsend[mine]

    def far_v():
        lines[2].wait_recv()
        placed(place_far, v_line, far_send)
        for one in v_fars:
            one.start()
        v_far[mine] = far_send[mine]

    mine = rows_at(me * cap, cap)

    def attention(wqkv, wout, qkv, att, inv, probs, bias):
        loads = [
            pltpu.make_async_copy(wqkv_hbm, wqkv, load.at[4]),
            pltpu.make_async_copy(wout_hbm, wout, load.at[5]),
        ]
        for one in loads + first_loads[2:]:
            one.start()
        spot = slot_row(te_ref[...], groups, cap)

        positions(spot, place)
        first_loads[0].wait()
        gate = column_of(gate_ref[...])
        gy_low[...] = (gate * cot[...].astype(f32)).astype(bf16)
        if ends:
            spot_own[...] = jnp.broadcast_to(spot, spot_own.shape)

            @pl.when(outer)
            def _():
                lines[0].start()
                lines[1].start()

        placed(place, gy_low, gy_send)
        for one in gy_copies:
            one.start()
        gy_got[mine] = gy_send[mine]
        segs = seg_ref[...].astype(f32)
        seg_col = column_of(segs)
        for i in range(rows // BAND):
            first, wide = band(i)
            causal = (lax.broadcasted_iota(jnp.int32, (BAND, wide), 0) + i * BAND) >= (
                lax.broadcasted_iota(jnp.int32, (BAND, wide), 1) + first
            )
            same = seg_col[i * BAND : (i + 1) * BAND] == segs[:, first : first + wide]
            bias[i * BAND : (i + 1) * BAND, 0:wide] = jnp.where(causal & same, 0.0, NEG_LARGE)

        first_loads[1].wait()

        @pl.loop(0, rows // BAND)
        def _(r):
            at = rows_at(r * BAND, BAND)
            centre, inverse = centred(tok[at].astype(f32))
            low[at] = (centre * inverse * g1_ref[...].reshape(1, width)).astype(bf16)

        loads[0].wait()

        @pl.loop(0, 3 * width // GROUP)
        def _(c):
            at = rows_at(c * GROUP, GROUP)
            qkv[:, at] = dot(low[...], wqkv[:, at]).astype(bf16)

        left = lax.broadcasted_iota(jnp.int32, (1, PAIR), 1) < HEAD_DIM
        none, unit = jnp.zeros((), bf16), jnp.ones((), bf16)

        def attend(h):
            at = rows_at(h * PAIR, PAIR)
            k_at = rows_at(width + h * PAIR, PAIR)
            v_at = rows_at(2 * width + h * PAIR, PAIR)
            for i in range(rows // BAND):
                first, wide = band(i)
                here = slice(i * BAND, (i + 1) * BAND)
                keys = qkv[first : first + wide, k_at]
                values = qkv[first : first + wide, v_at]
                query = qkv[here, at] * jnp.asarray(HEAD_DIM**-0.5, bf16)
                query = jnp.concatenate(
                    [jnp.where(left, query, none), jnp.where(left, none, query)], axis=0
                )
                scores = dot_nt(query, keys).reshape(2, BAND, wide) + bias[here, 0:wide][None]
                weights = jnp.exp(scores - jnp.max(scores, axis=-1, keepdims=True)).astype(bf16)
                probs[h, 2 * i * BAND : 2 * (i + 1) * BAND, 0:wide] = weights.reshape(
                    2 * BAND, wide
                )
                one = dot(weights[0], jnp.where(left, values, unit))
                two = dot(weights[1], jnp.where(left, unit, values))
                scale = 1.0 / pltpu.roll(jnp.where(left, two, one), HEAD_DIM, 1)
                inv[here, at] = scale
                att[here, at] = (jnp.where(left, one, two) * scale).astype(bf16)

        pl.loop(0, pairs)(attend)
        stores = [
            pltpu.make_async_copy(src, dst, store.at[i])
            for i, (src, dst) in enumerate(
                ((qkv, qkv_out), (probs, probs_out), (att, att_out), (inv, inv_out))
            )
        ]
        for one in stores:
            one.start()
        loads[1].wait()

        @pl.loop(0, width // GROUP)
        def _(n):
            cols = rows_at(n * GROUP, GROUP)
            h1[:, cols] = dot(att[...], wout[:, cols])

        @pl.loop(0, rows // BAND)
        def _(r):
            at = rows_at(r * BAND, BAND)
            resid = tok[at].astype(f32) + h1[at]
            h1[at] = resid
            centre, inverse = centred(resid)
            low[at] = (centre * inverse * g2_ref[...].reshape(1, width)).astype(bf16)

        when(outer, lambda: lines[2].start())

        placed(place, low, sent)
        for one in v_copies:
            one.start()
        v_got[mine] = sent[mine]
        for one in stores:
            one.wait()

    pl.run_scoped(
        attention,
        pltpu.VMEM((width, 3 * width), bf16), pltpu.VMEM((width, width), bf16),
        pltpu.VMEM((rows, 3 * width), bf16), pltpu.VMEM((rows, width), bf16),
        pltpu.VMEM((rows, width), f32), pltpu.VMEM((pairs, 2 * rows, 3 * BAND), bf16),
        pltpu.VMEM((rows, 3 * BAND), f32),
    )

    def experts(act_far, gdown, gup, turned):
        stores = [pltpu.make_async_copy(h1, h1_out, store.at[4])]
        stores[0].start()
        for one in first_loads[2:]:
            one.wait()
        for one in gy_copies:
            one.wait_recv()

        @pl.loop(0, hidden // GROUP)
        def _(c):
            at = rows_at(c * GROUP, GROUP)
            gpre[:, at] = dot_nt(gy_got[...], wdown[at]).astype(bf16)

        many = GROUP // cap
        for g in range(slots // GROUP):
            for k in range(g * many, (g + 1) * many):
                if k:
                    v_copies[k - 1].wait_recv()
            at = rows_at(flip(me // many, g) * GROUP, GROUP)

            @pl.loop(0, hidden // CHUNK)
            def _(c):
                cols = rows_at(c * CHUNK, CHUNK)
                value, back = gelu_pair(dot(v_got[at], win[:, cols]))
                act[at, cols] = value.astype(bf16)
                gpre[at, cols] = (gpre[at, cols].astype(f32) * back).astype(bf16)

            for source, target, sem in ((act, act_out, act_store), (gpre, gpre_out, gpre_store)):
                stores.append(pltpu.make_async_copy(source.at[at], target.at[at], sem.at[g]))
                stores[-1].start()
            if g == 0:
                when(inner, far_gy)
            if g == 1:
                when(inner, far_v)

        turned[...] = v_got[...].T

        @pl.loop(0, hidden // GROUP)
        def _(c):
            cols = rows_at(c * GROUP, GROUP)
            gup[:, cols] = dot(turned[...], gpre[:, cols]).astype(bf16)

        shares = sides(dp)[2] if ends else [0]
        size, share = width // count, hidden // count
        for i, (one, part) in enumerate(zip(shares, ups)):
            source = gup.at[rows_at(one * size, size)]
            stores.append(pltpu.make_async_copy(source, part, store.at[5 + i]))
            stores[-1].start()
        if ends:
            relay = Relay(
                dp, me, [("inward", gup.at[rows_at(shares[0] * size, size)], up_land[0])],
                rel_s, rel_r,
            )
            relay.start(0)

        def down(kept, shared):
            for i in kept:

                @pl.loop(0, share // GROUP)
                def _(c):
                    cols = pl.ds(pl.multiple_of(shares[i] * share + c * GROUP, GROUP), GROUP)
                    at = pl.ds(pl.multiple_of(i * share + c * GROUP, GROUP), GROUP)
                    if shared:
                        total = gdown[at].astype(f32) + dot_tn(act_far[:, at], gy_far[...])
                    else:
                        total = dot_tn(act[:, cols], gy_got[...])
                    gdown[at] = total.astype(bf16)

        def leave(kept):
            for i in kept:
                at = slice(i * share, (i + 1) * share)
                pltpu.make_async_copy(gdown.at[at], downs[i], store.at[9 + i]).start()

        def taken(kept):
            for i in kept:
                at = slice(i * share, (i + 1) * share)
                pltpu.make_async_copy(gdown.at[at], downs[i], store.at[9 + i]).wait()

        def inside():
            down([0, 1], False)
            for g in range(slots // GROUP):
                for k in range(g * many, (g + 1) * many):
                    if k:
                        v_fars[k - 1].wait_recv()
                at = rows_at(flip(me // many, g) * GROUP, GROUP)
                for i in range(2):

                    @pl.loop(0, 2)
                    def _(c):
                        cols = pl.ds(pl.multiple_of(shares[i] * share + c * (share // 2), 128), share // 2)
                        kept = pl.ds(pl.multiple_of(i * share + c * (share // 2), 128), share // 2)
                        act_far[at, kept] = gelu(dot(v_far[at], win[:, cols])).astype(bf16)

            for one in gy_fars:
                one.wait_recv()
            down([0, 1], True)
            leave([0, 1])
            for one in gy_fars + v_fars:
                one.wait_send()
            taken([0, 1])

        down([2, 3] if ends else [0], False)
        leave([2, 3] if ends else [0])
        if ends:
            pl.when(inner)(inside)

            @pl.when(outer)
            def _():
                for one in lines:
                    one.wait_send()

        taken([2, 3] if ends else [0])
        for one in gy_copies + v_copies:
            one.wait_send()
        for one in stores:
            one.wait()
        if ends:
            relay.landed(0)
            relay.sent(0)

    pl.run_scoped(
        experts,
        pltpu.VMEM((slots, hidden // 2) if ends else (16, 128), bf16),
        pltpu.VMEM((hidden, width), bf16), pltpu.VMEM((width, hidden), bf16),
        pltpu.VMEM((width, slots), bf16),
    )


def forward(groups, cap, ends, tokens, segs, experts, gates, g1, w_qkv, w_out, g2, w_in, w_down, cot):
    rows, width = tokens.shape
    hidden = w_in.shape[1]
    slots = groups * cap
    pairs = width // PAIR
    wide = 3 * BAND
    count = 4 if ends else 1
    parts = [(width // count, hidden)] * count + [(hidden // count, width)] * count
    parts += [(width // count, hidden)] * ends
    shapes = [
        ((rows, width), f32), ((rows, 3 * width), bf16), ((rows, width), bf16), ((rows, width), f32),
        ((pairs, 2 * rows, wide), bf16), ((slots, hidden), bf16), ((slots, hidden), bf16),
    ] + [(one, bf16) for one in parts]
    sems = pltpu.SemaphoreType.DMA
    lines = pltpu.VMEM((rows, width), bf16)
    block = pltpu.VMEM((slots, width), bf16)
    tiny = (16, 128)
    far = block if ends else pltpu.VMEM(tiny, bf16)
    far_line = lines if ends else pltpu.VMEM(tiny, bf16)
    return pl.pallas_call(
        functools.partial(forward_kernel, groups, cap, int(ends)),
        out_shape=[jax.ShapeDtypeStruct(*one) for one in shapes],
        in_specs=[ANY, VMEM, VMEM, VMEM, VMEM, ANY, ANY, VMEM, ANY, ANY, ANY],
        out_specs=[ANY] * len(shapes),
        scratch_shapes=[
            lines, lines, pltpu.VMEM(w_in.shape, bf16), pltpu.VMEM(w_down.shape, bf16), lines,
            pltpu.VMEM((rows, width), f32), pltpu.VMEM((slots, rows), bf16), block, block, block,
            block, lines, pltpu.VMEM((8, rows), f32), far_line, far_line, pltpu.VMEM((8, rows), f32),
            pltpu.VMEM((slots, rows) if ends else tiny, bf16), far, far, far, far,
            pltpu.VMEM((slots, hidden), bf16), pltpu.VMEM((slots, hidden), bf16),
            sems((6,)), sems((13,)), sems((slots // GROUP,)), sems((slots // GROUP,)),
        ]
        + [sems((groups,))] * 8
        + [sems((3,))] * 2
        + [sems((1,))] * 2,
        compiler_params=pltpu.CompilerParams(
            collective_id=0, has_side_effects=True, vmem_limit_bytes=60 * MIB
        ),
        cost_estimate=pl.CostEstimate(
            flops=200 * 10**9, bytes_accessed=40 * 10**6, transcendentals=10**7
        ),
        name="forward",
    )(tokens, segs, experts, gates, g1, w_qkv, w_out, g2, w_in, w_down, cot)


def backward_kernel(groups, cap, copies, ends, *refs):
    (
        act_hbm, gpre_hbm, win_hbm, wdown_hbm, te_ref, gate_ref, h1_hbm, cot_hbm, tok_hbm, g1_ref,
        g2_ref, att_hbm, inv_hbm, probs_hbm, qkv_hbm, wqkv_hbm, wout_hbm,
    ) = refs[:17]
    parts, refs = refs[17 : 17 + 9 * ends], refs[17 + 9 * ends :]
    block_out, gtok_out, whole_out, total_ref = refs[:4]
    landed, refs = refs[4 : 4 + 9 * ends], refs[4 + 9 * ends :]
    (
        gv_send, gvr, y_send, yr, dense, other, got, ring, ring_got, final, whole, gains_ref,
        gains_pair, gains_chip, gains_part, gains_ring, load, store, gv_ssem, gv_rsem, y_ssem, y_rsem,
        s_pair, r_pair, s_chip, r_chip, s_ring, r_ring, s_out, r_out, s_gain, r_gain, rel_s, rel_r,
        pool_sem, *pools,
    ) = refs
    dp, me = lax.axis_index("dp"), lax.axis_index("expert")
    slots, width = gvr.shape
    rows, hidden = tok_hbm.shape[0], win_hbm.shape[1]
    rounds = [lax.rem(dp + k, copies) for k in range(copies)]
    half = groups // 2
    per, wide = got.shape[1:]
    many = CHUNK // cap
    mine = rows_at(me * cap, cap)

    def exchange(source, target, ssem, rsem):
        return [
            pltpu.make_async_remote_copy(
                src_ref=source.at[rows_at(flip(me, k) * cap, cap)],
                dst_ref=target.at[rows_at(me * cap, cap)],
                send_sem=ssem.at[k],
                recv_sem=rsem.at[k],
                device_id=(dp, flip(me, k)),
                device_id_type=MESH,
            )
            for k in range(1, groups)
        ]

    gv_copies = exchange(gv_send, gvr, gv_ssem, gv_rsem)
    y_copies = exchange(y_send, yr, y_ssem, y_rsem)
    relay = None
    if ends:
        up_far, up_near, up_out, up_own, up_far_in, down_far, down_near, down_out, down_own = parts
        relay = Relay(
            dp, me,
            [
                ("inward", up_near, landed[0]), ("inward", down_own, landed[1]),
                ("inward", up_own, landed[2]), ("across", down_far, landed[3]),
                ("across", pools[0], landed[4]), ("across", pools[1], landed[5]),
                ("across", down_near, landed[6]), ("outward", pools[2], landed[7]),
                ("outward", pools[3], landed[8]),
            ],
            rel_s, rel_r,
        )

    chip, core = me // 2, me % 2
    there = flip(me, 1)
    chips = [flip(chip, k) for k in range(half)]
    started = []
    sets = [(0, width), (width, 3 * width // 2), (5 * width // 2, 3 * width // 2)]
    pair, far = {}, {}

    def send(source, target, ssem, rsem, device):
        return pltpu.make_async_remote_copy(
            src_ref=source, dst_ref=target, send_sem=ssem, recv_sem=rsem, device_id=device,
            device_id_type=MESH,
        )

    def go(copy):
        copy.start()
        started.append(copy)
        return copy

    def pair_send(i):
        cols = slice(sets[i][0], sum(sets[i]))
        pair[i] = go(
            send(
                dense.at[rows_at((1 - core) * (half * per), half * per), cols], other.at[:, cols],
                s_pair.at[i], r_pair.at[i], (dp, there),
            )
        )

    def combine(i):
        cols = slice(sets[i][0], sum(sets[i]))
        pair[i].wait_recv()
        for k in range(half - 1, -1, -1):
            at = rows_at(chips[k] * per, per)
            own = rows_at((core * half + chips[k]) * per, per)
            other[at, cols] = add(dense[own, cols], other[at, cols])
            if k:
                far[i, k] = go(
                    send(
                        other.at[at, cols], got.at[k, :, cols], s_chip.at[3 * k + i],
                        r_chip.at[3 * k + i], (dp, chips[k] * 2 + core),
                    )
                )

    def first():
        if ends:
            relay.start(0, 3)

    def between():
        if ends:
            relay.merged(up_far, up_far_in, pools[0], pools[4], pool_sem)
            relay.start(4)

    def second():
        if ends:
            relay.sent(0)
            relay.start(1)
            relay.landed(0)
            relay.merged(up_near, landed[0], pools[1], pools[4], pool_sem)
            relay.start(5)
            relay.landed(3)
            relay.merged(down_out, landed[3], pools[2], pools[5], pool_sem)
            relay.start(7)

    def third():
        if ends:
            relay.sent(1)
            relay.start(2)

    def outward():
        if ends:
            relay.landed(4)
            relay.merged(up_out, landed[4], pools[3], pools[4], pool_sem)
            relay.start(8)

    def fourth():
        if ends:
            relay.start(6)

    def experts(act, gpre, win, wdown):
        loads = [
            pltpu.make_async_copy(src, dst, load.at[i])
            for i, (src, dst) in enumerate(
                ((win_hbm, win), (gpre_hbm, gpre), (wdown_hbm, wdown), (act_hbm, act))
            )
        ]
        for one in loads:
            one.start()
        greet(
            [(dp, flip(me, k)) for k in range(1, groups)] + [(one, me) for one in rounds[1:]]
        )
        first()
        for one in loads[:2]:
            one.wait()
        for g in range(slots // CHUNK - 1, -1, -1):
            at = rows_at(flip(me // many, g) * CHUNK, CHUNK)

            @pl.loop(0, width // GROUP)
            def _(n):
                cols = rows_at(n * GROUP, GROUP)
                gv_send[at, cols] = dot_nt(gpre[at], win[cols]).astype(bf16)

            for k in range(g * many, (g + 1) * many):
                if k:
                    gv_copies[k - 1].start()
        gvr[mine] = gv_send[mine]
        for one in loads[2:]:
            one.wait()

        @pl.loop(0, width // GROUP)
        def _(n):
            cols = rows_at(n * GROUP, GROUP)
            y_send[:, cols] = dot(act[...], wdown[:, cols]).astype(bf16)

        between()

    pl.run_scoped(
        experts,
        pltpu.VMEM((slots, hidden), bf16), pltpu.VMEM((slots, hidden), bf16),
        pltpu.VMEM((width, hidden), bf16), pltpu.VMEM((hidden, width), bf16),
    )

    def dense_part(
        h1, cot, tok, att, inv, probs, qkv, wqkv, wout, place, gh1, low, gatt, inner_sum, gqkv,
        turned, gk, gvv, outv, lines,
    ):
        loads = [
            pltpu.make_async_copy(src, dst, load.at[i])
            for i, (src, dst) in enumerate(
                (
                    (h1_hbm, h1), (cot_hbm, cot), (att_hbm, att), (wout_hbm, wout), (inv_hbm, inv),
                    (qkv_hbm, qkv), (probs_hbm, probs), (tok_hbm, tok), (wqkv_hbm, wqkv),
                )
            )
        ]
        loads[7].start()
        for i in (0, 1, 2, 3, 4, 5, 6, 8):
            loads[i].start()
        spot = column_of(slot_row(te_ref[...], groups, cap))
        for r in range(rows // BAND):
            at = slice(r * BAND, (r + 1) * BAND)
            here = lax.broadcasted_iota(jnp.int32, (BAND, slots), 1).astype(f32)
            place[at] = jnp.where(here == spot[at], 1.0, 0.0).astype(bf16)
        gate = column_of(gate_ref[...])
        gains_ref[...] = jnp.zeros_like(gains_ref)
        loads[7].wait()
        for r in range(rows // BAND):
            at = slice(r * BAND, (r + 1) * BAND)
            centre, inverse = centred(tok[at].astype(f32))
            outv[at] = (centre * inverse * g1_ref[...].reshape(1, width)).astype(bf16)
        lines[...] = outv[...].T
        for one in gv_copies:
            one.wait_recv()
        for i in range(2):
            loads[i].wait()

        @pl.loop(0, width // GROUP)
        def _(n):
            cols = rows_at(n * GROUP, GROUP)
            gh1[:, cols] = dot(place[...], gvr[:, cols])

        for r in range(rows // BAND):
            at = slice(r * BAND, (r + 1) * BAND)
            back = gh1[at]
            resid = h1[at]
            centre, inverse = centred(resid)
            unit = centre * inverse
            gains_ref[1:2] += jnp.sum(back * unit, axis=0, keepdims=True)
            slant = back * g2_ref[...].reshape(1, width)
            inner = slant - jnp.mean(slant, axis=-1, keepdims=True)
            inner = inner - unit * jnp.mean(slant * unit, axis=-1, keepdims=True)
            grad = cot[at].astype(f32) + inverse * inner
            gh1[at] = grad
            low[at] = grad.astype(bf16)
        for i in range(2, 5):
            loads[i].wait()

        @pl.loop(0, width // GROUP)
        def _(n):
            cols = rows_at(n * GROUP, GROUP)
            grad = dot_nt(low[...], wout[cols]) * inv[:, cols]
            gatt[:, cols] = grad.astype(bf16)
            inner_sum[:, cols] = grad * att[:, cols].astype(f32) * HEAD_DIM**-0.5

        turned[...] = att[...].T

        @pl.loop(0, width // GROUP)
        def _(n):
            cols = rows_at(n * GROUP, GROUP)
            dense[0:width, cols] = dot(turned[...], low[:, cols]).astype(bf16)

        pair_send(0)
        second()
        loads[5].wait()
        loads[6].wait()
        left = lax.broadcasted_iota(jnp.int32, (1, PAIR), 1) < HEAD_DIM
        none = jnp.zeros((), bf16)

        def halves(block):
            return jnp.concatenate([jnp.where(left, block, none), jnp.where(left, none, block)], axis=0)

        def attend(h):
            at = rows_at(h * PAIR, PAIR)
            k_at = rows_at(width + h * PAIR, PAIR)
            v_at = rows_at(2 * width + h * PAIR, PAIR)
            gk[...] = jnp.zeros_like(gk)
            gvv[...] = jnp.zeros_like(gvv)
            for i in range(rows // BAND):
                first, wide = band(i)
                mine, seen = slice(i * BAND, (i + 1) * BAND), slice(first, first + wide)
                keys = qkv[seen, k_at]
                values = qkv[seen, v_at] * jnp.asarray(HEAD_DIM**-0.5, bf16)
                query, grad = halves(qkv[mine, at]), halves(gatt[mine, at])
                share = probs[h, 2 * i * BAND : 2 * (i + 1) * BAND, 0:wide]
                inner = inner_sum[mine, at]
                middle = jnp.concatenate(
                    [
                        jnp.sum(jnp.where(left, inner, 0.0), axis=-1, keepdims=True),
                        jnp.sum(jnp.where(left, 0.0, inner), axis=-1, keepdims=True),
                    ],
                    axis=0,
                )
                graw = (share.astype(f32) * (dot_nt(grad, values) - middle)).astype(bf16)
                gquery = dot(graw, keys)
                gqkv[mine, at] = jnp.where(left, gquery[0:BAND], gquery[BAND:]).astype(bf16)
                gk[seen] += dot_tn(graw, query)
                gvv[seen] += dot_tn(share, grad)
            gqkv[:, k_at] = gk[...].astype(bf16)
            gqkv[:, v_at] = gvv[...].astype(bf16)
        heads = width // PAIR // 2
        for part in range(2):
            pl.loop(part * heads, (part + 1) * heads)(attend)
            for i in range(3):
                source = i * width + part * heads * PAIR
                target = width + (3 * part + i) * heads * PAIR
                dense[0:width, target : target + heads * PAIR] = dot(
                    lines[...], gqkv[:, source : source + heads * PAIR]
                ).astype(bf16)
            pair_send(part + 1)
            combine(part)
        loads[8].wait()

        def rest():
            @pl.loop(0, width // GROUP)
            def _(n):
                cols = rows_at(n * GROUP, GROUP)
                inner_sum[:, cols] = dot_nt(gqkv[...], wqkv[cols])

            for r in range(rows // BAND):
                at = slice(r * BAND, (r + 1) * BAND)
                back = inner_sum[at]
                centre, inverse = centred(tok[at].astype(f32))
                unit = centre * inverse
                gains_ref[0:1] += jnp.sum(back * unit, axis=0, keepdims=True)
                slant = back * g1_ref[...].reshape(1, width)
                inner = slant - jnp.mean(slant, axis=-1, keepdims=True)
                inner = inner - unit * jnp.mean(slant * unit, axis=-1, keepdims=True)
                outv[at] = (gh1[at] + inverse * inner).astype(bf16)
            pltpu.make_async_copy(outv, gtok_out, store.at[0]).start()

        def y_part():
            for one in y_copies:
                one.wait_recv()

            @pl.loop(0, width // GROUP)
            def _(n):
                cols = rows_at(n * GROUP, GROUP)
                low[:, cols] = (h1[:, cols] + gate * dot(place[...], yr[:, cols])).astype(bf16)

            out_one = pltpu.make_async_copy(low, block_out, store.at[1])
            out_one.start()
            out_one.wait()
            pltpu.make_async_copy(outv, gtok_out, store.at[0]).wait()

        combine(2)
        rest()
        dense_sums(y_part)

    def dense_sums(y_part):
        gain_pair = go(send(gains_ref, gains_pair, s_gain.at[0], r_gain.at[0], (dp, there)))
        third()
        gain_pair.wait_recv()
        gains_part[0] = gains_ref[...] + gains_pair[...]
        gain_far = [
            go(
                send(
                    gains_part.at[0], gains_chip.at[k], s_gain.at[k], r_gain.at[k],
                    (dp, chips[k] * 2 + core),
                )
            )
            for k in range(1, half)
        ]
        total = other[rows_at(chip * per, per)].astype(f32)
        for k in range(1, half):
            for i in range(3):
                far[i, k].wait_recv()
            total = total + got[k].astype(f32)
        share = 3 * width // copies
        thin = width // copies
        part = width // 2
        thirds = jnp.concatenate(
            [
                total[:, width + (3 * j + i) * part : width + (3 * j + i + 1) * part]
                for i in range(3)
                for j in range(2)
            ],
            axis=1,
        )
        for d in range(copies):
            ring[d] = jnp.concatenate(
                [thirds[:, d * share : (d + 1) * share], total[:, d * thin : (d + 1) * thin]],
                axis=1,
            ).astype(bf16)
        around = [
            go(send(ring.at[rounds[k]], ring_got.at[k], s_ring.at[k], r_ring.at[k], (rounds[k], me)))
            for k in range(1, copies)
        ]
        outward()
        for one in y_copies:
            one.start()
        yr[mine] = y_send[mine]
        gains = gains_part[0]
        for k in range(1, half):
            gain_far[k - 1].wait_recv()
            gains = gains + gains_chip[k]
        gains_part[1] = gains
        gain_around = [
            go(
                send(
                    gains_part.at[1], gains_ring.at[k], s_gain.at[half + k], r_gain.at[half + k],
                    (rounds[k], me),
                )
            )
            for k in range(1, copies)
        ]
        summed = ring[dp].astype(f32)
        for k in range(1, copies):
            around[k - 1].wait_recv()
            summed = summed + ring_got[k].astype(f32)
        fourth()
        place = rows_at((core * half + chip) * per, per)
        final[...] = summed.astype(bf16)
        whole[place] = final[...]
        spread = [
            go(
                send(
                    final, whole.at[place], s_out.at[k], r_out.at[k], (dp, chips[k] * 2 + core)
                )
            )
            for k in range(half - 1, 0, -1)
        ]
        y_part()
        for k in range(1, copies):
            gain_around[k - 1].wait_recv()
            gains = gains + gains_ring[k]
        total_ref[...] = gains
        for one in spread:
            one.wait_recv()
        ours = whole.at[rows_at(core * (half * per), half * per)]
        go(send(ours, ours, s_out.at[0], r_out.at[0], (dp, there))).wait_recv()
        last = pltpu.make_async_copy(whole, whole_out, store.at[2])
        last.start()
        last.wait()
        for one in started:
            one.wait_send()

    pl.run_scoped(
        dense_part,
        pltpu.VMEM((rows, width), f32), pltpu.VMEM((rows, width), bf16),
        pltpu.VMEM((rows, width), bf16), pltpu.VMEM((rows, width), bf16),
        pltpu.VMEM((rows, width), f32), pltpu.VMEM(probs_hbm.shape, bf16),
        pltpu.VMEM((rows, 3 * width), bf16), pltpu.VMEM((width, 3 * width), bf16),
        pltpu.VMEM((width, width), bf16), pltpu.VMEM((rows, slots), bf16),
        pltpu.VMEM((rows, width), f32), pltpu.VMEM((rows, width), bf16),
        pltpu.VMEM((rows, width), bf16), pltpu.VMEM((rows, width), f32),
        pltpu.VMEM((rows, 3 * width), bf16), pltpu.VMEM((width, rows), bf16),
        pltpu.VMEM((rows, PAIR), f32), pltpu.VMEM((rows, PAIR), f32),
        pltpu.VMEM((rows, width), bf16), pltpu.VMEM((width, rows), bf16),
    )
    for one in gv_copies + y_copies:
        one.wait_send()
    if ends:
        for i in range(9):
            if i not in (0, 3, 4):
                relay.landed(i)
            if i > 1:
                relay.sent(i)


def backward(
    groups, cap, copies, ends, per, act, gpre, w_in, w_down, experts, gates, h1, cot, tok, g1, g2, att,
    inv, probs, qkv, w_qkv, w_out, parts,
):
    slots, hidden = act.shape
    rows, width = tok.shape
    wide = 4 * width
    half = groups // 2
    thin = wide // copies
    sems = pltpu.SemaphoreType.DMA
    block = pltpu.VMEM((slots, width), bf16)
    tile = (8, width)
    up = (width // 4, hidden)
    down = (hidden // 4, width)
    land = [up, down, up, down, up, up, down, down, up] if ends else []
    pools = [up, up, down, up] if ends else []
    return pl.pallas_call(
        functools.partial(backward_kernel, groups, cap, copies, ends),
        out_shape=[
            jax.ShapeDtypeStruct((rows, width), bf16), jax.ShapeDtypeStruct((rows, width), bf16),
            jax.ShapeDtypeStruct((groups * per, thin), bf16), jax.ShapeDtypeStruct(tile, f32),
        ]
        + [jax.ShapeDtypeStruct(one, bf16) for one in land],
        in_specs=[ANY] * 4 + [VMEM] * 2 + [ANY] * 3 + [VMEM] * 2 + [ANY] * (6 + len(parts)),
        out_specs=[ANY] * 3 + [VMEM] + [ANY] * len(land),
        scratch_shapes=[
            block, block, block, block,
            pltpu.VMEM((groups * per, wide), bf16), pltpu.VMEM((half * per, wide), bf16),
            pltpu.VMEM((half, per, wide), bf16), pltpu.VMEM((copies, per, thin), bf16),
            pltpu.VMEM((copies, per, thin), bf16), pltpu.VMEM((per, thin), bf16),
            pltpu.VMEM((groups * per, thin), bf16), pltpu.VMEM(tile, f32), pltpu.VMEM(tile, f32),
            pltpu.VMEM((half, *tile), f32), pltpu.VMEM((2, *tile), f32),
            pltpu.VMEM((copies, *tile), f32), sems((9,)), sems((3,)), sems((groups,)),
            sems((groups,)), sems((groups,)), sems((groups,)), sems((3,)), sems((3,)),
            sems((3 * half,)), sems((3 * half,)), sems((copies,)), sems((copies,)), sems((groups,)),
            sems((groups,)), sems((half + copies,)), sems((half + copies,)), sems((9,)), sems((9,)),
            sems((2,)),
        ]
        + [pltpu.VMEM(one, bf16) for one in pools]
        + [pltpu.VMEM(one, bf16) for one in (up, down) if ends],
        compiler_params=pltpu.CompilerParams(
            collective_id=1, has_side_effects=True, vmem_limit_bytes=60 * MIB
        ),
        cost_estimate=pl.CostEstimate(
            flops=200 * 10**9, bytes_accessed=40 * 10**6, transcendentals=0
        ),
        name="backward",
    )(
        act, gpre, w_in, w_down, experts, gates, h1, cot, tok, g1, g2, att, inv, probs, qkv, w_qkv,
        w_out, *parts,
    )


def finish_kernel(*refs):
    (
        up_own, up_in, up_across, up_out, up_outward, down_own, down_in, down_across, down_out,
        down_outward, block, gtok, whole_ref, gains_ref, up_ref, down_ref, qkv_hbm, out_hbm, one_ref,
        two_ref, block_ref, gtok_ref, a, b, c, d, e, f, up, down, qkv_ref, out_ref,
        block_line, gtok_line, load, store,
    ) = refs
    dp = lax.axis_index("dp")
    outer = (dp == 0) | (dp == 3)
    inner = jnp.logical_not(outer)
    hand_in = [
        pltpu.make_async_copy(block, block_line, load.at[6]),
        pltpu.make_async_copy(gtok, gtok_line, load.at[7]),
    ]
    handed = [
        pltpu.make_async_copy(block_line, block_ref, store.at[0]),
        pltpu.make_async_copy(gtok_line, gtok_ref, store.at[1]),
    ]

    def loads(sources, targets):
        return [
            pltpu.make_async_copy(src, dst, load.at[i])
            for i, (src, dst) in enumerate(zip(sources, targets))
        ]

    inside = loads((up_own, up_in, up_across, down_own, down_in, down_across), (a, b, c, d, e, f))
    outside = loads((up_out, up_outward, down_out, down_outward), (a, b, d, e))

    @pl.when(inner)
    def _():
        for one in inside:
            one.start()

    @pl.when(outer)
    def _():
        for one in outside:
            one.start()

    for one in hand_in:
        one.start()

    def summed(target, goal, terms, first):
        part = target.shape[0] // 3
        lines = part // 4
        for piece in range(3):

            @pl.loop(0, 4)
            def _(r):
                at = rows_at(piece * part + r * lines, lines)
                total = terms[0][at].astype(f32)
                for term in terms[1:]:
                    total = total + term[at].astype(f32)
                target[at] = total

            out(target, goal, first, piece).start()

    def out(target, goal, first, piece):
        part = target.shape[0] // 3
        at = slice(piece * part, (piece + 1) * part)
        return pltpu.make_async_copy(target.at[at], goal.at[at], store.at[first + piece])

    @pl.when(inner)
    def _():
        for one in inside[:3]:
            one.wait()
        summed(up, up_ref, (a, b, c), 6)
        for one in inside[3:]:
            one.wait()
        summed(down, down_ref, (d, e, f), 9)

    @pl.when(outer)
    def _():
        for one in outside[:2]:
            one.wait()
        summed(up, up_ref, (a, b), 6)
        for one in outside[2:]:
            one.wait()
        summed(down, down_ref, (d, e), 9)

    thin = qkv_ref.shape[0]
    turned = whole_ref[...].astype(f32).T
    qkv_ref[...] = turned[:thin]
    out_ref[...] = turned[thin:]
    handed += [
        pltpu.make_async_copy(qkv_ref, qkv_hbm, store.at[4]),
        pltpu.make_async_copy(out_ref, out_hbm, store.at[5]),
    ]
    for one in hand_in:
        one.wait()
    for one in handed:
        one.start()
    size = one_ref.shape[1]
    for row, target in ((0, one_ref), (1, two_ref)):
        line = jnp.zeros((1, size), f32)
        for plane in range(4):
            part = gains_ref[row : row + 1, plane * size : (plane + 1) * size]
            line = jnp.where(dp == plane, part, line)
        target[...] = line
    for one in handed:
        one.wait()
    for piece in range(3):
        out(up, up_ref, 6, piece).wait()
        out(down, down_ref, 9, piece).wait()


def finish(ups, downs, block, gtok, whole, gains):
    up, down = ups[0].shape, downs[0].shape
    width = whole.shape[1]
    thin = width // 4
    sems = pltpu.SemaphoreType.DMA
    return pl.pallas_call(
        finish_kernel,
        out_shape=[
            jax.ShapeDtypeStruct(up, f32), jax.ShapeDtypeStruct(down, f32),
            jax.ShapeDtypeStruct((3 * thin, whole.shape[0]), f32),
            jax.ShapeDtypeStruct((thin, whole.shape[0]), f32),
            jax.ShapeDtypeStruct((1, thin), f32), jax.ShapeDtypeStruct((1, thin), f32),
            jax.ShapeDtypeStruct(block.shape, bf16), jax.ShapeDtypeStruct(gtok.shape, bf16),
        ],
        in_specs=[ANY] * 12 + [VMEM] * 2,
        out_specs=[ANY] * 4 + [VMEM] * 2 + [ANY] * 2,
        scratch_shapes=[pltpu.VMEM(up, bf16)] * 3
        + [pltpu.VMEM(down, bf16)] * 3
        + [
            pltpu.VMEM(up, f32), pltpu.VMEM(down, f32), pltpu.VMEM((3 * thin, whole.shape[0]), f32),
            pltpu.VMEM((thin, whole.shape[0]), f32), pltpu.VMEM(block.shape, bf16),
            pltpu.VMEM(gtok.shape, bf16), sems((8,)), sems((12,)),
        ],
        compiler_params=pltpu.CompilerParams(vmem_limit_bytes=60 * MIB),
        name="finish",
    )(*ups, *downs, block, gtok, whole, gains)


def shards(
    tokens, segment_ids, token_expert, gates, ln1_gain, w_qkv, w_out, ln2_gain, expert_in,
    expert_out, cotangent,
):
    rows, width = tokens.shape
    groups, copies = lax.axis_size("expert"), lax.axis_size("dp")
    cap = 2 * rows // groups
    per = -(-width // (16 * groups)) * 16
    w_in, w_down = expert_in[0], expert_out[0]
    experts, gate_row = token_expert.reshape(1, rows), gates.reshape(1, rows)
    ends = copies == 4
    h1, qkv, att, inv, probs, act, gpre, *parts = forward(
        groups, cap, ends, tokens, segment_ids, experts, gate_row, ln1_gain, w_qkv, w_out,
        ln2_gain, w_in, w_down, cotangent,
    )
    if ends:
        up_far, up_near, up_out, up_own, down_far, down_near, down_out, down_own, up_far_in = parts
        parts = [up_far, up_near, up_out, up_own, up_far_in, down_far, down_near, down_out, down_own]
    block_out, grad_tokens, whole, gains, *landed = backward(
        groups, cap, copies, ends, per, act, gpre, w_in, w_down, experts, gate_row, h1, cotangent,
        tokens, ln1_gain, ln2_gain, att, inv, probs, qkv, w_qkv, w_out, parts if ends else [],
    )
    if ends:
        _, down_own_in, up_own_in, _, _, up_across, down_across, down_outward, up_outward = landed
        up_share, down_share, share_qkv, share_out, share_one, share_two, block, gtok = finish(
            (up_own, up_own_in, up_across, up_out, up_outward),
            (down_own, down_own_in, down_across, down_out, down_outward),
            block_out, grad_tokens, whole[:width], gains,
        )
        return (
            block, gtok, share_one[0], share_qkv.T, share_out.T, share_two[0], up_share[None],
            down_share[None],
        )
    up_share, down_share = (
        lax.psum_scatter(one[None], "dp", scatter_dimension=1, tiled=True) for one in parts
    )
    whole = whole[:width].astype(f32)
    share = width // copies
    gains = lax.dynamic_slice_in_dim(gains, lax.axis_index("dp") * share, share, 1)
    return (
        block_out,
        grad_tokens,
        gains[0],
        whole[:, : 3 * share],
        whole[:, 3 * share :],
        gains[1],
        up_share.astype(f32),
        down_share.astype(f32),
    )


def solution(mesh):
    tokens, experts = P(("dp", "expert"), None), P("expert", None, None)
    return jax.shard_map(
        shards,
        mesh=mesh,
        in_specs=(
            tokens, tokens, tokens, P(("dp", "expert")), P(), P(), P(), P(), experts, experts,
            tokens,
        ),
        out_specs=(
            tokens, tokens, P("dp"), P(None, "dp"), P(None, "dp"), P("dp"),
            P("expert", "dp", None), P("expert", "dp", None),
        ),
        check_vma=False,
    )
```
